32 devices in a mesh: gx: 8 (over z, x), gy: 4 (over y, core).
Axes of the slice: x: 2, y: 2, z: 4, core: 2. Of those that a mesh axis runs over, the one named last changes fastest.
Arguments:
- velocity: float32 [1, 2048, 2048], P(None, 'gx', 'gy'), may hold values from -6 to 6
Outputs:
- du_dx: float32 [1, 2048, 2048], P(None, 'gx', 'gy')
- du_dy: float32 [1, 2048, 2048], P(None, 'gx', 'gy')
- d2u_dx2: float32 [1, 2048, 2048], P(None, 'gx', 'gy')
- d2u_dy2: float32 [1, 2048, 2048], P(None, 'gx', 'gy')
The draws below stay inside these ranges and needn't reach their ends.
All inputs are finite; a program needn't handle non-finite values.
Results may differ from the reference program's by a relative error of at most 0.00007.
Values sent between devices are 32-bit elements; how exact they have to be, the bound alone decides.
No kernel may reach another device: no remote copies, remote signals or barrier semaphores. Data moves between devices by JAX's collectives and lax.ppermute only.
A program may use at most 64 MiB of HBM per device.

```python
import jax
import jax.numpy as jnp
from jax import lax

NX = 2048
NY = 2048
PLANES = 1


def steps_of(key, dims, split, smallest, largest):
    loudness = 1.0
    for axis_at, blocks in split:
        heights = jax.random.uniform(jax.random.fold_in(jax.random.fold_in(key, 6), axis_at), (blocks,), jnp.float32, smallest / len(split), largest / len(split))
        loudness = loudness * jnp.repeat(jnp.exp(heights), dims[axis_at] // blocks).reshape((-1,) + (1,) * (len(dims) - 1 - axis_at))
    return loudness


def noise(own_key, extent, width, bound, shards=(), kind=jnp.bfloat16):
    entries = jax.random.normal(own_key, extent, jnp.float32) * width
    if len(shards) > 0:
        entries = steps_of(own_key, extent, shards, -0.22, 0.18) * entries
    return jnp.clip(entries, min=-bound, max=bound).astype(kind)


def setup_inputs(seed: int = 0) -> dict:
    key_of = jax.random.split(jax.random.key(seed), 2)
    velocity = noise(key_of[0], (PLANES, NX, NY), 1.0, 6.0, ((1, 8), (2, 4)), jnp.float32)
    return {"velocity": velocity}


FIRST_NEAR = 7.0 / 9.0
FIRST_FAR = 1.0 / 36.0
SECOND_NEAR = 12.0 / 11.0
SECOND_FAR = 3.0 / 44.0
FIRST_COUPLING = 1.0 / 3.0
SECOND_COUPLING = 2.0 / 11.0


def stencils(field, axis):
    plus_one = jnp.roll(field, -1, axis)
    minus_one = jnp.roll(field, 1, axis)
    plus_two = jnp.roll(field, -2, axis)
    minus_two = jnp.roll(field, 2, axis)
    first_order = FIRST_NEAR * (plus_one - minus_one) + FIRST_FAR * (plus_two - minus_two)
    second_order = SECOND_NEAR * (plus_one - 2.0 * field + minus_one) + SECOND_FAR * (plus_two - 2.0 * field + minus_two)
    return first_order, second_order


def periodic_solve(source, coupling, axis):
    length = source.shape[axis]
    waves = jnp.arange(length).astype(source.dtype) * (2.0 * jnp.pi / length)
    divisor = 1.0 + 2.0 * coupling * jnp.cos(waves)
    if axis == 0:
        divisor = divisor[:, None]
    else:
        divisor = divisor[None, :]
    spectrum = jnp.fft.fft(source, axis=axis) / divisor
    return jnp.real(jnp.fft.ifft(spectrum, axis=axis)).astype(source.dtype)


def one_plane(plane):
    first_x, second_x = stencils(plane, 0)
    first_y, second_y = stencils(plane, 1)
    return (periodic_solve(first_x, FIRST_COUPLING, 0), periodic_solve(first_y, FIRST_COUPLING, 1),
            periodic_solve(second_x, SECOND_COUPLING, 0), periodic_solve(second_y, SECOND_COUPLING, 1))


def reference(velocity):
    du_dx, du_dy, d2u_dx2, d2u_dy2 = lax.map(one_plane, velocity)
    return (du_dx, du_dy, d2u_dx2, d2u_dy2)
```

```python
import math

import jax
import jax.numpy as jnp
import ml_dtypes
import numpy as np
from jax import lax
from jax.experimental import pallas as pl
from jax.experimental.pallas import tpu as pltpu
from jax.sharding import PartitionSpec as P

F32 = jnp.float32
BF16 = jnp.bfloat16

FIRST_IN, FIRST_OUT = 7.0 / 9.0 + 1.0 / 36.0, 1.0 / 36.0
SECOND_IN, SECOND_OUT = 12.0 / 11.0 + 3.0 / 44.0, 3.0 / 44.0

COUPLINGS = (1.0 / 3.0, 2.0 / 11.0)
RATIOS = tuple((math.sqrt(1.0 - 4.0 * a * a) - 1.0) / (2.0 * a) for a in COUPLINGS)
SCALES = tuple(1.0 / math.sqrt(1.0 - 4.0 * a * a) for a in COUPLINGS)

WINDOW = 256
TILE = 128
EDGE = 32
MESSAGE = 8

ANY = pl.BlockSpec(memory_space=pl.ANY)
VMEM = pl.BlockSpec(memory_space=pltpu.VMEM)


def inverse_parts():
    distance = np.abs(np.subtract.outer(np.arange(WINDOW), np.arange(WINDOW)))
    parts = []
    for ratio, scale in zip(RATIOS, SCALES):
        entries = scale * ratio ** distance.astype(np.float64)
        high = entries.astype(ml_dtypes.bfloat16)
        parts += [high, (entries - high.astype(np.float64)).astype(ml_dtypes.bfloat16)]
    return np.stack(parts)


def right_sides(cells, axis):
    length = cells.shape[axis]
    step = lambda a, k: pltpu.roll(a, k % length, axis)
    here = step(cells, -1) - cells
    before, after, far = step(here, 1), step(here, -1), step(here, 2)
    first = FIRST_IN * (here + before) + FIRST_OUT * (after + far)
    second = SECOND_IN * (here - before) + SECOND_OUT * (after - far)
    return first, second


def row_weights(rows, entry):
    at = lax.broadcasted_iota(jnp.int32, (rows, 1), 0)
    column = jnp.zeros((rows, 1), F32)
    for row in range(rows):
        if entry(row) != 0.0:
            column = jnp.where(at == row, F32(entry(row)), column)
    return column


def powers(ratio, exponent):
    size = jnp.exp(exponent.astype(F32) * math.log(-ratio))
    return jnp.where(exponent % 2 == 0, size, -size)


def message(strip, high):
    at = lax.broadcasted_iota(jnp.int32, (EDGE, 1), 0)
    known = (at >= 2) & (at < EDGE - 2)
    exponent = (EDGE - 3 - at) if high else (at - 2)
    tails = []
    for ratio, rhs in zip(RATIOS, right_sides(strip, 0)):
        weight = jnp.where(known, powers(ratio, exponent), 0.0)
        tails.append(jnp.sum(rhs * weight, axis=0, keepdims=True))
    near = pltpu.roll(strip[EDGE - 8 :], 4, 0) if high else strip[:8]
    row = lax.broadcasted_iota(jnp.int32, near.shape, 0)
    return jnp.where(row < 4, near, jnp.where(row == 4, tails[0], tails[1]))


def pack_kernel(u_ref, to_high_x, to_low_x, to_y, to_core, near_low, near_high, low_x, high_x, low_y, high_y, sems):
    rows, columns = u_ref.shape
    copies = [
        pltpu.make_async_copy(u_ref.at[:, pl.ds(0, TILE)], low_y, sems.at[0]),
        pltpu.make_async_copy(u_ref.at[:, pl.ds(columns - TILE, TILE)], high_y, sems.at[1]),
        pltpu.make_async_copy(u_ref.at[pl.ds(0, EDGE)], low_x, sems.at[2]),
        pltpu.make_async_copy(u_ref.at[pl.ds(rows - EDGE, EDGE)], high_x, sems.at[3]),
    ]
    for copy in copies:
        copy.start()
    even = lax.rem(lax.axis_index("gy"), 2) == 0
    copies[2].wait()
    to_low_x[...] = message(low_x[...], False)[: to_low_x.shape[0]]
    copies[3].wait()
    to_high_x[...] = message(high_x[...], True)
    copies[0].wait()
    low = low_y[...].T[:EDGE]
    copies[1].wait()
    high = high_y[...].T[TILE - EDGE :]
    near_low[...] = low[:8]
    near_high[...] = high[EDGE - 8 :]
    to_low, to_high = message(low, False), message(high, True)
    to_y[:, pl.ds(0, rows)] = jnp.where(even, to_low, to_high)[: to_y.shape[0]]
    to_core[...] = jnp.where(even, to_high, to_low)


def interior_kernel(u_ref, k_ref, dx, dy, dxx, dyy, strips_x, strips_y, high_x, rest_x, high_y, rest_y, solved_x, solved_y, sems):
    rows, columns = u_ref.shape

    def split(value, at, high, rest):
        upper = value.astype(BF16)
        high[at] = upper
        rest[at] = (value - upper.astype(F32)).astype(BF16)

    at = lax.broadcasted_iota(jnp.int32, (rows, 1), 0)
    known = (at >= 2) & (at < rows - 2)
    for j in range(columns // TILE):
        lanes = slice(j * TILE, (j + 1) * TILE)
        for s, rhs in enumerate(right_sides(u_ref[:, lanes], 0)):
            split(jnp.where(known, rhs, 0.0), (s, slice(None), lanes), high_x, rest_x)
    dot = lambda a, b: jnp.dot(a, b, preferred_element_type=F32)
    started = []

    def send(source, target):
        copy = pltpu.make_async_copy(source, target, sems.at[len(started)])
        copy.start()
        started.append(copy)

    outs_x, outs_y = (dx, dxx), (dy, dyy)
    span = min(columns, WINDOW)
    for j in range(columns // span):
        lanes = slice(j * span, (j + 1) * span)
        for s in range(2):
            upper, lower = k_ref[2 * s, :rows, :rows], k_ref[2 * s + 1, :rows, :rows]
            high, rest = high_x[s, :, lanes], rest_x[s, :, lanes]
            solved = dot(upper, high) + dot(upper, rest) + dot(lower, high)
            solved_x[s, :, lanes] = solved
            strips_x[s, 0, :, lanes] = solved[:EDGE]
            strips_x[s, 1, :, lanes] = solved[rows - EDGE :]
    if rows > 2 * EDGE:
        inner = pl.ds(EDGE, rows - 2 * EDGE)
        for s in range(2):
            send(solved_x.at[s, inner], outs_x[s].at[inner])

    at = lax.broadcasted_iota(jnp.int32, (1, columns), 1)
    known = (at >= 2) & (at < columns - 2)
    step = min(rows, 64)
    for i in range(rows // step):
        lines = slice(i * step, (i + 1) * step)
        for s, rhs in enumerate(right_sides(u_ref[lines, :], 1)):
            split(jnp.where(known, rhs, 0.0), (s, lines), high_y, rest_y)
    left = lax.broadcasted_iota(jnp.int32, (1, TILE), 1) < TILE // 2
    count = max((columns - WINDOW) // TILE, 0) + 1
    step = min(rows, 128)
    for i in range(rows // step):
        lines = slice(i * step, (i + 1) * step)
        for s in range(2):
            upper, lower = k_ref[2 * s, :span, :span], k_ref[2 * s + 1, :span, :span]
            windows = []
            for w in range(count):
                lanes = slice(w * TILE, w * TILE + span)
                high, rest = high_y[s, lines, lanes], rest_y[s, lines, lanes]
                windows.append(dot(high, upper) + dot(rest, upper) + dot(high, lower))
            tiles = columns // TILE
            for t in range(tiles):
                if t == 0:
                    tile = windows[0][:, :TILE]
                elif t == tiles - 1:
                    tile = windows[-1][:, span - TILE :]
                else:
                    tile = jnp.where(left, windows[t - 1][:, TILE:], windows[t][:, :TILE])
                if t == 0:
                    strips_y[s, 0, lines] = tile
                elif t == tiles - 1:
                    strips_y[s, 1, lines] = tile
                else:
                    solved_y[s, lines, (t - 1) * TILE : t * TILE] = tile
        if columns > 2 * TILE:
            for s in range(2):
                lines = pl.ds(i * step, step)
                send(solved_y.at[s, lines], outs_y[s].at[lines, pl.ds(TILE, columns - 2 * TILE)])
    for copy in started:
        copy.wait()


def side_terms(around, tails, high):
    found = []
    for s, rhs in enumerate(right_sides(around, 0)):
        ratio, scale = RATIOS[s], SCALES[s]
        pick = lambda row: rhs[row : row + 1]
        if high:
            outer, beyond, nearest, second = pick(4), pick(5), pick(3), pick(2)
        else:
            outer, beyond, nearest, second = pick(3), pick(2), pick(4), pick(5)
        total = ratio * (outer + ratio * (beyond + ratio * tails[s])) + nearest
        found.append((scale * total, scale * second))
    return found


def both_sides(from_low, from_high, own_low, own_high):
    row = lax.broadcasted_iota(jnp.int32, own_low.shape, 0)
    low = jnp.where(row < 4, from_low, pltpu.roll(own_low, 4, 0))
    high = jnp.where(row < 4, pltpu.roll(own_high, 4, 0), pltpu.roll(from_high, 4, 0))
    tails = lambda m: (m[4:5], m[5:6])
    return side_terms(low, tails(from_low), False), side_terms(high, tails(from_high), True)


def finish_kernel(from_low_x, from_high_x, from_y, from_core, near_low, near_high, own_x, strips_x, strips_y, *refs):
    dx, dy, dxx, dyy, done_x, done_y, held, sems = refs[4:]
    rows, columns = dx.shape
    started = []

    def send(source, target):
        copy = pltpu.make_async_copy(source, target, sems.at[len(started)])
        copy.start()
        started.append(copy)

    even = lax.rem(lax.axis_index("gy"), 2) == 0
    held[...] = jnp.zeros_like(held)
    held[0, : from_y.shape[0]] = from_y[:, pl.ds(0, rows)]
    held[1] = from_core[...]
    from_low = jnp.where(even, held[0], held[1])
    from_high = jnp.where(even, held[1], held[0])
    terms = both_sides(from_low, from_high, near_low[...], near_high[...])
    factors, basis = [], []
    lane = lax.broadcasted_iota(jnp.int32, (1, 4 * TILE), 1)
    row8 = lax.broadcasted_iota(jnp.int32, (8, 1), 0)
    stacked = jnp.zeros((8, rows), F32)
    table = jnp.zeros((8, 4 * TILE), F32)
    for side in range(2):
        for s in range(2):
            block = 2 * s + side
            within = lane - block * TILE
            inside = (within >= 0) & (within < TILE)
            distance = (TILE - 1 - within) if side else within
            for which in range(2):
                index = 4 * side + 2 * s + which
                power = jnp.where(inside, powers(RATIOS[s], jnp.abs(distance - which)), 0.0)
                stacked = jnp.where(row8 == index, terms[side][s][which], stacked)
                table = jnp.where(row8 == index, power, table)
    upper = lambda a: a.astype(BF16).astype(F32)
    lower = lambda a: a - upper(a)
    zero = jnp.zeros((8, 1), F32)
    lhs = jnp.concatenate([upper(stacked), lower(stacked), upper(stacked), jnp.broadcast_to(zero, stacked.shape)], axis=0)
    rhs = jnp.concatenate([upper(table), upper(table), lower(table), jnp.broadcast_to(zero, table.shape)], axis=0)
    added = lax.dot_general(
        lhs.astype(BF16), rhs.astype(BF16), (((0,), (0,)), ((), ())), preferred_element_type=F32
    )
    for s, out in enumerate((dy, dyy)):
        for side in range(2):
            block = 2 * s + side
            done_y[s, side] = strips_y[s, side] + added[:, block * TILE : (block + 1) * TILE]
            send(done_y.at[s, side], out.at[:, pl.ds(side * (columns - TILE), TILE)])

    held_x = jnp.concatenate([from_high_x[...], jnp.zeros((MESSAGE - from_high_x.shape[0], columns), F32)], axis=0)
    terms = both_sides(from_low_x[...], held_x, own_x[0], own_x[1])
    at = lax.broadcasted_iota(jnp.int32, (EDGE, 1), 0)
    for s, out in enumerate((dx, dxx)):
        for side in range(2):
            distance = (EDGE - 1 - at) if side else at
            near, second = terms[side][s]
            extra = near * powers(RATIOS[s], distance) + second * powers(RATIOS[s], jnp.abs(distance - 1))
            done_x[s, side] = strips_x[s, side] + extra
            send(done_x.at[s, side], out.at[pl.ds(side * (rows - EDGE), EDGE)])
    for copy in started:
        copy.wait()


def local(velocity):
    u = velocity[0]
    rows, columns = u.shape
    wide = max(rows, columns)
    on_chip = lambda *shape: pltpu.VMEM(shape, F32)
    gx, gy = lax.axis_size("gx"), lax.axis_size("gy")
    to_high_x, to_low_x, to_y, to_core, near_low, near_high = pl.pallas_call(
        pack_kernel,
        name="pack",
        out_shape=(
            on_chip(MESSAGE, columns),
            on_chip(MESSAGE - 2, columns),
            on_chip(MESSAGE - 1, wide),
            on_chip(MESSAGE, rows),
            on_chip(8, rows),
            on_chip(8, rows),
        ),
        in_specs=[ANY],
        out_specs=[VMEM] * 6,
        scratch_shapes=[
            on_chip(EDGE, columns),
            on_chip(EDGE, columns),
            on_chip(rows, TILE),
            on_chip(rows, TILE),
            pltpu.SemaphoreType.DMA((4,)),
        ],
    )(u)
    from_low_x = lax.ppermute(to_high_x, "gx", [(i, (i + 1) % gx) for i in range(gx)])
    across = [(i, (i - 1) % gy) if i % 2 == 0 else (i, (i + 1) % gy) for i in range(gy)]
    within = [(i, i + 1) if i % 2 == 0 else (i, i - 1) for i in range(gy)]
    from_y = lax.ppermute(to_y, "gy", across)
    from_high_x = lax.ppermute(to_low_x, "gx", [(i, (i - 1) % gx) for i in range(gx)])
    from_core = lax.ppermute(to_core, "gy", within)

    in_hbm = pltpu.HBM(u.shape, F32)
    u_near = pltpu.with_memory_space_constraint(u, pltpu.VMEM)
    inverses = pltpu.with_memory_space_constraint(jnp.asarray(inverse_parts()), pltpu.VMEM)
    dx, dy, dxx, dyy, strips_x, strips_y = pl.pallas_call(
        interior_kernel,
        name="interior",
        out_shape=(in_hbm,) * 4 + (on_chip(2, 2, EDGE, columns), on_chip(2, 2, rows, TILE)),
        in_specs=[VMEM, VMEM],
        out_specs=[ANY] * 4 + [VMEM] * 2,
        scratch_shapes=[pltpu.VMEM((2, rows, columns), BF16)] * 4
        + [
            on_chip(2, rows, columns),
            on_chip(2, rows, max(columns - 2 * TILE, TILE)),
            pltpu.SemaphoreType.DMA((16,)),
        ],
        cost_estimate=pl.CostEstimate(flops=2 * 2**28, bytes_accessed=5 * 2**19, transcendentals=0),
    )(u_near, inverses)
    own_x = jnp.stack([u[:8], u[rows - 8 :]])
    near = lambda a: pltpu.with_memory_space_constraint(a, pltpu.VMEM)
    out = jax.ShapeDtypeStruct(u.shape, F32)
    outs = pl.pallas_call(
        finish_kernel,
        name="finish",
        out_shape=(in_hbm,) * 4,
        in_specs=[VMEM] * 9 + [ANY] * 4,
        out_specs=[ANY] * 4,
        input_output_aliases={9 + k: k for k in range(4)},
        scratch_shapes=[
            on_chip(2, 2, EDGE, columns),
            on_chip(2, 2, rows, TILE),
            on_chip(2, MESSAGE, rows),
            pltpu.SemaphoreType.DMA((8,)),
        ],
    )(near(from_low_x), near(from_high_x), near(from_y), near(from_core), near(near_low), near(near_high), near(own_x), near(strips_x), near(strips_y), dx, dy, dxx, dyy)
    return tuple(o[None] for o in outs)


def solution(mesh):
    placed = P(None, "gx", "gy")
    return jax.shard_map(local, mesh=mesh, in_specs=(placed,), out_specs=(placed,) * 4, check_vma=False)
```

```python
import math

import jax
import jax.numpy as jnp
from jax import lax
from jax.experimental import pallas as pl
from jax.experimental.pallas import tpu as pltpu
from jax.sharding import PartitionSpec as P

F32 = jnp.float32
BF16 = jnp.bfloat16

FIRST_IN, FIRST_OUT = 7.0 / 9.0 + 1.0 / 36.0, 1.0 / 36.0
SECOND_IN, SECOND_OUT = 12.0 / 11.0 + 3.0 / 44.0, 3.0 / 44.0

COUPLINGS = (1.0 / 3.0, 2.0 / 11.0)
RATIOS = tuple((math.sqrt(1.0 - 4.0 * a * a) - 1.0) / (2.0 * a) for a in COUPLINGS)
SCALES = tuple(1.0 / math.sqrt(1.0 - 4.0 * a * a) for a in COUPLINGS)

WINDOW = 256
TILE = 128
EDGE = 32
REACH = 64
MESSAGE = 8

ANY = pl.BlockSpec(memory_space=pl.ANY)
VMEM = pl.BlockSpec(memory_space=pltpu.VMEM)


def right_sides(cells, axis):
    length = cells.shape[axis]
    step = lambda a, k: pltpu.roll(a, k % length, axis)
    here = step(cells, -1) - cells
    before, after, far = step(here, 1), step(here, -1), step(here, 2)
    first = FIRST_IN * (here + before) + FIRST_OUT * (after + far)
    second = SECOND_IN * (here - before) + SECOND_OUT * (after - far)
    return first, second


def powers(ratio, exponent):
    product = jnp.where(exponent < REACH, F32(1.0), F32(0.0))
    for bit in range(REACH.bit_length() - 1):
        factor = jnp.where((exponent & (1 << bit)) != 0, F32(ratio ** (1 << bit)), F32(1.0))
        product = product * factor
    return product


def tail_weights(high):
    at = lax.broadcasted_iota(jnp.int32, (EDGE, TILE), 0)
    known = (at >= 2) & (at < EDGE - 2)
    exponent = (EDGE - 3 - at) if high else (at - 2)
    return [jnp.where(known, powers(ratio, exponent), 0.0) for ratio in RATIOS]


def message(strip, high, weights):
    tails = [
        jnp.sum(rhs * weight[:, : strip.shape[1]], axis=0, keepdims=True)
        for rhs, weight in zip(right_sides(strip, 0), weights)
    ]
    near = pltpu.roll(strip[EDGE - 8 :], 4, 0) if high else strip[:8]
    row = lax.broadcasted_iota(jnp.int32, near.shape, 0)
    return jnp.where(row < 4, near, jnp.where(row == 4, tails[0], tails[1]))


def tiles_of(length):
    step = min(length, TILE)
    return [pl.ds(k * step, step) for k in range(length // step)]


def halves(value):
    upper = value.astype(BF16).astype(F32)
    return upper, value - upper


def put_inverses(k_ref):
    i = lax.broadcasted_iota(jnp.int32, (TILE, TILE), 0)
    j = lax.broadcasted_iota(jnp.int32, (TILE, TILE), 1)
    blocks = WINDOW // TILE
    for s in range(2):
        for apart in range(1 - blocks, blocks):
            upper, lower = halves(SCALES[s] * powers(RATIOS[s], jnp.abs(j - i + apart * TILE)))
            for p, part in enumerate((upper, lower)):
                for first in range(blocks):
                    if 0 <= first + apart < blocks:
                        at_i, at_j = pl.ds(first * TILE, TILE), pl.ds((first + apart) * TILE, TILE)
                        k_ref[2 * s + p, at_i, at_j] = part.astype(BF16)


def put_side_tables(table_x, table_y):
    at = lax.broadcasted_iota(jnp.int32, (EDGE, TILE), 0)
    lane = lax.broadcasted_iota(jnp.int32, (8, TILE), 1)
    row = lax.broadcasted_iota(jnp.int32, (8, TILE), 0)
    for s in range(2):
        for side in range(2):
            within = (TILE - 1 - lane) if side else lane
            lines = jnp.zeros((8, TILE), F32)
            for which in range(2):
                distance = (EDGE - 1 - at) if side else at
                table_x[s, side, which] = powers(RATIOS[s], jnp.abs(distance - which))
                lines = jnp.where(row == 4 * side + 2 * s + which, powers(RATIOS[s], jnp.abs(within - which)), lines)
            upper, lower = halves(lines)
            stack = jnp.concatenate([upper, upper, lower, jnp.zeros_like(upper)], axis=0)
            block = 2 * s + side
            table_y[:, pl.ds(block * TILE, TILE)] = stack.astype(BF16)


def pack_kernel(
    u_ref, to_high_x, to_low_x, to_y, to_core, u_near, near_low, near_high, k_ref, table_x, table_y, sems
):
    rows, columns = u_ref.shape
    across = [pl.ds(0, TILE), pl.ds(columns - TILE, TILE)]
    pieces = [(pl.ds(0, rows), lanes) for lanes in across]
    if columns > 2 * TILE:
        middle = pl.ds(TILE, columns - 2 * TILE)
        pieces += [(pl.ds(0, EDGE), middle), (pl.ds(rows - EDGE, EDGE), middle)]
        if rows > 2 * EDGE:
            pieces.append((pl.ds(EDGE, rows - 2 * EDGE), middle))
    copies = [
        pltpu.make_async_copy(u_ref.at[lines, lanes], u_near.at[lines, lanes], sems.at[k])
        for k, (lines, lanes) in enumerate(pieces)
    ]
    for copy in copies:
        copy.start()
    even = lax.rem(lax.axis_index("gy"), 2) == 0
    weights_low, weights_high = tail_weights(False), tail_weights(True)
    put_inverses(k_ref)
    put_side_tables(table_x, table_y)
    copies[0].wait()
    copies[1].wait()
    low = u_near[:, across[0]].T[:EDGE]
    high = u_near[:, across[1]].T[TILE - EDGE :]
    near_low[...] = low[:8]
    near_high[...] = high[EDGE - 8 :]
    for lanes in tiles_of(rows):
        part = slice(lanes.start, lanes.start + lanes.size)
        to_low, to_high = message(low[:, part], False, weights_low), message(high[:, part], True, weights_high)
        to_y[:, lanes] = jnp.where(even, to_low, to_high)
        to_core[:, lanes] = jnp.where(even, to_high, to_low)
    for copy in copies[2:4]:
        copy.wait()
    for lanes in tiles_of(columns):
        to_low_x[:, lanes] = message(u_near[pl.ds(0, EDGE), lanes], False, weights_low)
        to_high_x[:, lanes] = message(u_near[pl.ds(rows - EDGE, EDGE), lanes], True, weights_high)
    for copy in copies[4:]:
        copy.wait()


def put_split(value, at, high, rest):
    upper = value.astype(BF16)
    high[at] = upper
    rest[at] = (value - upper.astype(F32)).astype(BF16)


def dot(a, b):
    return jnp.dot(a, b, preferred_element_type=F32)


def solve_x(u_ref, k_ref, outs, strips, high_ref, rest_ref, solved_ref, sems):
    rows, columns = u_ref.shape
    at = lax.broadcasted_iota(jnp.int32, (rows, 1), 0)
    known = (at >= 2) & (at < rows - 2)
    for lanes in tiles_of(columns):
        for s, rhs in enumerate(right_sides(u_ref[:, lanes], 0)):
            put_split(jnp.where(known, rhs, 0.0), (s, slice(None), lanes), high_ref, rest_ref)
    span = min(columns, WINDOW)
    for s in range(2):
        for j in range(columns // span):
            lanes = slice(j * span, (j + 1) * span)
            upper, lower = k_ref[2 * s, :rows, :rows], k_ref[2 * s + 1, :rows, :rows]
            high, rest = high_ref[s, :, lanes], rest_ref[s, :, lanes]
            solved = dot(upper, high) + dot(upper, rest) + dot(lower, high)
            solved_ref[s, :, lanes] = solved
            strips[s, 0, :, lanes] = solved[:EDGE]
            strips[s, 1, :, lanes] = solved[rows - EDGE :]
    if rows > 2 * EDGE:
        inner = pl.ds(EDGE, rows - 2 * EDGE)
        copies = [pltpu.make_async_copy(solved_ref.at[s, inner], outs[s].at[inner], sems.at[s]) for s in range(2)]
        for copy in copies:
            copy.start()
        return copies
    return []


def solve_y(u_ref, k_ref, outs, strips, high_ref, rest_ref, solved_ref, sems):
    rows, columns = u_ref.shape
    at = lax.broadcasted_iota(jnp.int32, (1, columns), 1)
    known = (at >= 2) & (at < columns - 2)
    step = min(rows, 64)
    for i in range(rows // step):
        lines = slice(i * step, (i + 1) * step)
        for s, rhs in enumerate(right_sides(u_ref[lines, :], 1)):
            put_split(jnp.where(known, rhs, 0.0), (s, lines), high_ref, rest_ref)
    left = lax.broadcasted_iota(jnp.int32, (1, TILE), 1) < TILE // 2
    span = min(columns, WINDOW)
    count = max((columns - WINDOW) // TILE, 0) + 1
    tiles = columns // TILE
    step = min(rows, 128)
    copies = []
    for s in range(2):
        upper, lower = k_ref[2 * s, :span, :span], k_ref[2 * s + 1, :span, :span]
        for i in range(rows // step):
            lines = slice(i * step, (i + 1) * step)
            windows = []
            for w in range(count):
                lanes = slice(w * TILE, w * TILE + span)
                high, rest = high_ref[s, lines, lanes], rest_ref[s, lines, lanes]
                windows.append(dot(high, upper) + dot(rest, upper) + dot(high, lower))
            for t in range(tiles):
                if t == 0:
                    strips[s, 0, lines] = windows[0][:, :TILE]
                elif t == tiles - 1:
                    strips[s, 1, lines] = windows[-1][:, span - TILE :]
                else:
                    tile = jnp.where(left, windows[t - 1][:, TILE:], windows[t][:, :TILE])
                    solved_ref[s, lines, (t - 1) * TILE : t * TILE] = tile
        if tiles > 2:
            copies.append(pltpu.make_async_copy(solved_ref.at[s], outs[s].at[:, pl.ds(TILE, columns - 2 * TILE)], sems.at[s]))
            copies[-1].start()
    return copies


def solves_x_early():
    return (lax.axis_index("gx") == 0) & (lax.axis_index("gy") < 2)


def solves_y_early():
    return lax.axis_index("gx") == 0


def lead_x_kernel(u_ref, k_ref, *refs):
    dx, dxx, strips_x, *scratch = refs[4:]

    @pl.when(solves_x_early())
    def _():
        for copy in solve_x(u_ref, k_ref, (dx, dxx), strips_x, *scratch):
            copy.wait()


def lead_y_kernel(u_ref, k_ref, *refs):
    dy, dyy, strips_y, *scratch = refs[4:]

    @pl.when(solves_y_early())
    def _():
        for copy in solve_y(u_ref, k_ref, (dy, dyy), strips_y, *scratch):
            copy.wait()


def interior_kernel(u_ref, k_ref, *refs):
    dx, dxx, strips_x, dy, dyy, strips_y, *scratch = refs[6:]
    for_x, for_y = scratch[:4], scratch[4:]

    @pl.when(solves_y_early() & jnp.logical_not(solves_x_early()))
    def _():
        for copy in solve_x(u_ref, k_ref, (dx, dxx), strips_x, *for_x):
            copy.wait()

    @pl.when(jnp.logical_not(solves_y_early()))
    def _():
        copies = solve_x(u_ref, k_ref, (dx, dxx), strips_x, *for_x)
        copies += solve_y(u_ref, k_ref, (dy, dyy), strips_y, *for_y)
        for copy in copies:
            copy.wait()


def side_terms(around, tails, high):
    found = []
    for s, rhs in enumerate(right_sides(around, 0)):
        ratio, scale = RATIOS[s], SCALES[s]
        pick = lambda row: rhs[row : row + 1]
        if high:
            outer, beyond, nearest, second = pick(4), pick(5), pick(3), pick(2)
        else:
            outer, beyond, nearest, second = pick(3), pick(2), pick(4), pick(5)
        total = ratio * (outer + ratio * (beyond + ratio * tails[s])) + nearest
        found.append((scale * total, scale * second))
    return found


def both_sides(from_low, from_high, own_low, own_high):
    row = lax.broadcasted_iota(jnp.int32, own_low.shape, 0)
    low = jnp.where(row < 4, from_low, pltpu.roll(own_low, 4, 0))
    high = jnp.where(row < 4, pltpu.roll(own_high, 4, 0), pltpu.roll(from_high, 4, 0))
    tails = lambda m: (m[4:5], m[5:6])
    return side_terms(low, tails(from_low), False), side_terms(high, tails(from_high), True)


def finish_kernel(
    from_low_x, from_y, from_high_x, from_core, u_near, near_low, near_high, table_x, table_y, strips_x, strips_y, *refs
):
    dx, dxx, dy, dyy, done_x, done_y, sems = refs[4:]
    rows, columns = dx.shape
    started = []

    def send(source, target):
        copy = pltpu.make_async_copy(source, target, sems.at[len(started)])
        copy.start()
        started.append(copy)

    even = lax.rem(lax.axis_index("gy"), 2) == 0
    across, within = from_y[:, pl.ds(0, rows)], from_core[:, pl.ds(0, rows)]
    from_low = jnp.where(even, across, within)
    from_high = jnp.where(even, within, across)
    terms = both_sides(from_low, from_high, near_low[...], near_high[...])
    row = lax.broadcasted_iota(jnp.int32, (8, 1), 0)
    stacked = jnp.zeros((8, rows), F32)
    for side in range(2):
        for s in range(2):
            for which in range(2):
                stacked = jnp.where(row == 4 * side + 2 * s + which, terms[side][s][which], stacked)
    upper, lower = halves(stacked)
    factors = jnp.concatenate([upper, lower, upper, jnp.zeros_like(upper)], axis=0).astype(BF16)
    added = lax.dot_general(factors, table_y[...], (((0,), (0,)), ((), ())), preferred_element_type=F32)
    for s, out in enumerate((dy, dyy)):
        for side in range(2):
            block = 2 * s + side
            done_y[s, side] = strips_y[s, side] + added[:, block * TILE : (block + 1) * TILE]
            send(done_y.at[s, side], out.at[:, pl.ds(side * (columns - TILE), TILE)])

    terms = both_sides(from_low_x[...], from_high_x[...], u_near[pl.ds(0, 8)], u_near[pl.ds(rows - 8, 8)])
    step = min(columns, TILE)
    for s, out in enumerate((dx, dxx)):
        for side in range(2):
            near, second = terms[side][s]
            for j in range(columns // step):
                lanes = slice(j * step, (j + 1) * step)
                extra = near[:, lanes] * table_x[s, side, 0, :, :step] + second[:, lanes] * table_x[s, side, 1, :, :step]
                done_x[s, side, :, lanes] = strips_x[s, side, :, lanes] + extra
            send(done_x.at[s, side], out.at[pl.ds(side * (rows - EDGE), EDGE)])
    for copy in started:
        copy.wait()


def on_chip(*shape):
    return pltpu.VMEM(shape, F32)


def near(array):
    return pltpu.with_memory_space_constraint(array, pltpu.VMEM)


def pack(u):
    rows, columns = u.shape
    wide = max(rows, columns)
    return pl.pallas_call(
        pack_kernel,
        name="pack",
        out_shape=(
            on_chip(MESSAGE, columns),
            on_chip(MESSAGE, columns),
            on_chip(MESSAGE, wide),
            on_chip(MESSAGE, wide),
            on_chip(rows, columns),
            on_chip(8, rows),
            on_chip(8, rows),
            pltpu.VMEM((4, WINDOW, WINDOW), BF16),
            on_chip(2, 2, 2, EDGE, TILE),
            pltpu.VMEM((32, 4 * TILE), BF16),
        ),
        in_specs=[ANY],
        out_specs=[VMEM] * 10,
        scratch_shapes=[pltpu.SemaphoreType.DMA((5,))],
    )(u)


def scratch_x(rows, columns):
    return [pltpu.VMEM((2, rows, columns), BF16)] * 2 + [on_chip(2, rows, columns), pltpu.SemaphoreType.DMA((2,))]


def scratch_y(rows, columns):
    inner = max(columns - 2 * TILE, TILE)
    return [pltpu.VMEM((2, rows, columns), BF16)] * 2 + [on_chip(2, rows, inner), pltpu.SemaphoreType.DMA((2,))]


def shapes_x(rows, columns):
    return (pltpu.HBM((rows, columns), F32),) * 2 + (on_chip(2, 2, EDGE, columns),)


def shapes_y(rows, columns):
    return (pltpu.HBM((rows, columns), F32),) * 2 + (on_chip(2, 2, rows, TILE),)


def lead(kernel, name, u_near, inverses, shapes, scratch, passing):
    return pl.pallas_call(
        kernel,
        name=name,
        out_shape=tuple(on_chip(*a.shape) for a in passing) + shapes,
        in_specs=[VMEM] * 4,
        out_specs=[VMEM] * 2 + [ANY] * 2 + [VMEM],
        input_output_aliases={2: 0, 3: 1},
        scratch_shapes=scratch,
    )(near(u_near), near(inverses), *(near(a) for a in passing))


def interior(u_near, inverses, solved_x, solved_y):
    size = u_near.shape
    return pl.pallas_call(
        interior_kernel,
        name="interior",
        out_shape=shapes_x(*size) + shapes_y(*size),
        in_specs=[VMEM] * 2 + ([ANY] * 2 + [VMEM]) * 2,
        out_specs=([ANY] * 2 + [VMEM]) * 2,
        input_output_aliases={2 + k: k for k in range(6)},
        scratch_shapes=scratch_x(*size) + scratch_y(*size),
        cost_estimate=pl.CostEstimate(flops=2 * 2**28, bytes_accessed=5 * 2**19, transcendentals=0),
    )(near(u_near), near(inverses), *solved_x[:2], near(solved_x[2]), *solved_y[:2], near(solved_y[2]))


def finish(arrays, parts):
    rows, columns = parts[0].shape
    return pl.pallas_call(
        finish_kernel,
        name="finish",
        out_shape=(pltpu.HBM(parts[0].shape, F32),) * 4,
        in_specs=[VMEM] * 11 + [ANY] * 4,
        out_specs=[ANY] * 4,
        input_output_aliases={11 + k: k for k in range(4)},
        scratch_shapes=[
            on_chip(2, 2, EDGE, columns),
            on_chip(2, 2, rows, TILE),
            pltpu.SemaphoreType.DMA((8,)),
        ],
    )(*(near(a) for a in arrays), *parts)


def local(velocity):
    to_high_x, to_low_x, to_y, to_core, u_near, near_low, near_high, inverses, *tables = pack(velocity[0])
    size = u_near.shape
    to_high_x, to_y, *solved_x = lead(
        lead_x_kernel, "lead_x", u_near, inverses, shapes_x(*size), scratch_x(*size), (to_high_x, to_y)
    )
    to_low_x, to_core, *solved_y = lead(
        lead_y_kernel, "lead_y", u_near, inverses, shapes_y(*size), scratch_y(*size), (to_low_x, to_core)
    )
    gx, gy = lax.axis_size("gx"), lax.axis_size("gy")
    across = [(i, (i - 1) % gy) if i % 2 == 0 else (i, (i + 1) % gy) for i in range(gy)]
    within = [(i, i + 1) if i % 2 == 0 else (i, i - 1) for i in range(gy)]
    messages = (
        lax.ppermute(to_high_x, "gx", [(i, (i + 1) % gx) for i in range(gx)]),
        lax.ppermute(to_y, "gy", across),
        lax.ppermute(to_low_x, "gx", [(i, (i - 1) % gx) for i in range(gx)]),
        lax.ppermute(to_core, "gy", within),
    )
    dx, dxx, strips_x, dy, dyy, strips_y = interior(u_near, inverses, solved_x, solved_y)
    arrays = (*messages, u_near, near_low, near_high, *tables, strips_x, strips_y)
    dx, dxx, dy, dyy = finish(arrays, (dx, dxx, dy, dyy))
    return tuple(o[None] for o in (dx, dy, dxx, dyy))


def solution(mesh):
    placed = P(None, "gx", "gy")
    return jax.shard_map(local, mesh=mesh, in_specs=(placed,), out_specs=(placed,) * 4, check_vma=False)
```

```python
import math

import jax
import jax.numpy as jnp
from jax import lax
from jax.experimental import pallas as pl
from jax.experimental.pallas import tpu as pltpu
from jax.sharding import PartitionSpec as P

F32 = jnp.float32
BF16 = jnp.bfloat16

FIRST_IN, FIRST_OUT = 7.0 / 9.0 + 1.0 / 36.0, 1.0 / 36.0
SECOND_IN, SECOND_OUT = 12.0 / 11.0 + 3.0 / 44.0, 3.0 / 44.0

COUPLINGS = (1.0 / 3.0, 2.0 / 11.0)
RATIOS = tuple((math.sqrt(1.0 - 4.0 * a * a) - 1.0) / (2.0 * a) for a in COUPLINGS)
SCALES = tuple(1.0 / math.sqrt(1.0 - 4.0 * a * a) for a in COUPLINGS)

WINDOW = 256
TILE = 128
EDGE = 32
REACH = 64
MESSAGE = 8

ANY = pl.BlockSpec(memory_space=pl.ANY)
VMEM = pl.BlockSpec(memory_space=pltpu.VMEM)
LIMIT = pltpu.CompilerParams(vmem_limit_bytes=16 * 2**20)


def right_sides(cells, axis):
    length = cells.shape[axis]
    step = lambda a, k: pltpu.roll(a, k % length, axis)
    here = step(cells, -1) - cells
    before, after, far = step(here, 1), step(here, -1), step(here, 2)
    first = FIRST_IN * (here + before) + FIRST_OUT * (after + far)
    second = SECOND_IN * (here - before) + SECOND_OUT * (after - far)
    return first, second


def powers(ratio, exponent):
    product = jnp.where(exponent < REACH, F32(1.0), F32(0.0))
    for bit in range(REACH.bit_length() - 1):
        factor = jnp.where((exponent & (1 << bit)) != 0, F32(ratio ** (1 << bit)), F32(1.0))
        product = product * factor
    return product


def tail_weights(high):
    at = lax.broadcasted_iota(jnp.int32, (EDGE, TILE), 0)
    known = (at >= 2) & (at < EDGE - 2)
    exponent = (EDGE - 3 - at) if high else (at - 2)
    return [jnp.where(known, powers(ratio, exponent), 0.0) for ratio in RATIOS]


def message(strip, high, weights):
    tails = [
        jnp.sum(rhs * weight[:, : strip.shape[1]], axis=0, keepdims=True)
        for rhs, weight in zip(right_sides(strip, 0), weights)
    ]
    near = pltpu.roll(strip[EDGE - 8 :], 4, 0) if high else strip[:8]
    row = lax.broadcasted_iota(jnp.int32, near.shape, 0)
    return jnp.where(row < 4, near, jnp.where(row == 4, tails[0], tails[1]))


def tiles_of(length):
    step = min(length, TILE)
    return [pl.ds(k * step, step) for k in range(length // step)]


def halves(value):
    upper = value.astype(BF16).astype(F32)
    return upper, value - upper


def put_inverses(k_ref):
    i = lax.broadcasted_iota(jnp.int32, (TILE, TILE), 0)
    j = lax.broadcasted_iota(jnp.int32, (TILE, TILE), 1)
    blocks = WINDOW // TILE
    for s in range(2):
        for apart in range(1 - blocks, blocks):
            upper, lower = halves(SCALES[s] * powers(RATIOS[s], jnp.abs(j - i + apart * TILE)))
            for p, part in enumerate((upper, lower)):
                for first in range(blocks):
                    if 0 <= first + apart < blocks:
                        at_i, at_j = pl.ds(first * TILE, TILE), pl.ds((first + apart) * TILE, TILE)
                        k_ref[2 * s + p, at_i, at_j] = part.astype(BF16)


def put_side_tables(table_x, table_y):
    at = lax.broadcasted_iota(jnp.int32, (EDGE, TILE), 0)
    lane = lax.broadcasted_iota(jnp.int32, (8, TILE), 1)
    row = lax.broadcasted_iota(jnp.int32, (8, TILE), 0)
    for s in range(2):
        for side in range(2):
            within = (TILE - 1 - lane) if side else lane
            lines = jnp.zeros((8, TILE), F32)
            for which in range(2):
                distance = (EDGE - 1 - at) if side else at
                table_x[s, side, which] = powers(RATIOS[s], jnp.abs(distance - which))
                lines = jnp.where(row == 4 * side + 2 * s + which, powers(RATIOS[s], jnp.abs(within - which)), lines)
            upper, lower = halves(lines)
            stack = jnp.concatenate([upper, upper, lower, jnp.zeros_like(upper)], axis=0)
            block = 2 * s + side
            table_y[:, pl.ds(block * TILE, TILE)] = stack.astype(BF16)


def low_goes_first():
    next_chip_first = 2 * lax.axis_index("gx") < lax.axis_size("gx")
    return next_chip_first == (lax.rem(lax.axis_index("gy"), 2) == 0)


def trades_along_y():
    gx, gy = lax.axis_size("gx"), lax.axis_size("gy")
    next_chip = [(y, (y - 1) % gy if y % 2 == 0 else (y + 1) % gy) for y in range(gy)]
    same_chip = [(y, y + 1 if y % 2 == 0 else y - 1) for y in range(gy)]
    first, second = [], []
    for x in range(gx):
        orders = (next_chip, same_chip) if 2 * x < gx else (same_chip, next_chip)
        for found, pairs in zip((first, second), orders):
            found += [(x * gy + source, x * gy + target) for source, target in pairs]
    return first, second


def pack_kernel(
    u_ref, to_high_x, to_low_x, to_y_first, to_y_second, u_near, near_low, near_high, k_ref, table_x, table_y, sems
):
    rows, columns = u_ref.shape
    across = [pl.ds(0, TILE), pl.ds(columns - TILE, TILE)]
    pieces = [(pl.ds(0, rows), lanes) for lanes in across]
    if columns > 2 * TILE:
        middle = pl.ds(TILE, columns - 2 * TILE)
        pieces += [(pl.ds(0, EDGE), middle), (pl.ds(rows - EDGE, EDGE), middle)]
        if rows > 2 * EDGE:
            pieces.append((pl.ds(EDGE, rows - 2 * EDGE), middle))
    copies = [
        pltpu.make_async_copy(u_ref.at[lines, lanes], u_near.at[lines, lanes], sems.at[k])
        for k, (lines, lanes) in enumerate(pieces)
    ]
    for copy in copies:
        copy.start()
    low_first = low_goes_first()
    weights_low, weights_high = tail_weights(False), tail_weights(True)
    put_inverses(k_ref)
    put_side_tables(table_x, table_y)
    copies[0].wait()
    copies[1].wait()
    low = u_near[:, across[0]].T[:EDGE]
    high = u_near[:, across[1]].T[TILE - EDGE :]
    near_low[...] = low[:8]
    near_high[...] = high[EDGE - 8 :]
    for lanes in tiles_of(rows):
        part = slice(lanes.start, lanes.start + lanes.size)
        to_low, to_high = message(low[:, part], False, weights_low), message(high[:, part], True, weights_high)
        to_y_first[:, lanes] = jnp.where(low_first, to_low, to_high)
        to_y_second[:, lanes] = jnp.where(low_first, to_high, to_low)
    for copy in copies[2:4]:
        copy.wait()
    for lanes in tiles_of(columns):
        to_low_x[:, lanes] = message(u_near[pl.ds(0, EDGE), lanes], False, weights_low)
        to_high_x[:, lanes] = message(u_near[pl.ds(rows - EDGE, EDGE), lanes], True, weights_high)
    for copy in copies[4:]:
        copy.wait()


def put_split(value, at, high, rest):
    upper = value.astype(BF16)
    high[at] = upper
    rest[at] = (value - upper.astype(F32)).astype(BF16)


def dot(a, b):
    return jnp.dot(a, b, preferred_element_type=F32)


def solve_x(u_ref, k_ref, strips, solved_ref, high_ref, rest_ref):
    rows, columns = u_ref.shape
    at = lax.broadcasted_iota(jnp.int32, (rows, 1), 0)
    known = (at >= 2) & (at < rows - 2)
    for lanes in tiles_of(columns):
        for s, rhs in enumerate(right_sides(u_ref[:, lanes], 0)):
            put_split(jnp.where(known, rhs, 0.0), (s, slice(None), lanes), high_ref, rest_ref)
    span = min(columns, WINDOW)
    for s in range(2):
        for j in range(columns // span):
            lanes = slice(j * span, (j + 1) * span)
            upper, lower = k_ref[2 * s, :rows, :rows], k_ref[2 * s + 1, :rows, :rows]
            high, rest = high_ref[s, :, lanes], rest_ref[s, :, lanes]
            solved = dot(upper, high) + dot(upper, rest) + dot(lower, high)
            solved_ref[s, :, lanes] = solved
            strips[s, 0, :, lanes] = solved[:EDGE]
            strips[s, 1, :, lanes] = solved[rows - EDGE :]


def solve_y(u_ref, k_ref, strips, solved_ref, high_ref, rest_ref):
    rows, columns = u_ref.shape
    at = lax.broadcasted_iota(jnp.int32, (1, columns), 1)
    known = (at >= 2) & (at < columns - 2)
    step = min(rows, 64)
    for i in range(rows // step):
        lines = slice(i * step, (i + 1) * step)
        for s, rhs in enumerate(right_sides(u_ref[lines, :], 1)):
            put_split(jnp.where(known, rhs, 0.0), (s, lines), high_ref, rest_ref)
    left = lax.broadcasted_iota(jnp.int32, (1, TILE), 1) < TILE // 2
    span = min(columns, WINDOW)
    count = max((columns - WINDOW) // TILE, 0) + 1
    tiles = columns // TILE
    step = min(rows, 128)
    for s in range(2):
        upper, lower = k_ref[2 * s, :span, :span], k_ref[2 * s + 1, :span, :span]
        for i in range(rows // step):
            lines = slice(i * step, (i + 1) * step)
            windows = []
            for w in range(count):
                lanes = slice(w * TILE, w * TILE + span)
                high, rest = high_ref[s, lines, lanes], rest_ref[s, lines, lanes]
                windows.append(dot(high, upper) + dot(rest, upper) + dot(high, lower))
            for t in range(tiles):
                if t == 0:
                    strips[s, 0, lines] = windows[0][:, :TILE]
                elif t == tiles - 1:
                    strips[s, 1, lines] = windows[-1][:, span - TILE :]
                else:
                    tile = jnp.where(left, windows[t - 1][:, TILE:], windows[t][:, :TILE])
                    solved_ref[s, lines, (t - 1) * TILE : t * TILE] = tile


def solves_x_early():
    return (lax.axis_index("gx") == 0) & (lax.axis_index("gy") < 2)


def lead_kernel(u_ref, k_ref, *refs):
    messages, passed, (strips_x, solved_x, high_ref, rest_ref) = refs[:4], refs[4:8], refs[8:]
    for message_ref, passed_ref in zip(messages, passed):
        passed_ref[...] = message_ref[...]

    @pl.when(solves_x_early())
    def _():
        solve_x(u_ref, k_ref, strips_x, solved_x, high_ref, rest_ref)


def interior_kernel(u_ref, k_ref, early_strips, early_solved, *refs):
    strips_x, dx, dxx, strips_y, solved_y, high_ref, rest_ref, high_y, rest_y, solved_x, sems = refs
    rows, columns = u_ref.shape

    def inner_copies(source):
        if rows <= 2 * EDGE:
            return []
        inner = pl.ds(EDGE, rows - 2 * EDGE)
        return [pltpu.make_async_copy(source.at[s, inner], out.at[inner], sems.at[s]) for s, out in enumerate((dx, dxx))]

    @pl.when(solves_x_early())
    def _():
        copies = inner_copies(early_solved)
        for copy in copies:
            copy.start()
        strips_x[...] = early_strips[...]
        solve_y(u_ref, k_ref, strips_y, solved_y, high_y, rest_y)
        for copy in copies:
            copy.wait()

    @pl.when(jnp.logical_not(solves_x_early()))
    def _():
        solve_x(u_ref, k_ref, strips_x, solved_x, high_ref, rest_ref)
        copies = inner_copies(solved_x)
        for copy in copies:
            copy.start()
        solve_y(u_ref, k_ref, strips_y, solved_y, high_y, rest_y)
        for copy in copies:
            copy.wait()


def side_terms(around, tails, high):
    found = []
    for s, rhs in enumerate(right_sides(around, 0)):
        ratio, scale = RATIOS[s], SCALES[s]
        pick = lambda row: rhs[row : row + 1]
        if high:
            outer, beyond, nearest, second = pick(4), pick(5), pick(3), pick(2)
        else:
            outer, beyond, nearest, second = pick(3), pick(2), pick(4), pick(5)
        total = ratio * (outer + ratio * (beyond + ratio * tails[s])) + nearest
        found.append((scale * total, scale * second))
    return found


def both_sides(from_low, from_high, own_low, own_high):
    row = lax.broadcasted_iota(jnp.int32, own_low.shape, 0)
    low = jnp.where(row < 4, from_low, pltpu.roll(own_low, 4, 0))
    high = jnp.where(row < 4, pltpu.roll(own_high, 4, 0), pltpu.roll(from_high, 4, 0))
    tails = lambda m: (m[4:5], m[5:6])
    return side_terms(low, tails(from_low), False), side_terms(high, tails(from_high), True)


def finish_kernel(
    from_low_x, from_y_first, from_high_x, from_y_second, u_near, near_low, near_high, table_x, table_y, strips_x, strips_y, solved_y, *refs
):
    dx, dxx, dy, dyy, done_x, done_y, sems = refs[2:]
    rows, columns = dx.shape
    started = []

    def send(source, target):
        copy = pltpu.make_async_copy(source, target, sems.at[len(started)])
        copy.start()
        started.append(copy)

    if columns > 2 * TILE:
        for s, out in enumerate((dy, dyy)):
            send(solved_y.at[s], out.at[:, pl.ds(TILE, columns - 2 * TILE)])
    low_first = low_goes_first()
    first, second = from_y_first[:, pl.ds(0, rows)], from_y_second[:, pl.ds(0, rows)]
    from_low = jnp.where(low_first, first, second)
    from_high = jnp.where(low_first, second, first)
    terms = both_sides(from_low, from_high, near_low[...], near_high[...])
    row = lax.broadcasted_iota(jnp.int32, (8, 1), 0)
    stacked = jnp.zeros((8, rows), F32)
    for side in range(2):
        for s in range(2):
            for which in range(2):
                stacked = jnp.where(row == 4 * side + 2 * s + which, terms[side][s][which], stacked)
    upper, lower = halves(stacked)
    factors = jnp.concatenate([upper, lower, upper, jnp.zeros_like(upper)], axis=0).astype(BF16)
    added = lax.dot_general(factors, table_y[...], (((0,), (0,)), ((), ())), preferred_element_type=F32)
    for s, out in enumerate((dy, dyy)):
        for side in range(2):
            block = 2 * s + side
            done_y[s, side] = strips_y[s, side] + added[:, block * TILE : (block + 1) * TILE]
            send(done_y.at[s, side], out.at[:, pl.ds(side * (columns - TILE), TILE)])

    terms = both_sides(from_low_x[...], from_high_x[...], u_near[pl.ds(0, 8)], u_near[pl.ds(rows - 8, 8)])
    step = min(columns, TILE)
    for s, out in enumerate((dx, dxx)):
        for side in range(2):
            near, second = terms[side][s]
            for j in range(columns // step):
                lanes = slice(j * step, (j + 1) * step)
                extra = near[:, lanes] * table_x[s, side, 0, :, :step] + second[:, lanes] * table_x[s, side, 1, :, :step]
                done_x[s, side, :, lanes] = strips_x[s, side, :, lanes] + extra
            send(done_x.at[s, side], out.at[pl.ds(side * (rows - EDGE), EDGE)])
    for copy in started:
        copy.wait()


def on_chip(*shape):
    return pltpu.VMEM(shape, F32)


def near(array):
    return pltpu.with_memory_space_constraint(array, pltpu.VMEM)


def pack(u):
    rows, columns = u.shape
    wide = max(rows, columns)
    return pl.pallas_call(
        pack_kernel,
        name="pack",
        out_shape=(
            on_chip(MESSAGE, columns),
            on_chip(MESSAGE, columns),
            on_chip(MESSAGE, wide),
            on_chip(MESSAGE, wide),
            on_chip(rows, columns),
            on_chip(8, rows),
            on_chip(8, rows),
            pltpu.VMEM((4, WINDOW, WINDOW), BF16),
            on_chip(2, 2, 2, EDGE, TILE),
            pltpu.VMEM((32, 4 * TILE), BF16),
        ),
        in_specs=[ANY],
        out_specs=[VMEM] * 10,
        scratch_shapes=[pltpu.SemaphoreType.DMA((5,))],
        compiler_params=LIMIT,
    )(pltpu.with_memory_space_constraint(u, pltpu.HBM))


def split_refs(rows, columns):
    return [pltpu.VMEM((2, rows, columns), BF16)] * 2


def shapes_x(rows, columns):
    return on_chip(2, 2, EDGE, columns), on_chip(2, rows, columns)


def lead(u_near, inverses, messages):
    size = u_near.shape
    return pl.pallas_call(
        lead_kernel,
        name="lead",
        out_shape=tuple(on_chip(*a.shape) for a in messages) + shapes_x(*size),
        in_specs=[VMEM] * 6,
        out_specs=[VMEM] * 6,
        scratch_shapes=split_refs(*size),
        compiler_params=LIMIT,
    )(near(u_near), near(inverses), *(near(a) for a in messages))


def interior(u_near, inverses, early_strips, early_solved):
    rows, columns = u_near.shape
    strips_x, solved_x = shapes_x(rows, columns)
    return pl.pallas_call(
        interior_kernel,
        name="interior",
        out_shape=(strips_x,)
        + (pltpu.HBM(u_near.shape, F32),) * 2
        + (on_chip(2, 2, rows, TILE), on_chip(2, rows, max(columns - 2 * TILE, TILE))),
        in_specs=[VMEM] * 4,
        out_specs=[VMEM] + [ANY] * 2 + [VMEM] * 2,
        scratch_shapes=split_refs(rows, columns) * 2 + [solved_x, pltpu.SemaphoreType.DMA((2,))],
        compiler_params=LIMIT,
        cost_estimate=pl.CostEstimate(flops=2 * 2**28, bytes_accessed=5 * 2**19, transcendentals=0),
    )(near(u_near), near(inverses), near(early_strips), near(early_solved))


def finish(arrays, parts):
    rows, columns = parts[0].shape
    return pl.pallas_call(
        finish_kernel,
        name="finish",
        out_shape=(pltpu.HBM(parts[0].shape, F32),) * 4,
        in_specs=[VMEM] * 12 + [ANY] * 2,
        out_specs=[ANY] * 4,
        input_output_aliases={12: 0, 13: 1},
        scratch_shapes=[
            on_chip(2, 2, EDGE, columns),
            on_chip(2, 2, rows, TILE),
            pltpu.SemaphoreType.DMA((10,)),
        ],
        compiler_params=LIMIT,
    )(*(near(a) for a in arrays), *parts)


def local(velocity):
    to_high_x, to_low_x, to_y_first, to_y_second, u_near, near_low, near_high, inverses, *tables = pack(velocity[0])
    to_high_x, to_y_first, to_low_x, to_y_second, strips_x, solved_x = lead(
        u_near, inverses, (to_high_x, to_y_first, to_low_x, to_y_second)
    )
    gx = lax.axis_size("gx")
    first, second = trades_along_y()
    messages = (
        lax.ppermute(to_high_x, "gx", [(i, (i + 1) % gx) for i in range(gx)]),
        lax.ppermute(to_y_first, ("gx", "gy"), first),
        lax.ppermute(to_low_x, "gx", [(i, (i - 1) % gx) for i in range(gx)]),
        lax.ppermute(to_y_second, ("gx", "gy"), second),
    )
    strips_x, dx, dxx, strips_y, solved_y = interior(u_near, inverses, strips_x, solved_x)
    arrays = (*messages, u_near, near_low, near_high, *tables, strips_x, strips_y, solved_y)
    dx, dxx, dy, dyy = finish(arrays, (dx, dxx))
    return tuple(o[None] for o in (dx, dy, dxx, dyy))


def solution(mesh):
    placed = P(None, "gx", "gy")
    return jax.shard_map(local, mesh=mesh, in_specs=(placed,), out_specs=(placed,) * 4, check_vma=False)
```

```python
import math

import jax
import jax.numpy as jnp
from jax import lax
from jax.experimental import pallas as pl
from jax.experimental.pallas import tpu as pltpu
from jax.sharding import PartitionSpec as P

F32 = jnp.float32
BF16 = jnp.bfloat16

COUPLINGS = (1.0 / 3.0, 2.0 / 11.0)
CENTRES = (7.0 / 9.0, 12.0 / 11.0 + 6.0 / 44.0)
BESIDES = (1.0 / 36.0, 3.0 / 44.0)

ROOTS = tuple(math.sqrt(1.0 - 4.0 * a * a) for a in COUPLINGS)
RATIOS = tuple((root - 1.0) / (2.0 * a) for a, root in zip(COUPLINGS, ROOTS))
SCALES = tuple((c - b / a) / root for a, b, c, root in zip(COUPLINGS, BESIDES, CENTRES, ROOTS))
PEAKS = tuple((c + 2.0 * b * r) / root - h for b, c, r, root, h in zip(BESIDES, CENTRES, RATIOS, ROOTS, SCALES))

WINDOW = 256
TILE = 128
STRIP = 32
EDGE = 24
REACH = 64
MESSAGE = 8

ANY = pl.BlockSpec(memory_space=pl.ANY)
VMEM = pl.BlockSpec(memory_space=pltpu.VMEM)
LIMIT = pltpu.CompilerParams(vmem_limit_bytes=16 * 2**20)


def differences(cells, axis):
    length = cells.shape[axis]
    here = pltpu.roll(cells, length - 1, axis) - cells
    before = pltpu.roll(here, 1, axis)
    return here + before, here - before


def powers(ratio, exponent):
    product = jnp.where(exponent < REACH, F32(1.0), F32(0.0))
    for bit in range(REACH.bit_length() - 1):
        factor = jnp.where((exponent & (1 << bit)) != 0, F32(ratio ** (1 << bit)), F32(1.0))
        product = product * factor
    return product


def tail_weights(high):
    at = lax.broadcasted_iota(jnp.int32, (STRIP, TILE), 0)
    known = (at >= 1) & (at < STRIP - 1)
    exponent = (STRIP - 2 - at) if high else (at - 1)
    return [jnp.where(known, powers(ratio, exponent), 0.0) for ratio in RATIOS]


def message(strip, high, weights):
    tails = [
        jnp.sum(part * weight[:, : strip.shape[1]], axis=0, keepdims=True)
        for part, weight in zip(differences(strip, 0), weights)
    ]
    near = pltpu.roll(strip[STRIP - 8 :], 2, 0) if high else strip[:8]
    row = lax.broadcasted_iota(jnp.int32, near.shape, 0)
    return jnp.where(row < 2, near, jnp.where(row == 2, tails[0], tails[1]))


def tiles_of(length):
    step = min(length, TILE)
    return [pl.ds(k * step, step) for k in range(length // step)]


def halves(value):
    upper = value.astype(BF16).astype(F32)
    return upper, value - upper


def put_inverses(k_ref):
    i = lax.broadcasted_iota(jnp.int32, (TILE, TILE), 0)
    j = lax.broadcasted_iota(jnp.int32, (TILE, TILE), 1)
    blocks = WINDOW // TILE
    for s in range(2):
        for apart in range(1 - blocks, blocks):
            distance = jnp.abs(j - i + apart * TILE)
            weights = SCALES[s] * powers(RATIOS[s], distance)
            if apart == 0:
                weights = jnp.where(distance == 0, F32(SCALES[s] + PEAKS[s]), weights)
            upper, lower = halves(weights)
            for p, part in enumerate((upper, lower)):
                for first in range(blocks):
                    if 0 <= first + apart < blocks:
                        at_i, at_j = pl.ds(first * TILE, TILE), pl.ds((first + apart) * TILE, TILE)
                        k_ref[2 * s + p, at_i, at_j] = part.astype(BF16)


def put_side_tables(table_x, table_y):
    at = lax.broadcasted_iota(jnp.int32, (EDGE, TILE), 0)
    lane = lax.broadcasted_iota(jnp.int32, (8, TILE), 1)
    row = lax.broadcasted_iota(jnp.int32, (8, TILE), 0)
    for s in range(2):
        for side in range(2):
            table_x[s, side] = powers(RATIOS[s], (EDGE - 1 - at) if side else at)
            within = (TILE - 1 - lane) if side else lane
            first = 4 * side + 2 * s
            lines = jnp.where(row == first, powers(RATIOS[s], within), 0.0)
            lines = jnp.where((row == first + 1) & (within == 0), 1.0, lines)
            upper, lower = halves(lines)
            stack = jnp.concatenate([upper, upper, lower, jnp.zeros_like(upper)], axis=0)
            block = 2 * s + side
            table_y[:, pl.ds(block * TILE, TILE)] = stack.astype(BF16)


def low_goes_first():
    next_chip_first = 2 * lax.axis_index("gx") < lax.axis_size("gx")
    return next_chip_first == (lax.rem(lax.axis_index("gy"), 2) == 0)


def trades_along_y():
    gx, gy = lax.axis_size("gx"), lax.axis_size("gy")
    next_chip = [(y, (y - 1) % gy if y % 2 == 0 else (y + 1) % gy) for y in range(gy)]
    same_chip = [(y, y + 1 if y % 2 == 0 else y - 1) for y in range(gy)]
    first, second = [], []
    for x in range(gx):
        orders = (next_chip, same_chip) if 2 * x < gx else (same_chip, next_chip)
        for found, pairs in zip((first, second), orders):
            found += [(x * gy + source, x * gy + target) for source, target in pairs]
    return first, second


def pack_kernel(
    u_ref, to_high_x, to_low_x, to_y_first, to_y_second, u_near, near_low, near_high, k_ref, table_x, table_y, sems
):
    rows, columns = u_ref.shape
    across = [pl.ds(0, TILE), pl.ds(columns - TILE, TILE)]
    pieces = [(pl.ds(0, rows), lanes) for lanes in across]
    order = (2, 3, 0, 1, 4)
    if columns > 2 * TILE:
        middle = pl.ds(TILE, columns - 2 * TILE)
        pieces += [(pl.ds(0, STRIP), middle), (pl.ds(rows - STRIP, STRIP), middle)]
        if rows > 2 * STRIP:
            pieces.append((pl.ds(STRIP, rows - 2 * STRIP), middle))
    copies = [
        pltpu.make_async_copy(u_ref.at[lines, lanes], u_near.at[lines, lanes], sems.at[k])
        for k, (lines, lanes) in enumerate(pieces)
    ]
    for k in order:
        if k < len(copies):
            copies[k].start()
    low_first = low_goes_first()
    weights_low, weights_high = tail_weights(False), tail_weights(True)
    put_inverses(k_ref)
    put_side_tables(table_x, table_y)
    def put_x(lanes):
        to_low_x[:, lanes] = message(u_near[pl.ds(0, STRIP), lanes], False, weights_low)
        to_high_x[:, lanes] = message(u_near[pl.ds(rows - STRIP, STRIP), lanes], True, weights_high)

    for copy in copies[2:4]:
        copy.wait()
    for lanes in tiles_of(columns)[1:-1]:
        put_x(lanes)
    low, high = [], []
    for k in range(2):
        copies[k].wait()
        put_x(across[k])
        turned = u_near[:, across[k]].T
        side = turned[TILE - STRIP :] if k else turned[:STRIP]
        (near_high if k else near_low)[...] = side[STRIP - 8 :] if k else side[:8]
        for lanes in tiles_of(rows):
            part = side[:, lanes.start : lanes.start + lanes.size]
            (high if k else low).append(message(part, k == 1, (weights_low, weights_high)[k]))
    for lanes, to_low, to_high in zip(tiles_of(rows), low, high):
        to_y_first[:, lanes] = jnp.where(low_first, to_low, to_high)
        to_y_second[:, lanes] = jnp.where(low_first, to_high, to_low)
    for copy in copies[4:]:
        copy.wait()


def only_known(rhs, axis):
    length, step = rhs.shape[axis], 8 if axis == 0 else TILE
    at = lax.broadcasted_iota(jnp.int32, [step if k == axis else 1 for k in range(2)], axis)
    first, middle, last = (
        lax.slice_in_dim(rhs, low, high, axis=axis) for low, high in ((0, step), (step, length - step), (length - step, length))
    )
    parts = [jnp.where(at >= 1, first, 0.0), middle, jnp.where(at < step - 1, last, 0.0)]
    return jnp.concatenate([p for p in parts if p.shape[axis] > 0], axis=axis)


def product(a, b):
    dot = lambda p, q: jnp.dot(p, q, preferred_element_type=F32)
    return dot(a[0], b[0]) + dot(a[1], b[0]) + dot(a[0], b[1])


def split(value):
    upper = value.astype(BF16)
    return upper, (value - upper.astype(F32)).astype(BF16)


def solve_x(u_ref, k_ref, strips, solved_ref):
    rows, columns = u_ref.shape
    span = min(columns, WINDOW)
    for j in range(columns // span):
        tiles = [differences(u_ref[:, pl.ds(j * span + t.start, t.size)], 0) for t in tiles_of(span)]
        lanes = pl.ds(j * span, span)
        for s in range(2):
            inverse = k_ref[2 * s, :rows, :rows], k_ref[2 * s + 1, :rows, :rows]
            rhs = jnp.concatenate([only_known(tile[s], 0) for tile in tiles], axis=1)
            solved = product(inverse, split(rhs))
            solved_ref[s, :, lanes] = solved
            strips[s, 0, :, lanes] = solved[:EDGE]
            strips[s, 1, :, lanes] = solved[rows - EDGE :]


def solve_y(u_ref, k_ref, strips, solved_ref):
    rows, columns = u_ref.shape
    span = min(columns, WINDOW)
    lane = lax.broadcasted_iota(jnp.int32, (1, TILE), 1)
    step = min(rows, 64)
    both = [differences(u_ref[pl.ds(i * step, step), :], 1) for i in range(rows // step)]
    for s in range(2):
        inverse = k_ref[2 * s, :span, :span], k_ref[2 * s + 1, :span, :span]
        values = jnp.concatenate([only_known(piece[s], 1) for piece in both], axis=0)
        rhs = split(values)
        count = columns // span
        stacked = [jnp.concatenate([part[:, w * span : (w + 1) * span] for w in range(count)], axis=0) for part in rhs]
        solved = product(stacked, inverse)
        tiles = [solved[w * rows : (w + 1) * rows, t.start : t.start + t.size] for w in range(count) for t in tiles_of(span)]
        per = span // TILE
        added = {}
        for w in range(1, count):
            edge = w * span
            before = tiles[w * per - 1][:, TILE - 1 :] - PEAKS[s] * values[:, edge - 1 : edge]
            after = tiles[w * per][:, :1] - PEAKS[s] * values[:, edge : edge + 1]
            added[w * per] = before * powers(RATIOS[s], lane + 1)
            added[w * per - 1] = after * powers(RATIOS[s], TILE - lane)
        for t, value in added.items():
            tiles[t] = tiles[t] + value
        strips[s, 0] = tiles[0]
        strips[s, 1] = tiles[-1]
        for t in range(1, len(tiles) - 1):
            solved_ref[s, :, pl.ds((t - 1) * TILE, TILE)] = tiles[t]


def solves_x_early():
    return (lax.axis_index("gx") == 0) & (lax.axis_index("gy") < 2)


def lead_kernel(u_ref, k_ref, *refs):
    messages, passed, (strips_x, solved_x) = refs[:4], refs[4:8], refs[8:]
    for message_ref, passed_ref in zip(messages, passed):
        passed_ref[...] = message_ref[...]

    @pl.when(solves_x_early())
    def _():
        solve_x(u_ref, k_ref, strips_x, solved_x)


def interior_kernel(u_ref, k_ref, early_strips, early_solved, *refs):
    strips_x, dx, dxx, strips_y, solved_y, solved_x, sems = refs
    rows, columns = u_ref.shape

    def inner_copies(source):
        if rows <= 2 * EDGE:
            return []
        inner = pl.ds(EDGE, rows - 2 * EDGE)
        return [pltpu.make_async_copy(source.at[s, inner], out.at[inner], sems.at[s]) for s, out in enumerate((dx, dxx))]

    @pl.when(solves_x_early())
    def _():
        copies = inner_copies(early_solved)
        for copy in copies:
            copy.start()
        strips_x[...] = early_strips[...]
        solve_y(u_ref, k_ref, strips_y, solved_y)
        for copy in copies:
            copy.wait()

    @pl.when(jnp.logical_not(solves_x_early()))
    def _():
        solve_x(u_ref, k_ref, strips_x, solved_x)
        copies = inner_copies(solved_x)
        for copy in copies:
            copy.start()
        solve_y(u_ref, k_ref, strips_y, solved_y)
        for copy in copies:
            copy.wait()


def side_terms(around, tails, high):
    found = []
    for s, part in enumerate(differences(around, 0)):
        nearest, outer = (part[1:2], part[2:3]) if high else (part[2:3], part[1:2])
        total = nearest + RATIOS[s] * (outer + RATIOS[s] * tails[s])
        found.append((SCALES[s] * total, PEAKS[s] * nearest))
    return found


def both_sides(from_low, from_high, own_low, own_high):
    row = lax.broadcasted_iota(jnp.int32, own_low.shape, 0)
    low = jnp.where(row < 2, from_low, pltpu.roll(own_low, 2, 0))
    high = jnp.where(row < 2, pltpu.roll(own_high, 2, 0), pltpu.roll(from_high, 2, 0))
    tails = lambda m: (m[2:3], m[3:4])
    return side_terms(low, tails(from_low), False), side_terms(high, tails(from_high), True)


def finish_kernel(
    from_low_x, from_y_first, from_high_x, from_y_second, u_near, near_low, near_high, table_x, table_y, strips_x, strips_y, solved_y, *refs
):
    dx, dxx, dy, dyy, done_x, done_y, sems = refs[2:]
    rows, columns = dx.shape
    started = []

    def send(source, target):
        copy = pltpu.make_async_copy(source, target, sems.at[len(started)])
        copy.start()
        started.append(copy)

    if columns > 2 * TILE:
        for s, out in enumerate((dy, dyy)):
            send(solved_y.at[s], out.at[:, pl.ds(TILE, columns - 2 * TILE)])
    step = min(columns, TILE)
    row = lax.broadcasted_iota(jnp.int32, (8, 1), 0)
    tiles = tiles_of(columns)
    own = lambda start, lanes: u_near[pl.ds(start, 8), lanes]
    for lanes in tiles:
        terms = both_sides(from_low_x[:, lanes], from_high_x[:, lanes], own(0, lanes), own(rows - 8, lanes))
        for s in range(2):
            for side in range(2):
                near, first = terms[side][s]
                extra = near * table_x[s, side, :, :step]
                first = jnp.where(row == (7 if side else 0), first, 0.0)
                if side:
                    extra = jnp.concatenate([extra[: EDGE - 8], extra[EDGE - 8 :] + first], axis=0)
                else:
                    extra = jnp.concatenate([extra[:8] + first, extra[8:]], axis=0)
                done_x[s, side, :, lanes] = strips_x[s, side, :, lanes] + extra
    for s, out in enumerate((dx, dxx)):
        for side in range(2):
            send(done_x.at[s, side], out.at[pl.ds(side * (rows - EDGE), EDGE)])

    low_first = low_goes_first()
    for lines in tiles_of(rows):
        first, second = from_y_first[:, lines], from_y_second[:, lines]
        from_low, from_high = jnp.where(low_first, first, second), jnp.where(low_first, second, first)
        terms = both_sides(from_low, from_high, near_low[:, lines], near_high[:, lines])
        stacked = jnp.zeros((8, lines.size), F32)
        for side in range(2):
            for s in range(2):
                for which in range(2):
                    stacked = jnp.where(row == 4 * side + 2 * s + which, terms[side][s][which], stacked)
        upper, lower = halves(stacked)
        factors = jnp.concatenate([upper, lower, upper, jnp.zeros_like(upper)], axis=0).astype(BF16)
        added = lax.dot_general(factors, table_y[...], (((0,), (0,)), ((), ())), preferred_element_type=F32)
        for s, out in enumerate((dy, dyy)):
            for side in range(2):
                block = 2 * s + side
                done_y[s, side, lines] = strips_y[s, side, lines] + added[:, block * TILE : (block + 1) * TILE]
                send(done_y.at[s, side, lines], out.at[lines, pl.ds(side * (columns - TILE), TILE)])
    for copy in started:
        copy.wait()


def on_chip(*shape):
    return pltpu.VMEM(shape, F32)


def near(array):
    return pltpu.with_memory_space_constraint(array, pltpu.VMEM)


def pack(u):
    rows, columns = u.shape
    wide = max(rows, columns)
    return pl.pallas_call(
        pack_kernel,
        name="pack",
        out_shape=(
            on_chip(MESSAGE, columns),
            on_chip(MESSAGE, columns),
            on_chip(MESSAGE, wide),
            on_chip(MESSAGE, wide),
            on_chip(rows, columns),
            on_chip(8, rows),
            on_chip(8, rows),
            pltpu.VMEM((4, WINDOW, WINDOW), BF16),
            on_chip(2, 2, EDGE, TILE),
            pltpu.VMEM((32, 4 * TILE), BF16),
        ),
        in_specs=[ANY],
        out_specs=[VMEM] * 10,
        scratch_shapes=[pltpu.SemaphoreType.DMA((5,))],
        compiler_params=LIMIT,
    )(pltpu.with_memory_space_constraint(u, pltpu.HBM))


def shapes_x(rows, columns):
    return on_chip(2, 2, EDGE, columns), on_chip(2, rows, columns)


def lead(u_near, inverses, messages):
    size = u_near.shape
    return pl.pallas_call(
        lead_kernel,
        name="lead",
        out_shape=tuple(on_chip(*a.shape) for a in messages) + shapes_x(*size),
        in_specs=[VMEM] * 6,
        out_specs=[VMEM] * 6,
        compiler_params=LIMIT,
    )(near(u_near), near(inverses), *(near(a) for a in messages))


def interior(u_near, inverses, early_strips, early_solved):
    rows, columns = u_near.shape
    strips_x, solved_x = shapes_x(rows, columns)
    return pl.pallas_call(
        interior_kernel,
        name="interior",
        out_shape=(strips_x,)
        + (pltpu.HBM(u_near.shape, F32),) * 2
        + (on_chip(2, 2, rows, TILE), on_chip(2, rows, max(columns - 2 * TILE, TILE))),
        in_specs=[VMEM] * 4,
        out_specs=[VMEM] + [ANY] * 2 + [VMEM] * 2,
        scratch_shapes=[solved_x, pltpu.SemaphoreType.DMA((2,))],
        compiler_params=LIMIT,
        cost_estimate=pl.CostEstimate(flops=2 * 2**28, bytes_accessed=5 * 2**19, transcendentals=0),
    )(near(u_near), near(inverses), near(early_strips), near(early_solved))


def finish(arrays, parts):
    rows, columns = parts[0].shape
    return pl.pallas_call(
        finish_kernel,
        name="finish",
        out_shape=(pltpu.HBM(parts[0].shape, F32),) * 4,
        in_specs=[VMEM] * 12 + [ANY] * 2,
        out_specs=[ANY] * 4,
        input_output_aliases={12: 0, 13: 1},
        scratch_shapes=[
            on_chip(2, 2, EDGE, columns),
            on_chip(2, 2, rows, TILE),
            pltpu.SemaphoreType.DMA((6 + 4 * len(tiles_of(rows)),)),
        ],
        compiler_params=LIMIT,
    )(*(near(a) for a in arrays), *parts)


def local(velocity):
    to_high_x, to_low_x, to_y_first, to_y_second, u_near, near_low, near_high, inverses, *tables = pack(velocity[0])
    to_high_x, to_y_first, to_low_x, to_y_second, strips_x, solved_x = lead(
        u_near, inverses, (to_high_x, to_y_first, to_low_x, to_y_second)
    )
    gx = lax.axis_size("gx")
    first, second = trades_along_y()
    messages = (
        lax.ppermute(to_high_x, "gx", [(i, (i + 1) % gx) for i in range(gx)]),
        lax.ppermute(to_y_first, ("gx", "gy"), first),
        lax.ppermute(to_low_x, "gx", [(i, (i - 1) % gx) for i in range(gx)]),
        lax.ppermute(to_y_second, ("gx", "gy"), second),
    )
    strips_x, dx, dxx, strips_y, solved_y = interior(u_near, inverses, strips_x, solved_x)
    arrays = (*messages, u_near, near_low, near_high, *tables, strips_x, strips_y, solved_y)
    dx, dxx, dy, dyy = finish(arrays, (dx, dxx))
    return tuple(o[None] for o in (dx, dy, dxx, dyy))


def solution(mesh):
    placed = P(None, "gx", "gy")
    return jax.shard_map(local, mesh=mesh, in_specs=(placed,), out_specs=(placed,) * 4, check_vma=False)
```

```python
import math

import jax
import jax.numpy as jnp
from jax import lax
from jax.experimental import pallas as pl
from jax.experimental.pallas import tpu as pltpu
from jax.sharding import PartitionSpec as P

F32 = jnp.float32
BF16 = jnp.bfloat16

COUPLINGS = (1.0 / 3.0, 2.0 / 11.0)
CENTRES = (7.0 / 9.0, 12.0 / 11.0 + 6.0 / 44.0)
BESIDES = (1.0 / 36.0, 3.0 / 44.0)

ROOTS = tuple(math.sqrt(1.0 - 4.0 * a * a) for a in COUPLINGS)
RATIOS = tuple((root - 1.0) / (2.0 * a) for a, root in zip(COUPLINGS, ROOTS))
SCALES = tuple((c - b / a) / root for a, b, c, root in zip(COUPLINGS, BESIDES, CENTRES, ROOTS))
PEAKS = tuple((c + 2.0 * b * r) / root - h for b, c, r, root, h in zip(BESIDES, CENTRES, RATIOS, ROOTS, SCALES))

WINDOW = 256
TILE = 128
STRIP = 32
EDGE = 24
REACH = 64
MESSAGE = 4

ANY = pl.BlockSpec(memory_space=pl.ANY)
VMEM = pl.BlockSpec(memory_space=pltpu.VMEM)
LIMIT = pltpu.CompilerParams(vmem_limit_bytes=16 * 2**20)


def differences(cells, axis):
    length = cells.shape[axis]
    here = pltpu.roll(cells, length - 1, axis) - cells
    before = pltpu.roll(here, 1, axis)
    return here + before, here - before


def powers(ratio, exponent):
    product = jnp.where(exponent < REACH, F32(1.0), F32(0.0))
    for bit in range(REACH.bit_length() - 1):
        factor = jnp.where((exponent & (1 << bit)) != 0, F32(ratio ** (1 << bit)), F32(1.0))
        product = product * factor
    return product


def tail_weights(high):
    at = lax.broadcasted_iota(jnp.int32, (STRIP, TILE), 0)
    known = (at >= 1) & (at < STRIP - 1)
    exponent = (STRIP - 2 - at) if high else (at - 1)
    return [jnp.where(known, powers(ratio, exponent), 0.0) for ratio in RATIOS]


def message(strip, high, weights):
    tails = [
        jnp.sum(part * weight[:, : strip.shape[1]], axis=0, keepdims=True)
        for part, weight in zip(differences(strip, 0), weights)
    ]
    near = pltpu.roll(strip[STRIP - 8 :], 2, 0) if high else strip[:8]
    row = lax.broadcasted_iota(jnp.int32, near.shape, 0)
    return jnp.where(row < 2, near, jnp.where(row == 2, tails[0], tails[1]))[:MESSAGE]


def tiles_of(length):
    step = min(length, TILE)
    return [pl.ds(k * step, step) for k in range(length // step)]


def halves(value):
    upper = value.astype(BF16).astype(F32)
    return upper, value - upper


def put_inverses(k_ref):
    i = lax.broadcasted_iota(jnp.int32, (TILE, TILE), 0)
    j = lax.broadcasted_iota(jnp.int32, (TILE, TILE), 1)
    blocks = WINDOW // TILE
    for s in range(2):
        for apart in range(1 - blocks, blocks):
            distance = jnp.abs(j - i + apart * TILE)
            weights = SCALES[s] * powers(RATIOS[s], distance)
            if apart == 0:
                weights = jnp.where(distance == 0, F32(SCALES[s] + PEAKS[s]), weights)
            upper, lower = halves(weights)
            for p, part in enumerate((upper, lower)):
                for first in range(blocks):
                    if 0 <= first + apart < blocks:
                        at_i, at_j = pl.ds(first * TILE, TILE), pl.ds((first + apart) * TILE, TILE)
                        k_ref[2 * s + p, at_i, at_j] = part.astype(BF16)


def put_side_tables(table_x, table_y):
    at = lax.broadcasted_iota(jnp.int32, (EDGE, TILE), 0)
    lane = lax.broadcasted_iota(jnp.int32, (8, TILE), 1)
    row = lax.broadcasted_iota(jnp.int32, (8, TILE), 0)
    for s in range(2):
        for side in range(2):
            table_x[s, side] = powers(RATIOS[s], (EDGE - 1 - at) if side else at)
            within = (TILE - 1 - lane) if side else lane
            first = 4 * side + 2 * s
            lines = jnp.where(row == first, powers(RATIOS[s], within), 0.0)
            lines = jnp.where((row == first + 1) & (within == 0), 1.0, lines)
            upper, lower = halves(lines)
            stack = jnp.concatenate([upper, upper, lower, jnp.zeros_like(upper)], axis=0)
            block = 2 * s + side
            table_y[:, pl.ds(block * TILE, TILE)] = stack.astype(BF16)


def low_goes_first():
    next_chip_first = 2 * lax.axis_index("gx") < lax.axis_size("gx")
    return next_chip_first == (lax.rem(lax.axis_index("gy"), 2) == 0)


def trades_along_y():
    gx, gy = lax.axis_size("gx"), lax.axis_size("gy")
    next_chip = [(y, (y - 1) % gy if y % 2 == 0 else (y + 1) % gy) for y in range(gy)]
    same_chip = [(y, y + 1 if y % 2 == 0 else y - 1) for y in range(gy)]
    first, second = [], []
    for x in range(gx):
        orders = (next_chip, same_chip) if 2 * x < gx else (same_chip, next_chip)
        for found, pairs in zip((first, second), orders):
            found += [(x * gy + source, x * gy + target) for source, target in pairs]
    return first, second


def pack_kernel(
    u_ref, to_high_x, to_low_x, to_y_first, to_y_second, u_near, near_low, near_high, k_ref, table_x, table_y, sems
):
    rows, columns = u_ref.shape
    across = [pl.ds(0, TILE), pl.ds(columns - TILE, TILE)]
    pieces = [(pl.ds(0, rows), lanes) for lanes in across]
    order = (2, 3, 0, 1, 4)
    if columns > 2 * TILE:
        middle = pl.ds(TILE, columns - 2 * TILE)
        pieces += [(pl.ds(0, STRIP), middle), (pl.ds(rows - STRIP, STRIP), middle)]
        if rows > 2 * STRIP:
            pieces.append((pl.ds(STRIP, rows - 2 * STRIP), middle))
    copies = [
        pltpu.make_async_copy(u_ref.at[lines, lanes], u_near.at[lines, lanes], sems.at[k])
        for k, (lines, lanes) in enumerate(pieces)
    ]
    for k in order:
        if k < len(copies):
            copies[k].start()
    low_first = low_goes_first()
    weights_low, weights_high = tail_weights(False), tail_weights(True)
    put_inverses(k_ref)
    put_side_tables(table_x, table_y)
    def put_x(lanes):
        to_low_x[:, lanes] = message(u_near[pl.ds(0, STRIP), lanes], False, weights_low)
        to_high_x[:, lanes] = message(u_near[pl.ds(rows - STRIP, STRIP), lanes], True, weights_high)

    for copy in copies[2:4]:
        copy.wait()
    for lanes in tiles_of(columns)[1:-1]:
        put_x(lanes)
    low, high = [], []
    for k in range(2):
        copies[k].wait()
        put_x(across[k])
        turned = u_near[:, across[k]].T
        side = turned[TILE - STRIP :] if k else turned[:STRIP]
        (near_high if k else near_low)[...] = side[STRIP - 8 :] if k else side[:8]
        for lanes in tiles_of(rows):
            part = side[:, lanes.start : lanes.start + lanes.size]
            (high if k else low).append(message(part, k == 1, (weights_low, weights_high)[k]))
    for lanes, to_low, to_high in zip(tiles_of(rows), low, high):
        to_y_first[:, lanes] = jnp.where(low_first, to_low, to_high)
        to_y_second[:, lanes] = jnp.where(low_first, to_high, to_low)
    for copy in copies[4:]:
        copy.wait()


def only_known(rhs, axis):
    length, step = rhs.shape[axis], 8 if axis == 0 else TILE
    at = lax.broadcasted_iota(jnp.int32, [step if k == axis else 1 for k in range(2)], axis)
    first, middle, last = (
        lax.slice_in_dim(rhs, low, high, axis=axis) for low, high in ((0, step), (step, length - step), (length - step, length))
    )
    parts = [jnp.where(at >= 1, first, 0.0), middle, jnp.where(at < step - 1, last, 0.0)]
    return jnp.concatenate([p for p in parts if p.shape[axis] > 0], axis=axis)


def product(a, b):
    dot = lambda p, q: jnp.dot(p, q, preferred_element_type=F32)
    return dot(a[0], b[0]) + dot(a[1], b[0]) + dot(a[0], b[1])


def split(value):
    upper = value.astype(BF16)
    return upper, (value - upper.astype(F32)).astype(BF16)


def solve_x(u_ref, k_ref, strips, solved_ref, copies):
    rows, columns = u_ref.shape
    span = min(columns, WINDOW)
    for s in range(2):
        inverse = k_ref[2 * s, :rows, :rows], k_ref[2 * s + 1, :rows, :rows]
        for j in range(columns // span):
            tiles = [differences(u_ref[:, pl.ds(j * span + t.start, t.size)], 0) for t in tiles_of(span)]
            lanes = pl.ds(j * span, span)
            rhs = jnp.concatenate([only_known(tile[s], 0) for tile in tiles], axis=1)
            solved = product(inverse, split(rhs))
            solved_ref[s, :, lanes] = solved
            strips[s, 0, :, lanes] = solved[:EDGE]
            strips[s, 1, :, lanes] = solved[rows - EDGE :]
        if s < len(copies):
            copies[s].start()


def inner_copies(solved_ref, outs, sems):
    rows = solved_ref.shape[1]
    if rows <= 2 * EDGE:
        return []
    inner = pl.ds(EDGE, rows - 2 * EDGE)
    return [pltpu.make_async_copy(solved_ref.at[s, inner], out.at[inner], sems.at[s]) for s, out in enumerate(outs)]


def solve_y(u_ref, k_ref, strips, solved_ref):
    rows, columns = u_ref.shape
    span = min(columns, WINDOW)
    lane = lax.broadcasted_iota(jnp.int32, (1, TILE), 1)
    step = min(rows, 64)
    both = [differences(u_ref[pl.ds(i * step, step), :], 1) for i in range(rows // step)]
    for s in range(2):
        inverse = k_ref[2 * s, :span, :span], k_ref[2 * s + 1, :span, :span]
        values = jnp.concatenate([only_known(piece[s], 1) for piece in both], axis=0)
        rhs = split(values)
        count = columns // span
        stacked = [jnp.concatenate([part[:, w * span : (w + 1) * span] for w in range(count)], axis=0) for part in rhs]
        solved = product(stacked, inverse)
        tiles = [solved[w * rows : (w + 1) * rows, t.start : t.start + t.size] for w in range(count) for t in tiles_of(span)]
        per = span // TILE
        added = {}
        for w in range(1, count):
            edge = w * span
            before = tiles[w * per - 1][:, TILE - 1 :] - PEAKS[s] * values[:, edge - 1 : edge]
            after = tiles[w * per][:, :1] - PEAKS[s] * values[:, edge : edge + 1]
            added[w * per] = before * powers(RATIOS[s], lane + 1)
            added[w * per - 1] = after * powers(RATIOS[s], TILE - lane)
        for t, value in added.items():
            tiles[t] = tiles[t] + value
        strips[s, 0] = tiles[0]
        strips[s, 1] = tiles[-1]
        for t in range(1, len(tiles) - 1):
            solved_ref[s, :, pl.ds((t - 1) * TILE, TILE)] = tiles[t]


FIRST, BETWEEN, LAST = range(3)


def solves_x():
    ends = jnp.where(lax.axis_index("gy") < 2, FIRST, BETWEEN)
    return jnp.where(lax.axis_index("gx") == 0, ends, LAST)


def first_kernel(u_ref, k_ref, *refs):
    messages, passed, (dx, strips_x, solved_x, sems) = refs[:2], refs[2:4], refs[4:]
    for message_ref, passed_ref in zip(messages, passed):
        passed_ref[...] = message_ref[...]

    @pl.when(solves_x() == FIRST)
    def _():
        copies = inner_copies(solved_x, (dx,), sems)
        solve_x(u_ref, k_ref, strips_x, solved_x, copies)
        for copy in copies:
            copy.wait()


def between_kernel(u_ref, k_ref, *refs):
    messages, passed, (strips_x, solved_x) = refs[:2], refs[3:5], refs[5:]
    for message_ref, passed_ref in zip(messages, passed):
        passed_ref[...] = message_ref[...]

    @pl.when(solves_x() == BETWEEN)
    def _():
        solve_x(u_ref, k_ref, strips_x, solved_x, [])


def interior_kernel(u_ref, k_ref, _, first_strips, first_solved, between_strips, between_solved, *refs):
    strips_x, dx, dxx, strips_y, solved_y, solved_x, sems = refs
    for when, strips, solved in (
        (FIRST, first_strips, first_solved),
        (BETWEEN, between_strips, between_solved),
        (LAST, strips_x, solved_x),
    ):

        @pl.when(solves_x() == when)
        def _():
            copies = inner_copies(solved, (dx, dxx), sems)
            if when == LAST:
                solve_x(u_ref, k_ref, strips, solved, copies)
            else:
                if when == FIRST:
                    copies = copies[1:]
                for copy in copies:
                    copy.start()
                strips_x[...] = strips[...]
            solve_y(u_ref, k_ref, strips_y, solved_y)
            for copy in copies:
                copy.wait()


def side_terms(around, tails, high):
    found = []
    for s, part in enumerate(differences(around, 0)):
        nearest, outer = (part[1:2], part[2:3]) if high else (part[2:3], part[1:2])
        total = nearest + RATIOS[s] * (outer + RATIOS[s] * tails[s])
        found.append((SCALES[s] * total, PEAKS[s] * nearest))
    return found


def low_terms(message, own):
    row = lax.broadcasted_iota(jnp.int32, own.shape, 0)
    around = jnp.where(row < 2, jnp.concatenate([message, message], axis=0), pltpu.roll(own, 2, 0))
    return side_terms(around, (message[2:3], message[3:4]), False)


def high_terms(message, own):
    row = lax.broadcasted_iota(jnp.int32, own.shape, 0)
    around = pltpu.roll(jnp.where(row < 2, jnp.concatenate([message, message], axis=0), own), 2, 0)
    return side_terms(around, (message[2:3], message[3:4]), True)


def add_side_x(terms, side, lanes, table_x, strips_x, put):
    row = lax.broadcasted_iota(jnp.int32, (8, 1), 0)
    for s in range(2):
        near, first = terms[s]
        extra = near * table_x[s, side, :, : lanes.size]
        first = jnp.where(row == (7 if side else 0), first, 0.0)
        if side:
            extra = jnp.concatenate([extra[: EDGE - 8], extra[EDGE - 8 :] + first], axis=0)
        else:
            extra = jnp.concatenate([extra[:8] + first, extra[8:]], axis=0)
        put[s, :, lanes] = strips_x[s, side, :, lanes] + extra


def sides_kernel(
    from_y_first, from_y_second, near_low, near_high, table_y, strips_y, done_y
):
    rows = near_low.shape[1]
    row = lax.broadcasted_iota(jnp.int32, (8, 1), 0)
    low_first = low_goes_first()
    for lines in tiles_of(rows):
        first, second = from_y_first[:, lines], from_y_second[:, lines]
        from_low, from_high = jnp.where(low_first, first, second), jnp.where(low_first, second, first)
        terms = low_terms(from_low, near_low[:, lines]), high_terms(from_high, near_high[:, lines])
        stacked = jnp.zeros((8, lines.size), F32)
        for side in range(2):
            for s in range(2):
                for which in range(2):
                    stacked = jnp.where(row == 4 * side + 2 * s + which, terms[side][s][which], stacked)
        upper, lower = halves(stacked)
        factors = jnp.concatenate([upper, lower, upper, jnp.zeros_like(upper)], axis=0).astype(BF16)
        added = lax.dot_general(factors, table_y[...], (((0,), (0,)), ((), ())), preferred_element_type=F32)
        for s in range(2):
            for side in range(2):
                block = 2 * s + side
                done_y[s, side, lines] = strips_y[s, side, lines] + added[:, block * TILE : (block + 1) * TILE]


def finish_kernel(from_low_x, from_high_x, u_near, table_x, strips_x, done_y, solved_y, *refs):
    dx, dxx, dy, dyy, done_x, sems = refs[2:]
    rows, columns = dx.shape
    started = []

    def send(source, target):
        copy = pltpu.make_async_copy(source, target, sems.at[len(started)])
        copy.start()
        started.append(copy)

    for s, out in enumerate((dy, dyy)):
        for side in range(2):
            send(done_y.at[s, side], out.at[:, pl.ds(side * (columns - TILE), TILE)])
    for lanes in tiles_of(columns):
        add_side_x(low_terms(from_low_x[:, lanes], u_near[pl.ds(0, 8), lanes]), 0, lanes, table_x, strips_x, done_x.at[0])
        add_side_x(high_terms(from_high_x[:, lanes], u_near[pl.ds(rows - 8, 8), lanes]), 1, lanes, table_x, strips_x, done_x.at[1])
    for s, out in enumerate((dx, dxx)):
        for side in range(2):
            send(done_x.at[side, s], out.at[pl.ds(side * (rows - EDGE), EDGE)])
    if columns > 2 * TILE:
        for s, out in enumerate((dy, dyy)):
            send(solved_y.at[s], out.at[:, pl.ds(TILE, columns - 2 * TILE)])
    for copy in started:
        copy.wait()


def on_chip(*shape):
    return pltpu.VMEM(shape, F32)


def near(array):
    return pltpu.with_memory_space_constraint(array, pltpu.VMEM)


def pack(u):
    rows, columns = u.shape
    wide = max(rows, columns)
    return pl.pallas_call(
        pack_kernel,
        name="pack",
        out_shape=(
            on_chip(MESSAGE, columns),
            on_chip(MESSAGE, columns),
            on_chip(MESSAGE, wide),
            on_chip(MESSAGE, wide),
            on_chip(rows, columns),
            on_chip(8, rows),
            on_chip(8, rows),
            pltpu.VMEM((4, WINDOW, WINDOW), BF16),
            on_chip(2, 2, EDGE, TILE),
            pltpu.VMEM((32, 4 * TILE), BF16),
        ),
        in_specs=[ANY],
        out_specs=[VMEM] * 10,
        scratch_shapes=[pltpu.SemaphoreType.DMA((5,))],
        compiler_params=LIMIT,
    )(pltpu.with_memory_space_constraint(u, pltpu.HBM))


def shapes_x(rows, columns):
    return on_chip(2, 2, EDGE, columns), on_chip(2, rows, columns)


def lead(kernel, name, outs, scratch, u_near, inverses, *messages):
    return pl.pallas_call(
        kernel,
        name=name,
        out_shape=tuple(on_chip(*a.shape) for a in messages[:2]) + outs,
        in_specs=[VMEM] * (2 + len(messages)),
        out_specs=[VMEM] * 2 + [ANY] * (len(outs) - 2) + [VMEM] * 2,
        scratch_shapes=scratch,
        compiler_params=LIMIT,
    )(*(near(a) for a in (u_near, inverses, *messages)))


def interior(u_near, inverses, dx, *early):
    rows, columns = u_near.shape
    strips_x, solved_x = shapes_x(rows, columns)
    return pl.pallas_call(
        interior_kernel,
        name="interior",
        out_shape=(strips_x,)
        + (pltpu.HBM(u_near.shape, F32),) * 2
        + (on_chip(2, 2, rows, TILE), on_chip(2, rows, max(columns - 2 * TILE, TILE))),
        in_specs=[VMEM] * 2 + [ANY] + [VMEM] * 4,
        out_specs=[VMEM] + [ANY] * 2 + [VMEM] * 2,
        input_output_aliases={2: 1},
        scratch_shapes=[solved_x, pltpu.SemaphoreType.DMA((2,))],
        compiler_params=LIMIT,
        cost_estimate=pl.CostEstimate(flops=2 * 2**28, bytes_accessed=5 * 2**19, transcendentals=0),
    )(near(u_near), near(inverses), dx, *(near(a) for a in early))


def sides(arrays, strips_y):
    return pl.pallas_call(
        sides_kernel,
        name="sides",
        out_shape=on_chip(*strips_y.shape),
        in_specs=[VMEM] * 6,
        out_specs=VMEM,
        compiler_params=LIMIT,
    )(*(near(a) for a in (*arrays, strips_y)))


def finish(arrays, parts):
    columns = parts[0].shape[1]
    return pl.pallas_call(
        finish_kernel,
        name="finish",
        out_shape=(pltpu.HBM(parts[0].shape, F32),) * 4,
        in_specs=[VMEM] * 7 + [ANY] * 2,
        out_specs=[ANY] * 4,
        input_output_aliases={7: 0, 8: 1},
        scratch_shapes=[on_chip(2, 2, EDGE, columns), pltpu.SemaphoreType.DMA((10,))],
        compiler_params=LIMIT,
    )(*(near(a) for a in arrays), *parts)


def local(velocity):
    to_high_x, to_low_x, to_y_first, to_y_second, u_near, near_low, near_high, inverses, *tables = pack(velocity[0])
    size = u_near.shape
    outs = shapes_x(*size)
    to_high_x, to_y_first, dx, *early = lead(
        first_kernel,
        "solve_first",
        (pltpu.HBM(size, F32),) + outs,
        [pltpu.SemaphoreType.DMA((1,))],
        u_near,
        inverses,
        to_high_x,
        to_y_first,
    )
    to_low_x, to_y_second, *between = lead(between_kernel, "solve_between", outs, [], u_near, inverses, to_low_x, to_y_second, early[0])
    gx = lax.axis_size("gx")
    first, second = trades_along_y()
    from_low_x = lax.ppermute(to_high_x, "gx", [(i, (i + 1) % gx) for i in range(gx)])
    from_y_first = lax.ppermute(to_y_first, ("gx", "gy"), first)
    from_high_x = lax.ppermute(to_low_x, "gx", [(i, (i - 1) % gx) for i in range(gx)])
    from_y_second = lax.ppermute(to_y_second, ("gx", "gy"), second)
    strips_x, dx, dxx, strips_y, solved_y = interior(u_near, inverses, dx, *early, *between)
    table_x, table_y = tables
    done_y = sides((from_y_first, from_y_second, near_low, near_high, table_y), strips_y)
    dx, dxx, dy, dyy = finish((from_low_x, from_high_x, u_near, table_x, strips_x, done_y, solved_y), (dx, dxx))
    return tuple(o[None] for o in (dx, dy, dxx, dyy))


def solution(mesh):
    placed = P(None, "gx", "gy")
    return jax.shard_map(local, mesh=mesh, in_specs=(placed,), out_specs=(placed,) * 4, check_vma=False)
```

```python
import math

import jax
import jax.numpy as jnp
from jax import lax
from jax.experimental import pallas as pl
from jax.experimental.pallas import tpu as pltpu
from jax.sharding import PartitionSpec as P

F32 = jnp.float32
BF16 = jnp.bfloat16

COUPLINGS = (1.0 / 3.0, 2.0 / 11.0)
CENTRES = (7.0 / 9.0, 12.0 / 11.0 + 6.0 / 44.0)
BESIDES = (1.0 / 36.0, 3.0 / 44.0)

ROOTS = tuple(math.sqrt(1.0 - 4.0 * a * a) for a in COUPLINGS)
RATIOS = tuple((root - 1.0) / (2.0 * a) for a, root in zip(COUPLINGS, ROOTS))
SCALES = tuple((c - b / a) / root for a, b, c, root in zip(COUPLINGS, BESIDES, CENTRES, ROOTS))
PEAKS = tuple((c + 2.0 * b * r) / root - h for b, c, r, root, h in zip(BESIDES, CENTRES, RATIOS, ROOTS, SCALES))

WINDOW = 256
TILE = 128
STRIP = 32
EDGE = 24
REACH = 64
MESSAGE = 4

ANY = pl.BlockSpec(memory_space=pl.ANY)
VMEM = pl.BlockSpec(memory_space=pltpu.VMEM)
LIMIT = pltpu.CompilerParams(vmem_limit_bytes=16 * 2**20)


def differences(cells, axis):
    length = cells.shape[axis]
    here = pltpu.roll(cells, length - 1, axis) - cells
    before = pltpu.roll(here, 1, axis)
    return here + before, here - before


def powers(ratio, exponent):
    product = jnp.where(exponent < REACH, F32(1.0), F32(0.0))
    for bit in range(REACH.bit_length() - 1):
        factor = jnp.where((exponent & (1 << bit)) != 0, F32(ratio ** (1 << bit)), F32(1.0))
        product = product * factor
    return product


def tail_weights(high):
    at = lax.broadcasted_iota(jnp.int32, (STRIP, TILE), 0)
    known = (at >= 1) & (at < STRIP - 1)
    exponent = (STRIP - 2 - at) if high else (at - 1)
    return [jnp.where(known, powers(ratio, exponent), 0.0) for ratio in RATIOS]


def message(strip, high, weights):
    tails = [
        jnp.sum(part * weight[:, : strip.shape[1]], axis=0, keepdims=True)
        for part, weight in zip(differences(strip, 0), weights)
    ]
    near = pltpu.roll(strip[STRIP - 8 :], 2, 0) if high else strip[:8]
    row = lax.broadcasted_iota(jnp.int32, near.shape, 0)
    return jnp.where(row < 2, near, jnp.where(row == 2, tails[0], tails[1]))[:MESSAGE]


def tiles_of(length):
    step = min(length, TILE)
    return [pl.ds(k * step, step) for k in range(length // step)]


def halves(value):
    upper = value.astype(BF16).astype(F32)
    return upper, value - upper


def put_inverses(k_ref):
    i = lax.broadcasted_iota(jnp.int32, (TILE, TILE), 0)
    j = lax.broadcasted_iota(jnp.int32, (TILE, TILE), 1)
    blocks = WINDOW // TILE
    for s in range(2):
        for apart in range(1 - blocks, blocks):
            distance = jnp.abs(j - i + apart * TILE)
            weights = SCALES[s] * powers(RATIOS[s], distance)
            if apart == 0:
                weights = jnp.where(distance == 0, F32(SCALES[s] + PEAKS[s]), weights)
            upper, lower = halves(weights)
            for p, part in enumerate((upper, lower)):
                for first in range(blocks):
                    if 0 <= first + apart < blocks:
                        at_i, at_j = pl.ds(first * TILE, TILE), pl.ds((first + apart) * TILE, TILE)
                        k_ref[2 * s + p, at_i, at_j] = part.astype(BF16)


def put_side_tables(table_x, table_y):
    at = lax.broadcasted_iota(jnp.int32, (EDGE, TILE), 0)
    lane = lax.broadcasted_iota(jnp.int32, (8, TILE), 1)
    row = lax.broadcasted_iota(jnp.int32, (8, TILE), 0)
    for s in range(2):
        for side in range(2):
            table_x[s, side] = powers(RATIOS[s], (EDGE - 1 - at) if side else at)
            within = (TILE - 1 - lane) if side else lane
            first = 4 * side + 2 * s
            lines = jnp.where(row == first, powers(RATIOS[s], within), 0.0)
            lines = jnp.where((row == first + 1) & (within == 0), 1.0, lines)
            upper, lower = halves(lines)
            stack = jnp.concatenate([upper, upper, lower, jnp.zeros_like(upper)], axis=0)
            block = 2 * s + side
            table_y[:, pl.ds(block * TILE, TILE)] = stack.astype(BF16)


def low_goes_first():
    next_chip_first = lax.axis_index("gx") == 0
    return next_chip_first == (lax.rem(lax.axis_index("gy"), 2) == 0)


def trades_along_y():
    gx, gy = lax.axis_size("gx"), lax.axis_size("gy")
    next_chip = [(y, (y - 1) % gy if y % 2 == 0 else (y + 1) % gy) for y in range(gy)]
    same_chip = [(y, y + 1 if y % 2 == 0 else y - 1) for y in range(gy)]
    first, second = [], []
    for x in range(gx):
        orders = (next_chip, same_chip) if x == 0 else (same_chip, next_chip)
        for found, pairs in zip((first, second), orders):
            found += [(x * gy + source, x * gy + target) for source, target in pairs]
    return first, second


def pack_kernel(
    u_ref, to_high_x, to_low_x, to_y_first, to_y_second, u_near, near_low, near_high, k_ref, table_x, table_y, sems
):
    rows, columns = u_ref.shape
    across = [pl.ds(0, TILE), pl.ds(columns - TILE, TILE)]
    pieces = [(pl.ds(0, rows), lanes) for lanes in across]
    order = (2, 3, 0, 1, 4)
    if columns > 2 * TILE:
        middle = pl.ds(TILE, columns - 2 * TILE)
        pieces += [(pl.ds(0, STRIP), middle), (pl.ds(rows - STRIP, STRIP), middle)]
        if rows > 2 * STRIP:
            pieces.append((pl.ds(STRIP, rows - 2 * STRIP), middle))
    copies = [
        pltpu.make_async_copy(u_ref.at[lines, lanes], u_near.at[lines, lanes], sems.at[k])
        for k, (lines, lanes) in enumerate(pieces)
    ]
    for k in order:
        if k < len(copies):
            copies[k].start()
    low_first = low_goes_first()
    weights_low, weights_high = tail_weights(False), tail_weights(True)
    put_inverses(k_ref)
    put_side_tables(table_x, table_y)
    def put_x(lanes):
        to_low_x[:, lanes] = message(u_near[pl.ds(0, STRIP), lanes], False, weights_low)
        to_high_x[:, lanes] = message(u_near[pl.ds(rows - STRIP, STRIP), lanes], True, weights_high)

    for copy in copies[2:4]:
        copy.wait()
    for lanes in tiles_of(columns)[1:-1]:
        put_x(lanes)
    low, high = [], []
    for k in range(2):
        copies[k].wait()
        put_x(across[k])
        turned = u_near[:, across[k]].T
        side = turned[TILE - STRIP :] if k else turned[:STRIP]
        (near_high if k else near_low)[...] = side[STRIP - 8 :] if k else side[:8]
        for lanes in tiles_of(rows):
            part = side[:, lanes.start : lanes.start + lanes.size]
            (high if k else low).append(message(part, k == 1, (weights_low, weights_high)[k]))
    for lanes, to_low, to_high in zip(tiles_of(rows), low, high):
        to_y_first[:, lanes] = jnp.where(low_first, to_low, to_high)
        to_y_second[:, lanes] = jnp.where(low_first, to_high, to_low)
    for copy in copies[4:]:
        copy.wait()


def only_known(rhs, axis):
    length, step = rhs.shape[axis], 8 if axis == 0 else TILE
    at = lax.broadcasted_iota(jnp.int32, [step if k == axis else 1 for k in range(2)], axis)
    first, middle, last = (
        lax.slice_in_dim(rhs, low, high, axis=axis) for low, high in ((0, step), (step, length - step), (length - step, length))
    )
    parts = [jnp.where(at >= 1, first, 0.0), middle, jnp.where(at < step - 1, last, 0.0)]
    return jnp.concatenate([p for p in parts if p.shape[axis] > 0], axis=axis)


def product(a, b):
    dot = lambda p, q: jnp.dot(p, q, preferred_element_type=F32)
    return dot(a[0], b[0]) + dot(a[1], b[0]) + dot(a[0], b[1])


def split(value):
    upper = value.astype(BF16)
    return upper, (value - upper.astype(F32)).astype(BF16)


def solve_x(u_ref, k_ref, strips, solved_ref, copies):
    rows, columns = u_ref.shape
    span = min(columns, WINDOW)
    for s in range(2):
        inverse = k_ref[2 * s, :rows, :rows], k_ref[2 * s + 1, :rows, :rows]
        for j in range(columns // span):
            tiles = [differences(u_ref[:, pl.ds(j * span + t.start, t.size)], 0) for t in tiles_of(span)]
            lanes = pl.ds(j * span, span)
            rhs = jnp.concatenate([only_known(tile[s], 0) for tile in tiles], axis=1)
            solved = product(inverse, split(rhs))
            solved_ref[s, :, lanes] = solved
            strips[s, 0, :, lanes] = solved[:EDGE]
            strips[s, 1, :, lanes] = solved[rows - EDGE :]
        if s < len(copies):
            copies[s].start()


def inner_copies(solved_ref, outs, sems):
    rows = solved_ref.shape[1]
    if rows <= 2 * EDGE:
        return []
    inner = pl.ds(EDGE, rows - 2 * EDGE)
    return [pltpu.make_async_copy(solved_ref.at[s, inner], out.at[inner], sems.at[s]) for s, out in enumerate(outs)]


def solve_y(u_ref, k_ref, strips, solved_ref):
    rows, columns = u_ref.shape
    span = min(columns, WINDOW)
    lane = lax.broadcasted_iota(jnp.int32, (1, TILE), 1)
    step = min(rows, 64)
    both = [differences(u_ref[pl.ds(i * step, step), :], 1) for i in range(rows // step)]
    for s in range(2):
        inverse = k_ref[2 * s, :span, :span], k_ref[2 * s + 1, :span, :span]
        values = jnp.concatenate([only_known(piece[s], 1) for piece in both], axis=0)
        rhs = split(values)
        count = columns // span
        stacked = [jnp.concatenate([part[:, w * span : (w + 1) * span] for w in range(count)], axis=0) for part in rhs]
        solved = product(stacked, inverse)
        tiles = [solved[w * rows : (w + 1) * rows, t.start : t.start + t.size] for w in range(count) for t in tiles_of(span)]
        per = span // TILE
        added = {}
        for w in range(1, count):
            edge = w * span
            before = tiles[w * per - 1][:, TILE - 1 :] - PEAKS[s] * values[:, edge - 1 : edge]
            after = tiles[w * per][:, :1] - PEAKS[s] * values[:, edge : edge + 1]
            added[w * per] = before * powers(RATIOS[s], lane + 1)
            added[w * per - 1] = after * powers(RATIOS[s], TILE - lane)
        for t, value in added.items():
            tiles[t] = tiles[t] + value
        strips[s, 0] = tiles[0]
        strips[s, 1] = tiles[-1]
        for t in range(1, len(tiles) - 1):
            solved_ref[s, :, pl.ds((t - 1) * TILE, TILE)] = tiles[t]


FIRST, BETWEEN, LAST = range(3)


def solves_x():
    ends = jnp.where(lax.axis_index("gy") < 2, FIRST, BETWEEN)
    return jnp.where(lax.axis_index("gx") == 0, ends, LAST)


def first_kernel(u_ref, k_ref, *refs):
    messages, passed, (dx, strips_x, solved_x, sems) = refs[:2], refs[2:4], refs[4:]
    for message_ref, passed_ref in zip(messages, passed):
        passed_ref[...] = message_ref[...]

    @pl.when(solves_x() == FIRST)
    def _():
        copies = inner_copies(solved_x, (dx,), sems)
        solve_x(u_ref, k_ref, strips_x, solved_x, copies)
        for copy in copies:
            copy.wait()


def between_kernel(u_ref, k_ref, *refs):
    messages, passed, (strips_x, solved_x) = refs[:2], refs[3:5], refs[5:]
    for message_ref, passed_ref in zip(messages, passed):
        passed_ref[...] = message_ref[...]

    @pl.when(solves_x() == BETWEEN)
    def _():
        solve_x(u_ref, k_ref, strips_x, solved_x, [])


def interior_kernel(u_ref, k_ref, _, first_strips, first_solved, between_strips, between_solved, *refs):
    strips_x, dx, dxx, strips_y, solved_y, solved_x, sems = refs
    for when, strips, solved in (
        (FIRST, first_strips, first_solved),
        (BETWEEN, between_strips, between_solved),
        (LAST, strips_x, solved_x),
    ):

        @pl.when(solves_x() == when)
        def _():
            copies = inner_copies(solved, (dx, dxx), sems)
            if when == LAST:
                solve_x(u_ref, k_ref, strips, solved, copies)
            else:
                if when == FIRST:
                    copies = copies[1:]
                for copy in copies:
                    copy.start()
                strips_x[...] = strips[...]
            solve_y(u_ref, k_ref, strips_y, solved_y)
            for copy in copies:
                copy.wait()


def side_terms(around, tails, high):
    found = []
    for s, part in enumerate(differences(around, 0)):
        nearest, outer = (part[1:2], part[2:3]) if high else (part[2:3], part[1:2])
        total = nearest + RATIOS[s] * (outer + RATIOS[s] * tails[s])
        found.append((SCALES[s] * total, PEAKS[s] * nearest))
    return found


def low_terms(message, own):
    row = lax.broadcasted_iota(jnp.int32, own.shape, 0)
    around = jnp.where(row < 2, jnp.concatenate([message, message], axis=0), pltpu.roll(own, 2, 0))
    return side_terms(around, (message[2:3], message[3:4]), False)


def high_terms(message, own):
    row = lax.broadcasted_iota(jnp.int32, own.shape, 0)
    around = pltpu.roll(jnp.where(row < 2, jnp.concatenate([message, message], axis=0), own), 2, 0)
    return side_terms(around, (message[2:3], message[3:4]), True)


def add_side_x(terms, side, lanes, table_x, strips_x, put):
    row = lax.broadcasted_iota(jnp.int32, (8, 1), 0)
    for s in range(2):
        near, first = terms[s]
        extra = near * table_x[s, side, :, : lanes.size]
        first = jnp.where(row == (7 if side else 0), first, 0.0)
        if side:
            extra = jnp.concatenate([extra[: EDGE - 8], extra[EDGE - 8 :] + first], axis=0)
        else:
            extra = jnp.concatenate([extra[:8] + first, extra[8:]], axis=0)
        put[s, :, lanes] = strips_x[s, side, :, lanes] + extra


def sides_kernel(
    from_y_first, from_y_second, near_low, near_high, table_y, strips_y, done_y
):
    rows = near_low.shape[1]
    row = lax.broadcasted_iota(jnp.int32, (8, 1), 0)
    low_first = low_goes_first()
    for lines in tiles_of(rows):
        first, second = from_y_first[:, lines], from_y_second[:, lines]
        from_low, from_high = jnp.where(low_first, first, second), jnp.where(low_first, second, first)
        terms = low_terms(from_low, near_low[:, lines]), high_terms(from_high, near_high[:, lines])
        stacked = jnp.zeros((8, lines.size), F32)
        for side in range(2):
            for s in range(2):
                for which in range(2):
                    stacked = jnp.where(row == 4 * side + 2 * s + which, terms[side][s][which], stacked)
        upper, lower = halves(stacked)
        factors = jnp.concatenate([upper, lower, upper, jnp.zeros_like(upper)], axis=0).astype(BF16)
        added = lax.dot_general(factors, table_y[...], (((0,), (0,)), ((), ())), preferred_element_type=F32)
        for s in range(2):
            for side in range(2):
                block = 2 * s + side
                done_y[s, side, lines] = strips_y[s, side, lines] + added[:, block * TILE : (block + 1) * TILE]


def finish_kernel(from_low_x, from_high_x, u_near, table_x, strips_x, done_y, solved_y, *refs):
    dx, dxx, dy, dyy, done_x, sems = refs[2:]
    rows, columns = dx.shape
    started = []

    def send(source, target):
        copy = pltpu.make_async_copy(source, target, sems.at[len(started)])
        copy.start()
        started.append(copy)

    for s, out in enumerate((dy, dyy)):
        for side in range(2):
            send(done_y.at[s, side], out.at[:, pl.ds(side * (columns - TILE), TILE)])
    for lanes in tiles_of(columns):
        add_side_x(low_terms(from_low_x[:, lanes], u_near[pl.ds(0, 8), lanes]), 0, lanes, table_x, strips_x, done_x.at[0])
        add_side_x(high_terms(from_high_x[:, lanes], u_near[pl.ds(rows - 8, 8), lanes]), 1, lanes, table_x, strips_x, done_x.at[1])
    for s, out in enumerate((dx, dxx)):
        for side in range(2):
            send(done_x.at[side, s], out.at[pl.ds(side * (rows - EDGE), EDGE)])
    if columns > 2 * TILE:
        for s, out in enumerate((dy, dyy)):
            send(solved_y.at[s], out.at[:, pl.ds(TILE, columns - 2 * TILE)])
    for copy in started:
        copy.wait()


def on_chip(*shape):
    return pltpu.VMEM(shape, F32)


def near(array):
    return pltpu.with_memory_space_constraint(array, pltpu.VMEM)


def pack(u):
    rows, columns = u.shape
    wide = max(rows, columns)
    return pl.pallas_call(
        pack_kernel,
        name="pack",
        out_shape=(
            on_chip(MESSAGE, columns),
            on_chip(MESSAGE, columns),
            on_chip(MESSAGE, wide),
            on_chip(MESSAGE, wide),
            on_chip(rows, columns),
            on_chip(8, rows),
            on_chip(8, rows),
            pltpu.VMEM((4, WINDOW, WINDOW), BF16),
            on_chip(2, 2, EDGE, TILE),
            pltpu.VMEM((32, 4 * TILE), BF16),
        ),
        in_specs=[ANY],
        out_specs=[VMEM] * 10,
        scratch_shapes=[pltpu.SemaphoreType.DMA((5,))],
        compiler_params=LIMIT,
    )(pltpu.with_memory_space_constraint(u, pltpu.HBM))


def shapes_x(rows, columns):
    return on_chip(2, 2, EDGE, columns), on_chip(2, rows, columns)


def lead(kernel, name, outs, scratch, u_near, inverses, *messages):
    return pl.pallas_call(
        kernel,
        name=name,
        out_shape=tuple(on_chip(*a.shape) for a in messages[:2]) + outs,
        in_specs=[VMEM] * (2 + len(messages)),
        out_specs=[VMEM] * 2 + [ANY] * (len(outs) - 2) + [VMEM] * 2,
        scratch_shapes=scratch,
        compiler_params=LIMIT,
    )(*(near(a) for a in (u_near, inverses, *messages)))


def interior(u_near, inverses, dx, *early):
    rows, columns = u_near.shape
    strips_x, solved_x = shapes_x(rows, columns)
    return pl.pallas_call(
        interior_kernel,
        name="interior",
        out_shape=(strips_x,)
        + (pltpu.HBM(u_near.shape, F32),) * 2
        + (on_chip(2, 2, rows, TILE), on_chip(2, rows, max(columns - 2 * TILE, TILE))),
        in_specs=[VMEM] * 2 + [ANY] + [VMEM] * 4,
        out_specs=[VMEM] + [ANY] * 2 + [VMEM] * 2,
        input_output_aliases={2: 1},
        scratch_shapes=[solved_x, pltpu.SemaphoreType.DMA((2,))],
        compiler_params=LIMIT,
        cost_estimate=pl.CostEstimate(flops=2 * 2**28, bytes_accessed=5 * 2**19, transcendentals=0),
    )(near(u_near), near(inverses), dx, *(near(a) for a in early))


def sides(arrays, strips_y):
    return pl.pallas_call(
        sides_kernel,
        name="sides",
        out_shape=on_chip(*strips_y.shape),
        in_specs=[VMEM] * 6,
        out_specs=VMEM,
        compiler_params=LIMIT,
    )(*(near(a) for a in (*arrays, strips_y)))


def finish(arrays, parts):
    columns = parts[0].shape[1]
    return pl.pallas_call(
        finish_kernel,
        name="finish",
        out_shape=(pltpu.HBM(parts[0].shape, F32),) * 4,
        in_specs=[VMEM] * 7 + [ANY] * 2,
        out_specs=[ANY] * 4,
        input_output_aliases={7: 0, 8: 1},
        scratch_shapes=[on_chip(2, 2, EDGE, columns), pltpu.SemaphoreType.DMA((10,))],
        compiler_params=LIMIT,
    )(*(near(a) for a in arrays), *parts)


def local(velocity):
    to_high_x, to_low_x, to_y_first, to_y_second, u_near, near_low, near_high, inverses, *tables = pack(velocity[0])
    size = u_near.shape
    outs = shapes_x(*size)
    to_high_x, to_y_first, dx, *early = lead(
        first_kernel,
        "solve_first",
        (pltpu.HBM(size, F32),) + outs,
        [pltpu.SemaphoreType.DMA((1,))],
        u_near,
        inverses,
        to_high_x,
        to_y_first,
    )
    to_low_x, to_y_second, *between = lead(between_kernel, "solve_between", outs, [], u_near, inverses, to_low_x, to_y_second, early[0])
    gx = lax.axis_size("gx")
    first, second = trades_along_y()
    from_low_x = lax.ppermute(to_high_x, "gx", [(i, (i + 1) % gx) for i in range(gx)])
    from_y_first = lax.ppermute(to_y_first, ("gx", "gy"), first)
    from_high_x = lax.ppermute(to_low_x, "gx", [(i, (i - 1) % gx) for i in range(gx)])
    from_y_second = lax.ppermute(to_y_second, ("gx", "gy"), second)
    strips_x, dx, dxx, strips_y, solved_y = interior(u_near, inverses, dx, *early, *between)
    table_x, table_y = tables
    done_y = sides((from_y_first, from_y_second, near_low, near_high, table_y), strips_y)
    dx, dxx, dy, dyy = finish((from_low_x, from_high_x, u_near, table_x, strips_x, done_y, solved_y), (dx, dxx))
    return tuple(o[None] for o in (dx, dy, dxx, dyy))


def solution(mesh):
    placed = P(None, "gx", "gy")
    return jax.shard_map(local, mesh=mesh, in_specs=(placed,), out_specs=(placed,) * 4, check_vma=False)
```

```python
import math

import jax
import jax.numpy as jnp
from jax import lax
from jax.experimental import pallas as pl
from jax.experimental.pallas import tpu as pltpu
from jax.sharding import PartitionSpec as P

F32 = jnp.float32
BF16 = jnp.bfloat16

COUPLINGS = (1.0 / 3.0, 2.0 / 11.0)
CENTRES = (7.0 / 9.0, 12.0 / 11.0 + 6.0 / 44.0)
BESIDES = (1.0 / 36.0, 3.0 / 44.0)

ROOTS = tuple(math.sqrt(1.0 - 4.0 * a * a) for a in COUPLINGS)
RATIOS = tuple((root - 1.0) / (2.0 * a) for a, root in zip(COUPLINGS, ROOTS))
SCALES = tuple((c - b / a) / root for a, b, c, root in zip(COUPLINGS, BESIDES, CENTRES, ROOTS))
PEAKS = tuple((c + 2.0 * b * r) / root - h for b, c, r, root, h in zip(BESIDES, CENTRES, RATIOS, ROOTS, SCALES))

WINDOW = 256
TILE = 128
STRIP = 32
EDGE = 24
REACH = 64
MESSAGE = 4

ANY = pl.BlockSpec(memory_space=pl.ANY)
VMEM = pl.BlockSpec(memory_space=pltpu.VMEM)
LIMIT = pltpu.CompilerParams(vmem_limit_bytes=16 * 2**20)


def differences(cells, axis):
    length = cells.shape[axis]
    here = pltpu.roll(cells, length - 1, axis) - cells
    before = pltpu.roll(here, 1, axis)
    return here + before, here - before


def powers(ratio, exponent):
    product = jnp.where(exponent < REACH, F32(1.0), F32(0.0))
    for bit in range(REACH.bit_length() - 1):
        factor = jnp.where((exponent & (1 << bit)) != 0, F32(ratio ** (1 << bit)), F32(1.0))
        product = product * factor
    return product


def tail_weights(high):
    at = lax.broadcasted_iota(jnp.int32, (STRIP, TILE), 0)
    known = (at >= 1) & (at < STRIP - 1)
    exponent = (STRIP - 2 - at) if high else (at - 1)
    return [jnp.where(known, powers(ratio, exponent), 0.0) for ratio in RATIOS]


def message(strip, high, weights):
    tails = [
        jnp.sum(part * weight[:, : strip.shape[1]], axis=0, keepdims=True)
        for part, weight in zip(differences(strip, 0), weights)
    ]
    near = pltpu.roll(strip[STRIP - 8 :], 2, 0) if high else strip[:8]
    row = lax.broadcasted_iota(jnp.int32, near.shape, 0)
    return jnp.where(row < 2, near, jnp.where(row == 2, tails[0], tails[1]))[:MESSAGE]


def tiles_of(length):
    step = min(length, TILE)
    return [pl.ds(k * step, step) for k in range(length // step)]


def halves(value):
    upper = value.astype(BF16).astype(F32)
    return upper, value - upper


def put_inverses(k_ref):
    i = lax.broadcasted_iota(jnp.int32, (TILE, TILE), 0)
    j = lax.broadcasted_iota(jnp.int32, (TILE, TILE), 1)
    blocks = WINDOW // TILE
    for s in range(2):
        for apart in range(1 - blocks, blocks):
            distance = jnp.abs(j - i + apart * TILE)
            weights = SCALES[s] * powers(RATIOS[s], distance)
            if apart == 0:
                weights = jnp.where(distance == 0, F32(SCALES[s] + PEAKS[s]), weights)
            upper, lower = halves(weights)
            for p, part in enumerate((upper, lower)):
                for first in range(blocks):
                    if 0 <= first + apart < blocks:
                        at_i, at_j = pl.ds(first * TILE, TILE), pl.ds((first + apart) * TILE, TILE)
                        k_ref[2 * s + p, at_i, at_j] = part.astype(BF16)


def put_side_tables(table_x, table_y):
    at = lax.broadcasted_iota(jnp.int32, (EDGE, TILE), 0)
    lane = lax.broadcasted_iota(jnp.int32, (8, TILE), 1)
    row = lax.broadcasted_iota(jnp.int32, (8, TILE), 0)
    for s in range(2):
        for side in range(2):
            table_x[s, side] = powers(RATIOS[s], (EDGE - 1 - at) if side else at)
            within = (TILE - 1 - lane) if side else lane
            first = 4 * side + 2 * s
            lines = jnp.where(row == first, powers(RATIOS[s], within), 0.0)
            lines = jnp.where((row == first + 1) & (within == 0), 1.0, lines)
            upper, lower = halves(lines)
            stack = jnp.concatenate([upper, upper, lower, jnp.zeros_like(upper)], axis=0)
            block = 2 * s + side
            table_y[:, pl.ds(block * TILE, TILE)] = stack.astype(BF16)


def low_goes_first():
    next_chip_first = lax.axis_index("gx") == 0
    return next_chip_first == (lax.rem(lax.axis_index("gy"), 2) == 0)


def trades_along_y():
    gx, gy = lax.axis_size("gx"), lax.axis_size("gy")
    next_chip = [(y, (y - 1) % gy if y % 2 == 0 else (y + 1) % gy) for y in range(gy)]
    same_chip = [(y, y + 1 if y % 2 == 0 else y - 1) for y in range(gy)]
    first, second = [], []
    for x in range(gx):
        orders = (next_chip, same_chip) if x == 0 else (same_chip, next_chip)
        for found, pairs in zip((first, second), orders):
            found += [(x * gy + source, x * gy + target) for source, target in pairs]
    return first, second


def pack_kernel(
    u_ref, to_high_x, to_low_x, to_y_first, to_y_second, u_near, near_low, near_high, k_ref, table_x, table_y, sems
):
    rows, columns = u_ref.shape
    across = [pl.ds(0, TILE), pl.ds(columns - TILE, TILE)]
    pieces = [(pl.ds(0, rows), lanes) for lanes in across]
    order = (2, 3, 0, 1, 4)
    if columns > 2 * TILE:
        middle = pl.ds(TILE, columns - 2 * TILE)
        pieces += [(pl.ds(0, STRIP), middle), (pl.ds(rows - STRIP, STRIP), middle)]
        if rows > 2 * STRIP:
            pieces.append((pl.ds(STRIP, rows - 2 * STRIP), middle))
    copies = [
        pltpu.make_async_copy(u_ref.at[lines, lanes], u_near.at[lines, lanes], sems.at[k])
        for k, (lines, lanes) in enumerate(pieces)
    ]
    for k in order:
        if k < len(copies):
            copies[k].start()
    low_first = low_goes_first()
    weights_low, weights_high = tail_weights(False), tail_weights(True)
    put_inverses(k_ref)
    put_side_tables(table_x, table_y)

    def put_x(lanes):
        to_low_x[:, lanes] = message(u_near[pl.ds(0, STRIP), lanes], False, weights_low)
        to_high_x[:, lanes] = message(u_near[pl.ds(rows - STRIP, STRIP), lanes], True, weights_high)

    for copy in copies[2:4]:
        copy.wait()
    for lanes in tiles_of(columns)[1:-1]:
        put_x(lanes)
    low, high = [], []
    for k in range(2):
        copies[k].wait()
        put_x(across[k])
        turned = u_near[:, across[k]].T
        side = turned[TILE - STRIP :] if k else turned[:STRIP]
        (near_high if k else near_low)[...] = side[STRIP - 8 :] if k else side[:8]
        for lanes in tiles_of(rows):
            part = side[:, lanes.start : lanes.start + lanes.size]
            (high if k else low).append(message(part, k == 1, (weights_low, weights_high)[k]))
    for lanes, to_low, to_high in zip(tiles_of(rows), low, high):
        to_y_first[:, lanes] = jnp.where(low_first, to_low, to_high)
        to_y_second[:, lanes] = jnp.where(low_first, to_high, to_low)
    for copy in copies[4:]:
        copy.wait()


def only_known(rhs, axis):
    length, step = rhs.shape[axis], 8 if axis == 0 else TILE
    at = lax.broadcasted_iota(jnp.int32, [step if k == axis else 1 for k in range(2)], axis)
    first, middle, last = (
        lax.slice_in_dim(rhs, low, high, axis=axis) for low, high in ((0, step), (step, length - step), (length - step, length))
    )
    parts = [jnp.where(at >= 1, first, 0.0), middle, jnp.where(at < step - 1, last, 0.0)]
    return jnp.concatenate([p for p in parts if p.shape[axis] > 0], axis=axis)


def product(a, b):
    dot = lambda p, q: jnp.dot(p, q, preferred_element_type=F32)
    return dot(a[0], b[0]) + dot(a[1], b[0]) + dot(a[0], b[1])


def split(value):
    upper = value.astype(BF16)
    return upper, (value - upper.astype(F32)).astype(BF16)


def solve_x(u_ref, k_ref, strips, solved_ref, copies):
    rows, columns = u_ref.shape
    span = min(columns, WINDOW)
    for s in range(2):
        inverse = k_ref[2 * s, :rows, :rows], k_ref[2 * s + 1, :rows, :rows]
        for j in range(columns // span):
            tiles = [differences(u_ref[:, pl.ds(j * span + t.start, t.size)], 0) for t in tiles_of(span)]
            lanes = pl.ds(j * span, span)
            rhs = jnp.concatenate([only_known(tile[s], 0) for tile in tiles], axis=1)
            solved = product(inverse, split(rhs))
            solved_ref[s, :, lanes] = solved
            strips[s, 0, :, lanes] = solved[:EDGE]
            strips[s, 1, :, lanes] = solved[rows - EDGE :]
        if s in copies:
            copies[s].start()


def inner_copies(solved_ref, outs, sems, systems):
    rows = solved_ref.shape[1]
    if rows <= 2 * EDGE:
        return {}
    inner = pl.ds(EDGE, rows - 2 * EDGE)
    return {s: pltpu.make_async_copy(solved_ref.at[s, inner], outs[s].at[inner], sems.at[s]) for s in systems}


def solve_y(u_ref, k_ref, strips, solved_ref):
    rows, columns = u_ref.shape
    span = min(columns, WINDOW)
    lane = lax.broadcasted_iota(jnp.int32, (1, TILE), 1)
    step = min(rows, 64)
    both = [differences(u_ref[pl.ds(i * step, step), :], 1) for i in range(rows // step)]
    for s in range(2):
        inverse = k_ref[2 * s, :span, :span], k_ref[2 * s + 1, :span, :span]
        values = jnp.concatenate([only_known(piece[s], 1) for piece in both], axis=0)
        rhs = split(values)
        count = columns // span
        stacked = [jnp.concatenate([part[:, w * span : (w + 1) * span] for w in range(count)], axis=0) for part in rhs]
        solved = product(stacked, inverse)
        tiles = [solved[w * rows : (w + 1) * rows, t.start : t.start + t.size] for w in range(count) for t in tiles_of(span)]
        per = span // TILE
        added = {}
        for w in range(1, count):
            edge = w * span
            before = tiles[w * per - 1][:, TILE - 1 :] - PEAKS[s] * values[:, edge - 1 : edge]
            after = tiles[w * per][:, :1] - PEAKS[s] * values[:, edge : edge + 1]
            added[w * per] = before * powers(RATIOS[s], lane + 1)
            added[w * per - 1] = after * powers(RATIOS[s], TILE - lane)
        for t, value in added.items():
            tiles[t] = tiles[t] + value
        strips[s, 0] = tiles[0]
        strips[s, 1] = tiles[-1]
        for t in range(1, len(tiles) - 1):
            solved_ref[s, :, pl.ds((t - 1) * TILE, TILE)] = tiles[t]


FIRST, BETWEEN, LAST = range(3)


def solves_x():
    ends = jnp.where(lax.axis_index("gy") < 2, FIRST, BETWEEN)
    return jnp.where(lax.axis_index("gx") == 0, ends, LAST)


def first_kernel(u_ref, k_ref, *refs):
    messages, passed, (dx, strips_x, solved_x, sems) = refs[:2], refs[2:4], refs[4:]
    for message_ref, passed_ref in zip(messages, passed):
        passed_ref[...] = message_ref[...]

    @pl.when(solves_x() == FIRST)
    def _():
        copies = inner_copies(solved_x, (dx,), sems, (0,))
        solve_x(u_ref, k_ref, strips_x, solved_x, copies)
        for copy in copies.values():
            copy.wait()


def between_kernel(u_ref, k_ref, *refs):
    messages, passed, (strips_x, solved_x) = refs[:2], refs[3:5], refs[5:]
    for message_ref, passed_ref in zip(messages, passed):
        passed_ref[...] = message_ref[...]

    @pl.when(solves_x() == BETWEEN)
    def _():
        solve_x(u_ref, k_ref, strips_x, solved_x, {})


def interior_kernel(u_ref, k_ref, _, first_strips, first_solved, between_strips, between_solved, *refs):
    strips_x, dx, dxx, strips_y, solved_y, solved_x, sems = refs
    for when, strips, solved in (
        (FIRST, first_strips, first_solved),
        (BETWEEN, between_strips, between_solved),
        (LAST, strips_x, solved_x),
    ):

        @pl.when(solves_x() == when)
        def _():
            copies = inner_copies(solved, (dx, dxx), sems, (1,) if when == FIRST else (0, 1))
            if when == LAST:
                solve_x(u_ref, k_ref, strips, solved, copies)
            else:
                for copy in copies.values():
                    copy.start()
                strips_x[...] = strips[...]
            solve_y(u_ref, k_ref, strips_y, solved_y)
            for copy in copies.values():
                copy.wait()


def side_terms(around, tails, high):
    found = []
    for s, part in enumerate(differences(around, 0)):
        nearest, outer = (part[1:2], part[2:3]) if high else (part[2:3], part[1:2])
        total = nearest + RATIOS[s] * (outer + RATIOS[s] * tails[s])
        found.append((SCALES[s] * total, PEAKS[s] * nearest))
    return found


def low_terms(message, own):
    row = lax.broadcasted_iota(jnp.int32, own.shape, 0)
    around = jnp.where(row < 2, jnp.concatenate([message, message], axis=0), pltpu.roll(own, 2, 0))
    return side_terms(around, (message[2:3], message[3:4]), False)


def high_terms(message, own):
    row = lax.broadcasted_iota(jnp.int32, own.shape, 0)
    around = pltpu.roll(jnp.where(row < 2, jnp.concatenate([message, message], axis=0), own), 2, 0)
    return side_terms(around, (message[2:3], message[3:4]), True)


def add_side_x(terms, side, lanes, table_x, strips_x, put):
    row = lax.broadcasted_iota(jnp.int32, (8, 1), 0)
    for s in range(2):
        near, first = terms[s]
        extra = near * table_x[s, side, :, : lanes.size]
        first = jnp.where(row == (7 if side else 0), first, 0.0)
        if side:
            extra = jnp.concatenate([extra[: EDGE - 8], extra[EDGE - 8 :] + first], axis=0)
        else:
            extra = jnp.concatenate([extra[:8] + first, extra[8:]], axis=0)
        put[s, :, lanes] = strips_x[s, side, :, lanes] + extra


def sides_kernel(
    from_y_first, from_y_second, near_low, near_high, table_y, strips_y, solved_y, *done_y
):
    rows = near_low.shape[1]
    columns = done_y[0].shape[1]
    lanes_of = pl.ds(0, TILE), pl.ds(columns - TILE, TILE)
    if columns > 2 * TILE:
        for s in range(2):
            done_y[s][:, pl.ds(TILE, columns - 2 * TILE)] = solved_y[s]
    row = lax.broadcasted_iota(jnp.int32, (8, 1), 0)
    low_first = low_goes_first()
    for lines in tiles_of(rows):
        first, second = from_y_first[:, lines], from_y_second[:, lines]
        from_low, from_high = jnp.where(low_first, first, second), jnp.where(low_first, second, first)
        terms = low_terms(from_low, near_low[:, lines]), high_terms(from_high, near_high[:, lines])
        stacked = jnp.zeros((8, lines.size), F32)
        for side in range(2):
            for s in range(2):
                for which in range(2):
                    stacked = jnp.where(row == 4 * side + 2 * s + which, terms[side][s][which], stacked)
        upper, lower = halves(stacked)
        factors = jnp.concatenate([upper, lower, upper, jnp.zeros_like(upper)], axis=0).astype(BF16)
        added = lax.dot_general(factors, table_y[...], (((0,), (0,)), ((), ())), preferred_element_type=F32)
        for s in range(2):
            for side in range(2):
                block = 2 * s + side
                done_y[s][lines, lanes_of[side]] = strips_y[s, side, lines] + added[:, block * TILE : (block + 1) * TILE]


def finish_kernel(from_low_x, from_high_x, u_near, table_x, strips_x, done_y, done_yy, *refs):
    dx, dxx, dy, dyy, done_x, sems = refs[2:]
    rows, columns = dx.shape
    started = []

    def send(source, target):
        copy = pltpu.make_async_copy(source, target, sems.at[len(started)])
        copy.start()
        started.append(copy)

    send(done_y, dy)
    send(done_yy, dyy)
    for lanes in tiles_of(columns):
        add_side_x(low_terms(from_low_x[:, lanes], u_near[pl.ds(0, 8), lanes]), 0, lanes, table_x, strips_x, done_x.at[0])
        add_side_x(high_terms(from_high_x[:, lanes], u_near[pl.ds(rows - 8, 8), lanes]), 1, lanes, table_x, strips_x, done_x.at[1])
    for s, out in enumerate((dx, dxx)):
        for side in range(2):
            send(done_x.at[side, s], out.at[pl.ds(side * (rows - EDGE), EDGE)])
    for copy in started:
        copy.wait()


def on_chip(*shape):
    return pltpu.VMEM(shape, F32)


def near(array):
    return pltpu.with_memory_space_constraint(array, pltpu.VMEM)


def pack(u):
    rows, columns = u.shape
    wide = max(rows, columns)
    return pl.pallas_call(
        pack_kernel,
        name="pack",
        out_shape=(
            on_chip(MESSAGE, columns),
            on_chip(MESSAGE, columns),
            on_chip(MESSAGE, wide),
            on_chip(MESSAGE, wide),
            on_chip(rows, columns),
            on_chip(8, rows),
            on_chip(8, rows),
            pltpu.VMEM((4, WINDOW, WINDOW), BF16),
            on_chip(2, 2, EDGE, TILE),
            pltpu.VMEM((32, 4 * TILE), BF16),
        ),
        in_specs=[ANY],
        out_specs=[VMEM] * 10,
        scratch_shapes=[pltpu.SemaphoreType.DMA((5,))],
        compiler_params=LIMIT,
    )(pltpu.with_memory_space_constraint(u, pltpu.HBM))


def shapes_x(rows, columns):
    return on_chip(2, 2, EDGE, columns), on_chip(2, rows, columns)


def lead(kernel, name, outs, scratch, u_near, inverses, *messages):
    return pl.pallas_call(
        kernel,
        name=name,
        out_shape=tuple(on_chip(*a.shape) for a in messages[:2]) + outs,
        in_specs=[VMEM] * (2 + len(messages)),
        out_specs=[VMEM] * 2 + [ANY] * (len(outs) - 2) + [VMEM] * 2,
        scratch_shapes=scratch,
        compiler_params=LIMIT,
    )(*(near(a) for a in (u_near, inverses, *messages)))


def interior(u_near, inverses, dx, *early):
    rows, columns = u_near.shape
    strips_x, solved_x = shapes_x(rows, columns)
    return pl.pallas_call(
        interior_kernel,
        name="interior",
        out_shape=(strips_x,)
        + (pltpu.HBM(u_near.shape, F32),) * 2
        + (on_chip(2, 2, rows, TILE), on_chip(2, rows, max(columns - 2 * TILE, TILE))),
        in_specs=[VMEM] * 2 + [ANY] + [VMEM] * 4,
        out_specs=[VMEM] + [ANY] * 2 + [VMEM] * 2,
        input_output_aliases={2: 1},
        scratch_shapes=[solved_x, pltpu.SemaphoreType.DMA((2,))],
        compiler_params=LIMIT,
        cost_estimate=pl.CostEstimate(flops=2 * 2**28, bytes_accessed=5 * 2**19, transcendentals=0),
    )(near(u_near), near(inverses), dx, *(near(a) for a in early))


def sides(size, *arrays):
    return pl.pallas_call(
        sides_kernel,
        name="sides",
        out_shape=(on_chip(*size),) * 2,
        in_specs=[VMEM] * 7,
        out_specs=[VMEM] * 2,
        compiler_params=LIMIT,
    )(*(near(a) for a in arrays))


def finish(arrays, parts):
    columns = parts[0].shape[1]
    return pl.pallas_call(
        finish_kernel,
        name="finish",
        out_shape=(pltpu.HBM(parts[0].shape, F32),) * 4,
        in_specs=[VMEM] * 7 + [ANY] * 2,
        out_specs=[ANY] * 4,
        input_output_aliases={7: 0, 8: 1},
        scratch_shapes=[on_chip(2, 2, EDGE, columns), pltpu.SemaphoreType.DMA((6,))],
        compiler_params=LIMIT,
    )(*(near(a) for a in arrays), *parts)


def local(velocity):
    to_high_x, to_low_x, to_y_first, to_y_second, u_near, near_low, near_high, inverses, *tables = pack(velocity[0])
    size = u_near.shape
    outs = shapes_x(*size)
    to_high_x, to_y_first, dx, *early = lead(
        first_kernel,
        "solve_first",
        (pltpu.HBM(size, F32),) + outs,
        [pltpu.SemaphoreType.DMA((1,))],
        u_near,
        inverses,
        to_high_x,
        to_y_first,
    )
    to_low_x, to_y_second, *between = lead(between_kernel, "solve_between", outs, [], u_near, inverses, to_low_x, to_y_second, early[0])
    gx = lax.axis_size("gx")
    first, second = trades_along_y()
    from_low_x = lax.ppermute(to_high_x, "gx", [(i, (i + 1) % gx) for i in range(gx)])
    from_y_first = lax.ppermute(to_y_first, ("gx", "gy"), first)
    from_high_x = lax.ppermute(to_low_x, "gx", [(i, (i - 1) % gx) for i in range(gx)])
    from_y_second = lax.ppermute(to_y_second, ("gx", "gy"), second)
    strips_x, dx, dxx, strips_y, solved_y = interior(u_near, inverses, dx, *early, *between)
    table_x, table_y = tables
    done = sides(size, from_y_first, from_y_second, near_low, near_high, table_y, strips_y, solved_y)
    dx, dxx, dy, dyy = finish((from_low_x, from_high_x, u_near, table_x, strips_x, *done), (dx, dxx))
    return tuple(o[None] for o in (dx, dy, dxx, dyy))


def solution(mesh):
    placed = P(None, "gx", "gy")
    return jax.shard_map(local, mesh=mesh, in_specs=(placed,), out_specs=(placed,) * 4, check_vma=False)
```

```python
import math

import jax
import jax.numpy as jnp
from jax import lax
from jax.experimental import pallas as pl
from jax.experimental.pallas import tpu as pltpu
from jax.sharding import PartitionSpec as P

F32 = jnp.float32
BF16 = jnp.bfloat16

COUPLINGS = (1.0 / 3.0, 2.0 / 11.0)
CENTRES = (7.0 / 9.0, 12.0 / 11.0 + 6.0 / 44.0)
BESIDES = (1.0 / 36.0, 3.0 / 44.0)

ROOTS = tuple(math.sqrt(1.0 - 4.0 * a * a) for a in COUPLINGS)
RATIOS = tuple((root - 1.0) / (2.0 * a) for a, root in zip(COUPLINGS, ROOTS))
SCALES = tuple((c - b / a) / root for a, b, c, root in zip(COUPLINGS, BESIDES, CENTRES, ROOTS))
PEAKS = tuple((c + 2.0 * b * r) / root - h for b, c, r, root, h in zip(BESIDES, CENTRES, RATIOS, ROOTS, SCALES))

WINDOW = 256
TILE = 128
STRIP = 32
EDGE = 24
REACH = 64
MESSAGE = 4

ANY = pl.BlockSpec(memory_space=pl.ANY)
VMEM = pl.BlockSpec(memory_space=pltpu.VMEM)
LIMIT = pltpu.CompilerParams(vmem_limit_bytes=16 * 2**20)


def differences(cells, axis):
    length = cells.shape[axis]
    here = pltpu.roll(cells, length - 1, axis) - cells
    before = pltpu.roll(here, 1, axis)
    return here + before, here - before


def powers(ratio, exponent):
    product = jnp.where(exponent < REACH, F32(1.0), F32(0.0))
    for bit in range(REACH.bit_length() - 1):
        factor = jnp.where((exponent & (1 << bit)) != 0, F32(ratio ** (1 << bit)), F32(1.0))
        product = product * factor
    return product


def tail_weights(high):
    at = lax.broadcasted_iota(jnp.int32, (STRIP, TILE), 0)
    known = (at >= 1) & (at < STRIP - 1)
    exponent = (STRIP - 2 - at) if high else (at - 1)
    return [jnp.where(known, powers(ratio, exponent), 0.0) for ratio in RATIOS]


def message(strip, high, weights):
    tails = [
        jnp.sum(part * weight[:, : strip.shape[1]], axis=0, keepdims=True)
        for part, weight in zip(differences(strip, 0), weights)
    ]
    near = pltpu.roll(strip[STRIP - 8 :], 2, 0) if high else strip[:8]
    row = lax.broadcasted_iota(jnp.int32, near.shape, 0)
    return jnp.where(row < 2, near, jnp.where(row == 2, tails[0], tails[1]))[:MESSAGE]


def tiles_of(length):
    step = min(length, TILE)
    return [pl.ds(k * step, step) for k in range(length // step)]


def halves(value):
    upper = value.astype(BF16).astype(F32)
    return upper, value - upper


def put_inverses(k_ref):
    i = lax.broadcasted_iota(jnp.int32, (TILE, TILE), 0)
    j = lax.broadcasted_iota(jnp.int32, (TILE, TILE), 1)
    blocks = WINDOW // TILE
    for s in range(2):
        for apart in range(1 - blocks, blocks):
            distance = jnp.abs(j - i + apart * TILE)
            weights = SCALES[s] * powers(RATIOS[s], distance)
            if apart == 0:
                weights = jnp.where(distance == 0, F32(SCALES[s] + PEAKS[s]), weights)
            upper, lower = halves(weights)
            for p, part in enumerate((upper, lower)):
                for first in range(blocks):
                    if 0 <= first + apart < blocks:
                        at_i, at_j = pl.ds(first * TILE, TILE), pl.ds((first + apart) * TILE, TILE)
                        k_ref[2 * s + p, at_i, at_j] = part.astype(BF16)


def put_side_tables(table_x, table_y):
    at = lax.broadcasted_iota(jnp.int32, (EDGE, TILE), 0)
    lane = lax.broadcasted_iota(jnp.int32, (8, TILE), 1)
    row = lax.broadcasted_iota(jnp.int32, (8, TILE), 0)
    for s in range(2):
        for side in range(2):
            table_x[s, side] = powers(RATIOS[s], (EDGE - 1 - at) if side else at)
            within = (TILE - 1 - lane) if side else lane
            first = 4 * side + 2 * s
            lines = jnp.where(row == first, powers(RATIOS[s], within), 0.0)
            lines = jnp.where((row == first + 1) & (within == 0), 1.0, lines)
            upper, lower = halves(lines)
            stack = jnp.concatenate([upper, upper, lower, jnp.zeros_like(upper)], axis=0)
            block = 2 * s + side
            table_y[:, pl.ds(block * TILE, TILE)] = stack.astype(BF16)


def low_goes_first():
    next_chip_first = lax.axis_index("gx") == 0
    return next_chip_first == (lax.rem(lax.axis_index("gy"), 2) == 0)


def trades_along_y():
    gx, gy = lax.axis_size("gx"), lax.axis_size("gy")
    next_chip = [(y, (y - 1) % gy if y % 2 == 0 else (y + 1) % gy) for y in range(gy)]
    same_chip = [(y, y + 1 if y % 2 == 0 else y - 1) for y in range(gy)]
    first, second = [], []
    for x in range(gx):
        orders = (next_chip, same_chip) if x == 0 else (same_chip, next_chip)
        for found, pairs in zip((first, second), orders):
            found += [(x * gy + source, x * gy + target) for source, target in pairs]
    return first, second


def pack_kernel(
    u_ref, to_high_x, to_low_x, to_y_first, to_y_second, u_near, near_low, near_high, k_ref, table_x, table_y, sems
):
    rows, columns = u_ref.shape
    across = [pl.ds(0, TILE), pl.ds(columns - TILE, TILE)]
    pieces = [(pl.ds(0, rows), lanes) for lanes in across]
    order = (2, 3, 0, 1, 4)
    if columns > 2 * TILE:
        middle = pl.ds(TILE, columns - 2 * TILE)
        pieces += [(pl.ds(0, STRIP), middle), (pl.ds(rows - STRIP, STRIP), middle)]
        if rows > 2 * STRIP:
            pieces.append((pl.ds(STRIP, rows - 2 * STRIP), middle))
    copies = [
        pltpu.make_async_copy(u_ref.at[lines, lanes], u_near.at[lines, lanes], sems.at[k])
        for k, (lines, lanes) in enumerate(pieces)
    ]
    for k in order:
        if k < len(copies):
            copies[k].start()
    low_first = low_goes_first()
    weights_low, weights_high = tail_weights(False), tail_weights(True)
    put_inverses(k_ref)
    put_side_tables(table_x, table_y)

    def put_x(lanes):
        to_low_x[:, lanes] = message(u_near[pl.ds(0, STRIP), lanes], False, weights_low)
        to_high_x[:, lanes] = message(u_near[pl.ds(rows - STRIP, STRIP), lanes], True, weights_high)

    for copy in copies[2:4]:
        copy.wait()
    for lanes in tiles_of(columns)[1:-1]:
        put_x(lanes)
    low, high = [], []
    for k in range(2):
        copies[k].wait()
        put_x(across[k])
        turned = u_near[:, across[k]].T
        side = turned[TILE - STRIP :] if k else turned[:STRIP]
        (near_high if k else near_low)[...] = side[STRIP - 8 :] if k else side[:8]
        for lanes in tiles_of(rows):
            part = side[:, lanes.start : lanes.start + lanes.size]
            (high if k else low).append(message(part, k == 1, (weights_low, weights_high)[k]))
    for lanes, to_low, to_high in zip(tiles_of(rows), low, high):
        to_y_first[:, lanes] = jnp.where(low_first, to_low, to_high)
        to_y_second[:, lanes] = jnp.where(low_first, to_high, to_low)
    for copy in copies[4:]:
        copy.wait()


def only_known(rhs, axis):
    length, step = rhs.shape[axis], 8 if axis == 0 else TILE
    at = lax.broadcasted_iota(jnp.int32, [step if k == axis else 1 for k in range(2)], axis)
    first, middle, last = (
        lax.slice_in_dim(rhs, low, high, axis=axis) for low, high in ((0, step), (step, length - step), (length - step, length))
    )
    parts = [jnp.where(at >= 1, first, 0.0), middle, jnp.where(at < step - 1, last, 0.0)]
    return jnp.concatenate([p for p in parts if p.shape[axis] > 0], axis=axis)


def product(a, b):
    dot = lambda p, q: jnp.dot(p, q, preferred_element_type=F32)
    return dot(a[0], b[0]) + dot(a[1], b[0]) + dot(a[0], b[1])


def split(value):
    upper = value.astype(BF16)
    return upper, (value - upper.astype(F32)).astype(BF16)


def solve_x(u_ref, k_ref, strips, solved_ref, copies):
    rows, columns = u_ref.shape
    span = min(columns, WINDOW)
    for s in range(2):
        inverse = k_ref[2 * s, :rows, :rows], k_ref[2 * s + 1, :rows, :rows]
        for j in range(columns // span):
            tiles = [differences(u_ref[:, pl.ds(j * span + t.start, t.size)], 0) for t in tiles_of(span)]
            lanes = pl.ds(j * span, span)
            rhs = jnp.concatenate([only_known(tile[s], 0) for tile in tiles], axis=1)
            solved = product(inverse, split(rhs))
            solved_ref[s, :, lanes] = solved
            strips[s, 0, :, lanes] = solved[:EDGE]
            strips[s, 1, :, lanes] = solved[rows - EDGE :]
        if s in copies:
            copies[s].start()


def inner_copies(solved_ref, outs, sems, systems):
    rows = solved_ref.shape[1]
    if rows <= 2 * EDGE:
        return {}
    inner = pl.ds(EDGE, rows - 2 * EDGE)
    return {s: pltpu.make_async_copy(solved_ref.at[s, inner], outs[s].at[inner], sems.at[s]) for s in systems}


def solve_y(u_ref, k_ref, strips, solved_ref):
    rows, columns = u_ref.shape
    span = min(columns, WINDOW)
    lane = lax.broadcasted_iota(jnp.int32, (1, TILE), 1)
    step = min(rows, 64)
    both = [differences(u_ref[pl.ds(i * step, step), :], 1) for i in range(rows // step)]
    for s in range(2):
        inverse = k_ref[2 * s, :span, :span], k_ref[2 * s + 1, :span, :span]
        values = jnp.concatenate([only_known(piece[s], 1) for piece in both], axis=0)
        rhs = split(values)
        count = columns // span
        stacked = [jnp.concatenate([part[:, w * span : (w + 1) * span] for w in range(count)], axis=0) for part in rhs]
        solved = product(stacked, inverse)
        tiles = [solved[w * rows : (w + 1) * rows, t.start : t.start + t.size] for w in range(count) for t in tiles_of(span)]
        per = span // TILE
        added = {}
        for w in range(1, count):
            edge = w * span
            before = tiles[w * per - 1][:, TILE - 1 :] - PEAKS[s] * values[:, edge - 1 : edge]
            after = tiles[w * per][:, :1] - PEAKS[s] * values[:, edge : edge + 1]
            added[w * per] = before * powers(RATIOS[s], lane + 1)
            added[w * per - 1] = after * powers(RATIOS[s], TILE - lane)
        for t, value in added.items():
            tiles[t] = tiles[t] + value
        strips[s, 0] = tiles[0]
        strips[s, 1] = tiles[-1]
        for t in range(1, len(tiles) - 1):
            solved_ref[s, :, pl.ds((t - 1) * TILE, TILE)] = tiles[t]


FIRST, BETWEEN, LAST = range(3)


def solves_x():
    ends = jnp.where(lax.axis_index("gy") < 2, FIRST, BETWEEN)
    return jnp.where(lax.axis_index("gx") == 0, ends, LAST)


def first_kernel(u_ref, k_ref, *refs):
    dx, strips_x, solved_x, sems = refs[4:]

    @pl.when(solves_x() == FIRST)
    def _():
        copies = inner_copies(solved_x, (dx,), sems, (0,))
        solve_x(u_ref, k_ref, strips_x, solved_x, copies)
        for copy in copies.values():
            copy.wait()


def between_kernel(u_ref, k_ref, *refs):
    strips_x, solved_x = refs[5:]

    @pl.when(solves_x() == BETWEEN)
    def _():
        solve_x(u_ref, k_ref, strips_x, solved_x, {})


def interior_kernel(u_ref, k_ref, _, first_strips, first_solved, between_strips, between_solved, *refs):
    strips_x, dx, dxx, strips_y, solved_y, solved_x, sems = refs
    for when, strips, solved in (
        (FIRST, first_strips, first_solved),
        (BETWEEN, between_strips, between_solved),
        (LAST, strips_x, solved_x),
    ):

        @pl.when(solves_x() == when)
        def _():
            copies = inner_copies(solved, (dx, dxx), sems, (1,) if when == FIRST else (0, 1))
            if when == LAST:
                solve_x(u_ref, k_ref, strips, solved, copies)
            else:
                for copy in copies.values():
                    copy.start()
                strips_x[...] = strips[...]
            solve_y(u_ref, k_ref, strips_y, solved_y)
            for copy in copies.values():
                copy.wait()


def side_terms(around, tails, high):
    found = []
    for s, part in enumerate(differences(around, 0)):
        nearest, outer = (part[1:2], part[2:3]) if high else (part[2:3], part[1:2])
        total = nearest + RATIOS[s] * (outer + RATIOS[s] * tails[s])
        found.append((SCALES[s] * total, PEAKS[s] * nearest))
    return found


def low_terms(message, own):
    row = lax.broadcasted_iota(jnp.int32, own.shape, 0)
    around = jnp.where(row < 2, jnp.concatenate([message, message], axis=0), pltpu.roll(own, 2, 0))
    return side_terms(around, (message[2:3], message[3:4]), False)


def high_terms(message, own):
    row = lax.broadcasted_iota(jnp.int32, own.shape, 0)
    around = pltpu.roll(jnp.where(row < 2, jnp.concatenate([message, message], axis=0), own), 2, 0)
    return side_terms(around, (message[2:3], message[3:4]), True)


def add_side_x(terms, side, lanes, table_x, strips_x, put):
    row = lax.broadcasted_iota(jnp.int32, (8, 1), 0)
    for s in range(2):
        near, first = terms[s]
        extra = near * table_x[s, side, :, : lanes.size]
        first = jnp.where(row == (7 if side else 0), first, 0.0)
        if side:
            extra = jnp.concatenate([extra[: EDGE - 8], extra[EDGE - 8 :] + first], axis=0)
        else:
            extra = jnp.concatenate([extra[:8] + first, extra[8:]], axis=0)
        put[s, :, lanes] = strips_x[s, side, :, lanes] + extra


def sides_kernel(
    from_y_first, from_y_second, near_low, near_high, table_y, strips_y, solved_y, *done_y
):
    rows = near_low.shape[1]
    columns = done_y[0].shape[1]
    lanes_of = pl.ds(0, TILE), pl.ds(columns - TILE, TILE)
    if columns > 2 * TILE:
        for s in range(2):
            done_y[s][:, pl.ds(TILE, columns - 2 * TILE)] = solved_y[s]
    row = lax.broadcasted_iota(jnp.int32, (8, 1), 0)
    low_first = low_goes_first()
    for lines in tiles_of(rows):
        first, second = from_y_first[:, lines], from_y_second[:, lines]
        from_low, from_high = jnp.where(low_first, first, second), jnp.where(low_first, second, first)
        terms = low_terms(from_low, near_low[:, lines]), high_terms(from_high, near_high[:, lines])
        stacked = jnp.zeros((8, lines.size), F32)
        for side in range(2):
            for s in range(2):
                for which in range(2):
                    stacked = jnp.where(row == 4 * side + 2 * s + which, terms[side][s][which], stacked)
        upper, lower = halves(stacked)
        factors = jnp.concatenate([upper, lower, upper, jnp.zeros_like(upper)], axis=0).astype(BF16)
        added = lax.dot_general(factors, table_y[...], (((0,), (0,)), ((), ())), preferred_element_type=F32)
        for s in range(2):
            for side in range(2):
                block = 2 * s + side
                done_y[s][lines, lanes_of[side]] = strips_y[s, side, lines] + added[:, block * TILE : (block + 1) * TILE]


def finish_kernel(from_low_x, from_high_x, u_near, table_x, strips_x, done_y, done_yy, *refs):
    dx, dxx, dy, dyy, done_x, sems = refs[2:]
    rows, columns = dx.shape
    started = []

    def send(source, target):
        copy = pltpu.make_async_copy(source, target, sems.at[len(started)])
        copy.start()
        started.append(copy)

    send(done_y, dy)
    send(done_yy, dyy)
    for lanes in tiles_of(columns):
        add_side_x(low_terms(from_low_x[:, lanes], u_near[pl.ds(0, 8), lanes]), 0, lanes, table_x, strips_x, done_x.at[0])
        add_side_x(high_terms(from_high_x[:, lanes], u_near[pl.ds(rows - 8, 8), lanes]), 1, lanes, table_x, strips_x, done_x.at[1])
    for s, out in enumerate((dx, dxx)):
        for side in range(2):
            send(done_x.at[side, s], out.at[pl.ds(side * (rows - EDGE), EDGE)])
    for copy in started:
        copy.wait()


def on_chip(*shape):
    return pltpu.VMEM(shape, F32)


def near(array):
    return pltpu.with_memory_space_constraint(array, pltpu.VMEM)


def pack(u):
    rows, columns = u.shape
    wide = max(rows, columns)
    return pl.pallas_call(
        pack_kernel,
        name="pack",
        out_shape=(
            on_chip(MESSAGE, columns),
            on_chip(MESSAGE, columns),
            on_chip(MESSAGE, wide),
            on_chip(MESSAGE, wide),
            on_chip(rows, columns),
            on_chip(8, rows),
            on_chip(8, rows),
            pltpu.VMEM((4, WINDOW, WINDOW), BF16),
            on_chip(2, 2, EDGE, TILE),
            pltpu.VMEM((32, 4 * TILE), BF16),
        ),
        in_specs=[ANY],
        out_specs=[VMEM] * 10,
        scratch_shapes=[pltpu.SemaphoreType.DMA((5,))],
        compiler_params=LIMIT,
    )(pltpu.with_memory_space_constraint(u, pltpu.HBM))


def shapes_x(rows, columns):
    return on_chip(2, 2, EDGE, columns), on_chip(2, rows, columns)


def lead(kernel, name, outs, scratch, u_near, inverses, *messages):
    return pl.pallas_call(
        kernel,
        name=name,
        out_shape=tuple(on_chip(*a.shape) for a in messages[:2]) + outs,
        in_specs=[VMEM] * 2 + [ANY] * len(messages),
        out_specs=[ANY] * 2 + [ANY] * (len(outs) - 2) + [VMEM] * 2,
        input_output_aliases={2: 0, 3: 1},
        scratch_shapes=scratch,
        compiler_params=LIMIT,
    )(*(near(a) for a in (u_near, inverses, *messages)))


def interior(u_near, inverses, dx, *early):
    rows, columns = u_near.shape
    strips_x, solved_x = shapes_x(rows, columns)
    return pl.pallas_call(
        interior_kernel,
        name="interior",
        out_shape=(strips_x,)
        + (pltpu.HBM(u_near.shape, F32),) * 2
        + (on_chip(2, 2, rows, TILE), on_chip(2, rows, max(columns - 2 * TILE, TILE))),
        in_specs=[VMEM] * 2 + [ANY] + [VMEM] * 4,
        out_specs=[VMEM] + [ANY] * 2 + [VMEM] * 2,
        input_output_aliases={2: 1},
        scratch_shapes=[solved_x, pltpu.SemaphoreType.DMA((2,))],
        compiler_params=LIMIT,
        cost_estimate=pl.CostEstimate(flops=2 * 2**28, bytes_accessed=5 * 2**19, transcendentals=0),
    )(near(u_near), near(inverses), dx, *(near(a) for a in early))


def sides(size, *arrays):
    return pl.pallas_call(
        sides_kernel,
        name="sides",
        out_shape=(on_chip(*size),) * 2,
        in_specs=[VMEM] * 7,
        out_specs=[VMEM] * 2,
        compiler_params=LIMIT,
    )(*(near(a) for a in arrays))


def finish(arrays, parts):
    columns = parts[0].shape[1]
    return pl.pallas_call(
        finish_kernel,
        name="finish",
        out_shape=(pltpu.HBM(parts[0].shape, F32),) * 4,
        in_specs=[VMEM] * 7 + [ANY] * 2,
        out_specs=[ANY] * 4,
        input_output_aliases={7: 0, 8: 1},
        scratch_shapes=[on_chip(2, 2, EDGE, columns), pltpu.SemaphoreType.DMA((6,))],
        compiler_params=LIMIT,
    )(*(near(a) for a in arrays), *parts)


def local(velocity):
    to_high_x, to_low_x, to_y_first, to_y_second, u_near, near_low, near_high, inverses, *tables = pack(velocity[0])
    size = u_near.shape
    outs = shapes_x(*size)
    to_high_x, to_y_first, dx, *early = lead(
        first_kernel,
        "solve_first",
        (pltpu.HBM(size, F32),) + outs,
        [pltpu.SemaphoreType.DMA((1,))],
        u_near,
        inverses,
        to_high_x,
        to_y_first,
    )
    to_low_x, to_y_second, *between = lead(between_kernel, "solve_between", outs, [], u_near, inverses, to_low_x, to_y_second, early[0])
    gx = lax.axis_size("gx")
    first, second = trades_along_y()
    from_low_x = lax.ppermute(to_high_x, "gx", [(i, (i + 1) % gx) for i in range(gx)])
    from_y_first = lax.ppermute(to_y_first, ("gx", "gy"), first)
    from_high_x = lax.ppermute(to_low_x, "gx", [(i, (i - 1) % gx) for i in range(gx)])
    from_y_second = lax.ppermute(to_y_second, ("gx", "gy"), second)
    strips_x, dx, dxx, strips_y, solved_y = interior(u_near, inverses, dx, *early, *between)
    table_x, table_y = tables
    done = sides(size, from_y_first, from_y_second, near_low, near_high, table_y, strips_y, solved_y)
    dx, dxx, dy, dyy = finish((from_low_x, from_high_x, u_near, table_x, strips_x, *done), (dx, dxx))
    return tuple(o[None] for o in (dx, dy, dxx, dyy))


def solution(mesh):
    placed = P(None, "gx", "gy")
    return jax.shard_map(local, mesh=mesh, in_specs=(placed,), out_specs=(placed,) * 4, check_vma=False)
```

```python
import math

import jax
import jax.numpy as jnp
from jax import lax
from jax.experimental import pallas as pl
from jax.experimental.pallas import tpu as pltpu
from jax.sharding import PartitionSpec as P

F32 = jnp.float32
BF16 = jnp.bfloat16

COUPLINGS = (1.0 / 3.0, 2.0 / 11.0)
CENTRES = (7.0 / 9.0, 12.0 / 11.0 + 6.0 / 44.0)
BESIDES = (1.0 / 36.0, 3.0 / 44.0)

ROOTS = tuple(math.sqrt(1.0 - 4.0 * a * a) for a in COUPLINGS)
RATIOS = tuple((root - 1.0) / (2.0 * a) for a, root in zip(COUPLINGS, ROOTS))
SCALES = tuple((c - b / a) / root for a, b, c, root in zip(COUPLINGS, BESIDES, CENTRES, ROOTS))
PEAKS = tuple((c + 2.0 * b * r) / root - h for b, c, r, root, h in zip(BESIDES, CENTRES, RATIOS, ROOTS, SCALES))

WINDOW = 256
TILE = 128
STRIP = 32
EDGE = 24
REACH = 64
MESSAGE = 4

ANY = pl.BlockSpec(memory_space=pl.ANY)
VMEM = pl.BlockSpec(memory_space=pltpu.VMEM)
LIMIT = pltpu.CompilerParams(vmem_limit_bytes=16 * 2**20)


def differences(cells, axis):
    length = cells.shape[axis]
    here = pltpu.roll(cells, length - 1, axis) - cells
    before = pltpu.roll(here, 1, axis)
    return here + before, here - before


def powers(ratio, exponent):
    product = jnp.where(exponent < REACH, F32(1.0), F32(0.0))
    for bit in range(REACH.bit_length() - 1):
        factor = jnp.where((exponent & (1 << bit)) != 0, F32(ratio ** (1 << bit)), F32(1.0))
        product = product * factor
    return product


def tail_weights(high):
    at = lax.broadcasted_iota(jnp.int32, (STRIP, TILE), 0)
    known = (at >= 1) & (at < STRIP - 1)
    exponent = (STRIP - 2 - at) if high else (at - 1)
    return [jnp.where(known, powers(ratio, exponent), 0.0) for ratio in RATIOS]


def message(strip, high, weights):
    tails = [
        jnp.sum(part * weight[:, : strip.shape[1]], axis=0, keepdims=True)
        for part, weight in zip(differences(strip, 0), weights)
    ]
    near = pltpu.roll(strip[STRIP - 8 :], 2, 0) if high else strip[:8]
    row = lax.broadcasted_iota(jnp.int32, near.shape, 0)
    return jnp.where(row < 2, near, jnp.where(row == 2, tails[0], tails[1]))[:MESSAGE]


def tiles_of(length):
    step = min(length, TILE)
    return [pl.ds(k * step, step) for k in range(length // step)]


def halves(value):
    upper = value.astype(BF16).astype(F32)
    return upper, value - upper


def put_inverses(k_ref):
    i = lax.broadcasted_iota(jnp.int32, (TILE, TILE), 0)
    j = lax.broadcasted_iota(jnp.int32, (TILE, TILE), 1)
    blocks = WINDOW // TILE
    for s in range(2):
        for apart in range(1 - blocks, blocks):
            distance = jnp.abs(j - i + apart * TILE)
            weights = SCALES[s] * powers(RATIOS[s], distance)
            if apart == 0:
                weights = jnp.where(distance == 0, F32(SCALES[s] + PEAKS[s]), weights)
            upper, lower = halves(weights)
            for p, part in enumerate((upper, lower)):
                for first in range(blocks):
                    if 0 <= first + apart < blocks:
                        at_i, at_j = pl.ds(first * TILE, TILE), pl.ds((first + apart) * TILE, TILE)
                        k_ref[2 * s + p, at_i, at_j] = part.astype(BF16)


def put_side_tables(table_x, table_y):
    at = lax.broadcasted_iota(jnp.int32, (EDGE, TILE), 0)
    lane = lax.broadcasted_iota(jnp.int32, (8, TILE), 1)
    row = lax.broadcasted_iota(jnp.int32, (8, TILE), 0)
    for s in range(2):
        for side in range(2):
            table_x[s, side] = powers(RATIOS[s], (EDGE - 1 - at) if side else at)
            within = (TILE - 1 - lane) if side else lane
            first = 4 * side + 2 * s
            lines = jnp.where(row == first, powers(RATIOS[s], within), 0.0)
            lines = jnp.where((row == first + 1) & (within == 0), 1.0, lines)
            upper, lower = halves(lines)
            stack = jnp.concatenate([upper, upper, lower, jnp.zeros_like(upper)], axis=0)
            block = 2 * s + side
            table_y[:, pl.ds(block * TILE, TILE)] = stack.astype(BF16)


def low_goes_first():
    next_chip_first = lax.axis_index("gx") == 0
    return next_chip_first == (lax.rem(lax.axis_index("gy"), 2) == 0)


def trades_along_y():
    gx, gy = lax.axis_size("gx"), lax.axis_size("gy")
    next_chip = [(y, (y - 1) % gy if y % 2 == 0 else (y + 1) % gy) for y in range(gy)]
    same_chip = [(y, y + 1 if y % 2 == 0 else y - 1) for y in range(gy)]
    first, second = [], []
    for x in range(gx):
        orders = (next_chip, same_chip) if x == 0 else (same_chip, next_chip)
        for found, pairs in zip((first, second), orders):
            found += [(x * gy + source, x * gy + target) for source, target in pairs]
    return first, second


def pack_kernel(
    u_ref, to_high_x, to_low_x, to_y_first, to_y_second, u_near, near_low, near_high, k_ref, table_x, table_y, sems
):
    rows, columns = u_ref.shape
    across = [pl.ds(0, TILE), pl.ds(columns - TILE, TILE)]
    pieces = [(pl.ds(0, rows), lanes) for lanes in across]
    order = (0, 2, 1, 3, 4)
    if columns > 2 * TILE:
        middle = pl.ds(TILE, columns - 2 * TILE)
        pieces += [(pl.ds(0, STRIP), middle), (pl.ds(rows - STRIP, STRIP), middle)]
        if rows > 2 * STRIP:
            pieces.append((pl.ds(STRIP, rows - 2 * STRIP), middle))
    copies = [
        pltpu.make_async_copy(u_ref.at[lines, lanes], u_near.at[lines, lanes], sems.at[k])
        for k, (lines, lanes) in enumerate(pieces)
    ]
    for k in order:
        if k < len(copies):
            copies[k].start()
    low_first = low_goes_first()
    weights_low, weights_high = tail_weights(False), tail_weights(True)
    put_inverses(k_ref)
    put_side_tables(table_x, table_y)

    def put_x(lanes):
        to_low_x[:, lanes] = message(u_near[pl.ds(0, STRIP), lanes], False, weights_low)
        to_high_x[:, lanes] = message(u_near[pl.ds(rows - STRIP, STRIP), lanes], True, weights_high)

    low, high = [], []
    for k in range(2):
        copies[k].wait()
        put_x(across[k])
        turned = u_near[:, across[k]].T
        side = turned[TILE - STRIP :] if k else turned[:STRIP]
        (near_high if k else near_low)[...] = side[STRIP - 8 :] if k else side[:8]
        for lanes in tiles_of(rows):
            part = side[:, lanes.start : lanes.start + lanes.size]
            (high if k else low).append(message(part, k == 1, (weights_low, weights_high)[k]))
    for lanes, to_low, to_high in zip(tiles_of(rows), low, high):
        to_y_first[:, lanes] = jnp.where(low_first, to_low, to_high)
        to_y_second[:, lanes] = jnp.where(low_first, to_high, to_low)
    for copy in copies[2:4]:
        copy.wait()
    for lanes in tiles_of(columns)[1:-1]:
        put_x(lanes)
    for copy in copies[4:]:
        copy.wait()


def only_known(rhs, axis):
    length, step = rhs.shape[axis], 8 if axis == 0 else TILE
    at = lax.broadcasted_iota(jnp.int32, [step if k == axis else 1 for k in range(2)], axis)
    first, middle, last = (
        lax.slice_in_dim(rhs, low, high, axis=axis) for low, high in ((0, step), (step, length - step), (length - step, length))
    )
    parts = [jnp.where(at >= 1, first, 0.0), middle, jnp.where(at < step - 1, last, 0.0)]
    return jnp.concatenate([p for p in parts if p.shape[axis] > 0], axis=axis)


def product(a, b):
    dot = lambda p, q: jnp.dot(p, q, preferred_element_type=F32)
    return dot(a[0], b[0]) + dot(a[1], b[0]) + dot(a[0], b[1])


def split(value):
    upper = value.astype(BF16)
    return upper, (value - upper.astype(F32)).astype(BF16)


def solve_x(u_ref, k_ref, strips, solved_ref, copies):
    rows, columns = u_ref.shape
    span = min(columns, WINDOW)
    for s in range(2):
        inverse = k_ref[2 * s, :rows, :rows], k_ref[2 * s + 1, :rows, :rows]
        for j in range(columns // span):
            tiles = [differences(u_ref[:, pl.ds(j * span + t.start, t.size)], 0) for t in tiles_of(span)]
            lanes = pl.ds(j * span, span)
            rhs = jnp.concatenate([only_known(tile[s], 0) for tile in tiles], axis=1)
            solved = product(inverse, split(rhs))
            solved_ref[s, :, lanes] = solved
            strips[s, 0, :, lanes] = solved[:EDGE]
            strips[s, 1, :, lanes] = solved[rows - EDGE :]
        if s in copies:
            copies[s].start()


def inner_copies(solved_ref, outs, sems, systems):
    rows = solved_ref.shape[1]
    if rows <= 2 * EDGE:
        return {}
    inner = pl.ds(EDGE, rows - 2 * EDGE)
    return {s: pltpu.make_async_copy(solved_ref.at[s, inner], outs[s].at[inner], sems.at[s]) for s in systems}


def solve_y(u_ref, k_ref, strips, solved_ref):
    rows, columns = u_ref.shape
    span = min(columns, WINDOW)
    lane = lax.broadcasted_iota(jnp.int32, (1, TILE), 1)
    step = min(rows, 64)
    both = [differences(u_ref[pl.ds(i * step, step), :], 1) for i in range(rows // step)]
    for s in range(2):
        inverse = k_ref[2 * s, :span, :span], k_ref[2 * s + 1, :span, :span]
        values = jnp.concatenate([only_known(piece[s], 1) for piece in both], axis=0)
        rhs = split(values)
        count = columns // span
        stacked = [jnp.concatenate([part[:, w * span : (w + 1) * span] for w in range(count)], axis=0) for part in rhs]
        solved = product(stacked, inverse)
        tiles = [solved[w * rows : (w + 1) * rows, t.start : t.start + t.size] for w in range(count) for t in tiles_of(span)]
        per = span // TILE
        added = {}
        for w in range(1, count):
            edge = w * span
            before = tiles[w * per - 1][:, TILE - 1 :] - PEAKS[s] * values[:, edge - 1 : edge]
            after = tiles[w * per][:, :1] - PEAKS[s] * values[:, edge : edge + 1]
            added[w * per] = before * powers(RATIOS[s], lane + 1)
            added[w * per - 1] = after * powers(RATIOS[s], TILE - lane)
        for t, value in added.items():
            tiles[t] = tiles[t] + value
        strips[s, 0] = tiles[0]
        strips[s, 1] = tiles[-1]
        for t in range(1, len(tiles) - 1):
            solved_ref[s, :, pl.ds((t - 1) * TILE, TILE)] = tiles[t]


FIRST, BETWEEN, LAST = range(3)


def solves_x():
    ends = jnp.where(lax.axis_index("gy") < 2, FIRST, BETWEEN)
    return jnp.where(lax.axis_index("gx") == 0, ends, LAST)


def first_kernel(u_ref, k_ref, *refs):
    dx, strips_x, solved_x, sems = refs[4:]

    @pl.when(solves_x() == FIRST)
    def _():
        copies = inner_copies(solved_x, (dx,), sems, (0,))
        solve_x(u_ref, k_ref, strips_x, solved_x, copies)
        for copy in copies.values():
            copy.wait()


def between_kernel(u_ref, k_ref, *refs):
    strips_x, solved_x = refs[5:]

    @pl.when(solves_x() == BETWEEN)
    def _():
        solve_x(u_ref, k_ref, strips_x, solved_x, {})


def interior_kernel(u_ref, k_ref, _, first_strips, first_solved, between_strips, between_solved, *refs):
    strips_x, dx, dxx, strips_y, solved_y, solved_x, sems = refs
    for when, strips, solved in (
        (FIRST, first_strips, first_solved),
        (BETWEEN, between_strips, between_solved),
        (LAST, strips_x, solved_x),
    ):

        @pl.when(solves_x() == when)
        def _():
            copies = inner_copies(solved, (dx, dxx), sems, (1,) if when == FIRST else (0, 1))
            if when == LAST:
                solve_x(u_ref, k_ref, strips, solved, copies)
            else:
                for copy in copies.values():
                    copy.start()
                strips_x[...] = strips[...]
            solve_y(u_ref, k_ref, strips_y, solved_y)
            for copy in copies.values():
                copy.wait()


def side_terms(around, tails, high):
    found = []
    for s, part in enumerate(differences(around, 0)):
        nearest, outer = (part[1:2], part[2:3]) if high else (part[2:3], part[1:2])
        total = nearest + RATIOS[s] * (outer + RATIOS[s] * tails[s])
        found.append((SCALES[s] * total, PEAKS[s] * nearest))
    return found


def low_terms(message, own):
    row = lax.broadcasted_iota(jnp.int32, own.shape, 0)
    around = jnp.where(row < 2, jnp.concatenate([message, message], axis=0), pltpu.roll(own, 2, 0))
    return side_terms(around, (message[2:3], message[3:4]), False)


def high_terms(message, own):
    row = lax.broadcasted_iota(jnp.int32, own.shape, 0)
    around = pltpu.roll(jnp.where(row < 2, jnp.concatenate([message, message], axis=0), own), 2, 0)
    return side_terms(around, (message[2:3], message[3:4]), True)


def add_side_x(terms, side, lanes, table_x, strips_x, put):
    row = lax.broadcasted_iota(jnp.int32, (8, 1), 0)
    for s in range(2):
        near, first = terms[s]
        extra = near * table_x[s, side, :, : lanes.size]
        first = jnp.where(row == (7 if side else 0), first, 0.0)
        if side:
            extra = jnp.concatenate([extra[: EDGE - 8], extra[EDGE - 8 :] + first], axis=0)
        else:
            extra = jnp.concatenate([extra[:8] + first, extra[8:]], axis=0)
        put[s, :, lanes] = strips_x[s, side, :, lanes] + extra


def sides_kernel(
    from_y_first, from_y_second, near_low, near_high, table_y, strips_y, solved_y, *done_y
):
    rows = near_low.shape[1]
    columns = done_y[0].shape[1]
    lanes_of = pl.ds(0, TILE), pl.ds(columns - TILE, TILE)
    if columns > 2 * TILE:
        for s in range(2):
            done_y[s][:, pl.ds(TILE, columns - 2 * TILE)] = solved_y[s]
    row = lax.broadcasted_iota(jnp.int32, (8, 1), 0)
    low_first = low_goes_first()
    for lines in tiles_of(rows):
        first, second = from_y_first[:, lines], from_y_second[:, lines]
        from_low, from_high = jnp.where(low_first, first, second), jnp.where(low_first, second, first)
        terms = low_terms(from_low, near_low[:, lines]), high_terms(from_high, near_high[:, lines])
        stacked = jnp.zeros((8, lines.size), F32)
        for side in range(2):
            for s in range(2):
                for which in range(2):
                    stacked = jnp.where(row == 4 * side + 2 * s + which, terms[side][s][which], stacked)
        upper, lower = halves(stacked)
        factors = jnp.concatenate([upper, lower, upper, jnp.zeros_like(upper)], axis=0).astype(BF16)
        added = lax.dot_general(factors, table_y[...], (((0,), (0,)), ((), ())), preferred_element_type=F32)
        for s in range(2):
            for side in range(2):
                block = 2 * s + side
                done_y[s][lines, lanes_of[side]] = strips_y[s, side, lines] + added[:, block * TILE : (block + 1) * TILE]


def finish_kernel(from_low_x, from_high_x, u_near, table_x, strips_x, done_y, done_yy, *refs):
    dx, dxx, dy, dyy, done_x, sems = refs[2:]
    rows, columns = dx.shape
    started = []

    def send(source, target):
        copy = pltpu.make_async_copy(source, target, sems.at[len(started)])
        copy.start()
        started.append(copy)

    send(done_y, dy)
    send(done_yy, dyy)
    for lanes in tiles_of(columns):
        add_side_x(low_terms(from_low_x[:, lanes], u_near[pl.ds(0, 8), lanes]), 0, lanes, table_x, strips_x, done_x.at[0])
        add_side_x(high_terms(from_high_x[:, lanes], u_near[pl.ds(rows - 8, 8), lanes]), 1, lanes, table_x, strips_x, done_x.at[1])
    for s, out in enumerate((dx, dxx)):
        for side in range(2):
            send(done_x.at[side, s], out.at[pl.ds(side * (rows - EDGE), EDGE)])
    for copy in started:
        copy.wait()


def on_chip(*shape):
    return pltpu.VMEM(shape, F32)


def near(array):
    return pltpu.with_memory_space_constraint(array, pltpu.VMEM)


def pack(u):
    rows, columns = u.shape
    wide = max(rows, columns)
    return pl.pallas_call(
        pack_kernel,
        name="pack",
        out_shape=(
            on_chip(MESSAGE, columns),
            on_chip(MESSAGE, columns),
            on_chip(MESSAGE, wide),
            on_chip(MESSAGE, wide),
            on_chip(rows, columns),
            on_chip(8, rows),
            on_chip(8, rows),
            pltpu.VMEM((4, WINDOW, WINDOW), BF16),
            on_chip(2, 2, EDGE, TILE),
            pltpu.VMEM((32, 4 * TILE), BF16),
        ),
        in_specs=[ANY],
        out_specs=[VMEM] * 10,
        scratch_shapes=[pltpu.SemaphoreType.DMA((5,))],
        compiler_params=LIMIT,
    )(pltpu.with_memory_space_constraint(u, pltpu.HBM))


def shapes_x(rows, columns):
    return on_chip(2, 2, EDGE, columns), on_chip(2, rows, columns)


def lead(kernel, name, outs, scratch, u_near, inverses, *messages):
    return pl.pallas_call(
        kernel,
        name=name,
        out_shape=tuple(on_chip(*a.shape) for a in messages[:2]) + outs,
        in_specs=[VMEM] * 2 + [ANY] * len(messages),
        out_specs=[ANY] * 2 + [ANY] * (len(outs) - 2) + [VMEM] * 2,
        input_output_aliases={2: 0, 3: 1},
        scratch_shapes=scratch,
        compiler_params=LIMIT,
    )(*(near(a) for a in (u_near, inverses, *messages)))


def interior(u_near, inverses, dx, *early):
    rows, columns = u_near.shape
    strips_x, solved_x = shapes_x(rows, columns)
    return pl.pallas_call(
        interior_kernel,
        name="interior",
        out_shape=(strips_x,)
        + (pltpu.HBM(u_near.shape, F32),) * 2
        + (on_chip(2, 2, rows, TILE), on_chip(2, rows, max(columns - 2 * TILE, TILE))),
        in_specs=[VMEM] * 2 + [ANY] + [VMEM] * 4,
        out_specs=[VMEM] + [ANY] * 2 + [VMEM] * 2,
        input_output_aliases={2: 1},
        scratch_shapes=[solved_x, pltpu.SemaphoreType.DMA((2,))],
        compiler_params=LIMIT,
        cost_estimate=pl.CostEstimate(flops=2 * 2**28, bytes_accessed=5 * 2**19, transcendentals=0),
    )(near(u_near), near(inverses), dx, *(near(a) for a in early))


def sides(size, *arrays):
    return pl.pallas_call(
        sides_kernel,
        name="sides",
        out_shape=(on_chip(*size),) * 2,
        in_specs=[VMEM] * 7,
        out_specs=[VMEM] * 2,
        compiler_params=LIMIT,
    )(*(near(a) for a in arrays))


def finish(arrays, parts):
    columns = parts[0].shape[1]
    return pl.pallas_call(
        finish_kernel,
        name="finish",
        out_shape=(pltpu.HBM(parts[0].shape, F32),) * 4,
        in_specs=[VMEM] * 7 + [ANY] * 2,
        out_specs=[ANY] * 4,
        input_output_aliases={7: 0, 8: 1},
        scratch_shapes=[on_chip(2, 2, EDGE, columns), pltpu.SemaphoreType.DMA((6,))],
        compiler_params=LIMIT,
    )(*(near(a) for a in arrays), *parts)


def local(velocity):
    to_high_x, to_low_x, to_y_first, to_y_second, u_near, near_low, near_high, inverses, *tables = pack(velocity[0])
    size = u_near.shape
    outs = shapes_x(*size)
    to_high_x, to_y_first, dx, *early = lead(
        first_kernel,
        "solve_first",
        (pltpu.HBM(size, F32),) + outs,
        [pltpu.SemaphoreType.DMA((1,))],
        u_near,
        inverses,
        to_high_x,
        to_y_first,
    )
    to_low_x, to_y_second, *between = lead(between_kernel, "solve_between", outs, [], u_near, inverses, to_low_x, to_y_second, early[0])
    gx = lax.axis_size("gx")
    first, second = trades_along_y()
    from_low_x = lax.ppermute(to_high_x, "gx", [(i, (i + 1) % gx) for i in range(gx)])
    from_y_first = lax.ppermute(to_y_first, ("gx", "gy"), first)
    from_high_x = lax.ppermute(to_low_x, "gx", [(i, (i - 1) % gx) for i in range(gx)])
    from_y_second = lax.ppermute(to_y_second, ("gx", "gy"), second)
    strips_x, dx, dxx, strips_y, solved_y = interior(u_near, inverses, dx, *early, *between)
    table_x, table_y = tables
    done = sides(size, from_y_first, from_y_second, near_low, near_high, table_y, strips_y, solved_y)
    dx, dxx, dy, dyy = finish((from_low_x, from_high_x, u_near, table_x, strips_x, *done), (dx, dxx))
    return tuple(o[None] for o in (dx, dy, dxx, dyy))


def solution(mesh):
    placed = P(None, "gx", "gy")
    return jax.shard_map(local, mesh=mesh, in_specs=(placed,), out_specs=(placed,) * 4, check_vma=False)
```

```python
import math

import jax
import jax.numpy as jnp
from jax import lax
from jax.experimental import pallas as pl
from jax.experimental.pallas import tpu as pltpu
from jax.sharding import PartitionSpec as P

F32 = jnp.float32
BF16 = jnp.bfloat16

COUPLINGS = (1.0 / 3.0, 2.0 / 11.0)
CENTRES = (7.0 / 9.0, 12.0 / 11.0 + 6.0 / 44.0)
BESIDES = (1.0 / 36.0, 3.0 / 44.0)

ROOTS = tuple(math.sqrt(1.0 - 4.0 * a * a) for a in COUPLINGS)
RATIOS = tuple((root - 1.0) / (2.0 * a) for a, root in zip(COUPLINGS, ROOTS))
SCALES = tuple((c - b / a) / root for a, b, c, root in zip(COUPLINGS, BESIDES, CENTRES, ROOTS))
PEAKS = tuple((c + 2.0 * b * r) / root - h for b, c, r, root, h in zip(BESIDES, CENTRES, RATIOS, ROOTS, SCALES))

WINDOW = 256
TILE = 128
STRIP = 24
EDGE = 24
REACH = 64
MESSAGE = 4

ANY = pl.BlockSpec(memory_space=pl.ANY)
VMEM = pl.BlockSpec(memory_space=pltpu.VMEM)
LIMIT = pltpu.CompilerParams(vmem_limit_bytes=16 * 2**20)


def differences(cells, axis):
    length = cells.shape[axis]
    here = pltpu.roll(cells, length - 1, axis) - cells
    before = pltpu.roll(here, 1, axis)
    return here + before, here - before


def powers(ratio, exponent):
    product = jnp.where(exponent < REACH, F32(1.0), F32(0.0))
    for bit in range(REACH.bit_length() - 1):
        factor = jnp.where((exponent & (1 << bit)) != 0, F32(ratio ** (1 << bit)), F32(1.0))
        product = product * factor
    return product


def tail_weights(high):
    at = lax.broadcasted_iota(jnp.int32, (STRIP, TILE), 0)
    known = (at >= 1) & (at < STRIP - 1)
    exponent = (STRIP - 2 - at) if high else (at - 1)
    return [jnp.where(known, powers(ratio, exponent), 0.0) for ratio in RATIOS]


def message(strip, high, weights):
    tails = [
        jnp.sum(part * weight[:, : strip.shape[1]], axis=0, keepdims=True)
        for part, weight in zip(differences(strip, 0), weights)
    ]
    near = pltpu.roll(strip[STRIP - 8 :], 2, 0) if high else strip[:8]
    row = lax.broadcasted_iota(jnp.int32, near.shape, 0)
    return jnp.where(row < 2, near, jnp.where(row == 2, tails[0], tails[1]))[:MESSAGE]


def tiles_of(length):
    step = min(length, TILE)
    return [pl.ds(k * step, step) for k in range(length // step)]


def halves(value):
    upper = value.astype(BF16).astype(F32)
    return upper, value - upper


def put_inverses(k_ref):
    i = lax.broadcasted_iota(jnp.int32, (TILE, TILE), 0)
    j = lax.broadcasted_iota(jnp.int32, (TILE, TILE), 1)
    blocks = WINDOW // TILE
    for s in range(2):
        for apart in range(1 - blocks, blocks):
            distance = jnp.abs(j - i + apart * TILE)
            weights = SCALES[s] * powers(RATIOS[s], distance)
            if apart == 0:
                weights = jnp.where(distance == 0, F32(SCALES[s] + PEAKS[s]), weights)
            upper, lower = halves(weights)
            for p, part in enumerate((upper, lower)):
                for first in range(blocks):
                    if 0 <= first + apart < blocks:
                        at_i, at_j = pl.ds(first * TILE, TILE), pl.ds((first + apart) * TILE, TILE)
                        k_ref[2 * s + p, at_i, at_j] = part.astype(BF16)


def put_side_tables(table_x, table_y):
    at = lax.broadcasted_iota(jnp.int32, (EDGE, TILE), 0)
    lane = lax.broadcasted_iota(jnp.int32, (8, TILE), 1)
    row = lax.broadcasted_iota(jnp.int32, (8, TILE), 0)
    for s in range(2):
        for side in range(2):
            table_x[s, side] = powers(RATIOS[s], (EDGE - 1 - at) if side else at)
            within = (TILE - 1 - lane) if side else lane
            first = 4 * side + 2 * s
            lines = jnp.where(row == first, powers(RATIOS[s], within), 0.0)
            lines = jnp.where((row == first + 1) & (within == 0), 1.0, lines)
            upper, lower = halves(lines)
            stack = jnp.concatenate([upper, upper, lower, jnp.zeros_like(upper)], axis=0)
            block = 2 * s + side
            table_y[:, pl.ds(block * TILE, TILE)] = stack.astype(BF16)


def low_goes_first():
    next_chip_first = lax.axis_index("gx") == 0
    return next_chip_first == (lax.rem(lax.axis_index("gy"), 2) == 0)


def trades_along_y():
    gx, gy = lax.axis_size("gx"), lax.axis_size("gy")
    next_chip = [(y, (y - 1) % gy if y % 2 == 0 else (y + 1) % gy) for y in range(gy)]
    same_chip = [(y, y + 1 if y % 2 == 0 else y - 1) for y in range(gy)]
    first, second = [], []
    for x in range(gx):
        orders = (next_chip, same_chip) if x == 0 else (same_chip, next_chip)
        for found, pairs in zip((first, second), orders):
            found += [(x * gy + source, x * gy + target) for source, target in pairs]
    return first, second


def pack_kernel(
    u_ref, to_high_x, to_low_x, to_y_first, to_y_second, u_near, near_low, near_high, k_ref, table_x, table_y, sems
):
    rows, columns = u_ref.shape
    across = [pl.ds(0, TILE), pl.ds(columns - TILE, TILE)]
    pieces = [(pl.ds(0, rows), lanes) for lanes in across]
    order = (0, 2, 1, 3, 4)
    if columns > 2 * TILE:
        middle = pl.ds(TILE, columns - 2 * TILE)
        pieces += [(pl.ds(0, STRIP), middle), (pl.ds(rows - STRIP, STRIP), middle)]
        if rows > 2 * STRIP:
            pieces.append((pl.ds(STRIP, rows - 2 * STRIP), middle))
    copies = [
        pltpu.make_async_copy(u_ref.at[lines, lanes], u_near.at[lines, lanes], sems.at[k])
        for k, (lines, lanes) in enumerate(pieces)
    ]
    for k in order:
        if k < len(copies):
            copies[k].start()
    low_first = low_goes_first()
    weights_low, weights_high = tail_weights(False), tail_weights(True)
    put_inverses(k_ref)
    put_side_tables(table_x, table_y)

    def put_x(lanes):
        to_low_x[:, lanes] = message(u_near[pl.ds(0, STRIP), lanes], False, weights_low)
        to_high_x[:, lanes] = message(u_near[pl.ds(rows - STRIP, STRIP), lanes], True, weights_high)

    low, high = [], []
    for k in range(2):
        copies[k].wait()
        put_x(across[k])
        turned = u_near[:, across[k]].T
        side = turned[TILE - STRIP :] if k else turned[:STRIP]
        (near_high if k else near_low)[...] = side[STRIP - 8 :] if k else side[:8]
        for lanes in tiles_of(rows):
            part = side[:, lanes.start : lanes.start + lanes.size]
            (high if k else low).append(message(part, k == 1, (weights_low, weights_high)[k]))
    for lanes, to_low, to_high in zip(tiles_of(rows), low, high):
        to_y_first[:, lanes] = jnp.where(low_first, to_low, to_high)
        to_y_second[:, lanes] = jnp.where(low_first, to_high, to_low)
    for copy in copies[2:4]:
        copy.wait()
    for lanes in tiles_of(columns)[1:-1]:
        put_x(lanes)
    for copy in copies[4:]:
        copy.wait()


def only_known(rhs, axis):
    length, step = rhs.shape[axis], 8 if axis == 0 else TILE
    at = lax.broadcasted_iota(jnp.int32, [step if k == axis else 1 for k in range(2)], axis)
    first, middle, last = (
        lax.slice_in_dim(rhs, low, high, axis=axis) for low, high in ((0, step), (step, length - step), (length - step, length))
    )
    parts = [jnp.where(at >= 1, first, 0.0), middle, jnp.where(at < step - 1, last, 0.0)]
    return jnp.concatenate([p for p in parts if p.shape[axis] > 0], axis=axis)


def product(a, b):
    dot = lambda p, q: jnp.dot(p, q, preferred_element_type=F32)
    return dot(a[0], b[0]) + dot(a[1], b[0]) + dot(a[0], b[1])


def split(value):
    upper = value.astype(BF16)
    return upper, (value - upper.astype(F32)).astype(BF16)


def solve_x(u_ref, k_ref, strips, solved_ref, copies):
    rows, columns = u_ref.shape
    span = min(columns, WINDOW)
    for s in range(2):
        inverse = k_ref[2 * s, :rows, :rows], k_ref[2 * s + 1, :rows, :rows]
        for j in range(columns // span):
            tiles = [differences(u_ref[:, pl.ds(j * span + t.start, t.size)], 0) for t in tiles_of(span)]
            lanes = pl.ds(j * span, span)
            rhs = jnp.concatenate([only_known(tile[s], 0) for tile in tiles], axis=1)
            solved = product(inverse, split(rhs))
            solved_ref[s, :, lanes] = solved
            strips[s, 0, :, lanes] = solved[:EDGE]
            strips[s, 1, :, lanes] = solved[rows - EDGE :]
        if s in copies:
            copies[s].start()


def inner_copies(solved_ref, outs, sems, systems):
    rows = solved_ref.shape[1]
    if rows <= 2 * EDGE:
        return {}
    inner = pl.ds(EDGE, rows - 2 * EDGE)
    return {s: pltpu.make_async_copy(solved_ref.at[s, inner], outs[s].at[inner], sems.at[s]) for s in systems}


def solve_y(u_ref, k_ref, strips, solved_ref):
    rows, columns = u_ref.shape
    span = min(columns, WINDOW)
    lane = lax.broadcasted_iota(jnp.int32, (1, TILE), 1)
    step = min(rows, 64)
    both = [differences(u_ref[pl.ds(i * step, step), :], 1) for i in range(rows // step)]
    for s in range(2):
        inverse = k_ref[2 * s, :span, :span], k_ref[2 * s + 1, :span, :span]
        values = jnp.concatenate([only_known(piece[s], 1) for piece in both], axis=0)
        rhs = split(values)
        count = columns // span
        stacked = [jnp.concatenate([part[:, w * span : (w + 1) * span] for w in range(count)], axis=0) for part in rhs]
        solved = product(stacked, inverse)
        tiles = [solved[w * rows : (w + 1) * rows, t.start : t.start + t.size] for w in range(count) for t in tiles_of(span)]
        per = span // TILE
        added = {}
        for w in range(1, count):
            edge = w * span
            before = tiles[w * per - 1][:, TILE - 1 :] - PEAKS[s] * values[:, edge - 1 : edge]
            after = tiles[w * per][:, :1] - PEAKS[s] * values[:, edge : edge + 1]
            added[w * per] = before * powers(RATIOS[s], lane + 1)
            added[w * per - 1] = after * powers(RATIOS[s], TILE - lane)
        for t, value in added.items():
            tiles[t] = tiles[t] + value
        strips[s, 0] = tiles[0]
        strips[s, 1] = tiles[-1]
        for t in range(1, len(tiles) - 1):
            solved_ref[s, :, pl.ds((t - 1) * TILE, TILE)] = tiles[t]


FIRST, BETWEEN, LAST = range(3)


def solves_x():
    ends = jnp.where(lax.axis_index("gy") < 2, FIRST, BETWEEN)
    return jnp.where(lax.axis_index("gx") == 0, ends, LAST)


def first_kernel(u_ref, k_ref, *refs):
    dx, strips_x, solved_x, sems = refs[4:]

    @pl.when(solves_x() == FIRST)
    def _():
        copies = inner_copies(solved_x, (dx,), sems, (0,))
        solve_x(u_ref, k_ref, strips_x, solved_x, copies)
        for copy in copies.values():
            copy.wait()


def between_kernel(u_ref, k_ref, *refs):
    strips_x, solved_x = refs[5:]

    @pl.when(solves_x() == BETWEEN)
    def _():
        solve_x(u_ref, k_ref, strips_x, solved_x, {})


def interior_kernel(u_ref, k_ref, _, first_strips, first_solved, between_strips, between_solved, *refs):
    strips_x, dx, dxx, strips_y, solved_y, solved_x, sems = refs
    for when, strips, solved in (
        (FIRST, first_strips, first_solved),
        (BETWEEN, between_strips, between_solved),
        (LAST, strips_x, solved_x),
    ):

        @pl.when(solves_x() == when)
        def _():
            copies = inner_copies(solved, (dx, dxx), sems, (1,) if when == FIRST else (0, 1))
            if when == LAST:
                solve_x(u_ref, k_ref, strips, solved, copies)
            else:
                for copy in copies.values():
                    copy.start()
                strips_x[...] = strips[...]
            solve_y(u_ref, k_ref, strips_y, solved_y)
            for copy in copies.values():
                copy.wait()


def side_terms(around, tails, high):
    found = []
    for s, part in enumerate(differences(around, 0)):
        nearest, outer = (part[1:2], part[2:3]) if high else (part[2:3], part[1:2])
        total = nearest + RATIOS[s] * (outer + RATIOS[s] * tails[s])
        found.append((SCALES[s] * total, PEAKS[s] * nearest))
    return found


def low_terms(message, own):
    row = lax.broadcasted_iota(jnp.int32, own.shape, 0)
    around = jnp.where(row < 2, jnp.concatenate([message, message], axis=0), pltpu.roll(own, 2, 0))
    return side_terms(around, (message[2:3], message[3:4]), False)


def high_terms(message, own):
    row = lax.broadcasted_iota(jnp.int32, own.shape, 0)
    around = pltpu.roll(jnp.where(row < 2, jnp.concatenate([message, message], axis=0), own), 2, 0)
    return side_terms(around, (message[2:3], message[3:4]), True)


def add_side_x(terms, side, lanes, table_x, strips_x, put):
    row = lax.broadcasted_iota(jnp.int32, (8, 1), 0)
    for s in range(2):
        near, first = terms[s]
        extra = near * table_x[s, side, :, : lanes.size]
        first = jnp.where(row == (7 if side else 0), first, 0.0)
        if side:
            extra = jnp.concatenate([extra[: EDGE - 8], extra[EDGE - 8 :] + first], axis=0)
        else:
            extra = jnp.concatenate([extra[:8] + first, extra[8:]], axis=0)
        put[s, :, lanes] = strips_x[s, side, :, lanes] + extra


def sides_kernel(
    from_y_first, from_y_second, near_low, near_high, table_y, strips_y, solved_y, *done_y
):
    rows = near_low.shape[1]
    columns = done_y[0].shape[1]
    lanes_of = pl.ds(0, TILE), pl.ds(columns - TILE, TILE)
    if columns > 2 * TILE:
        for s in range(2):
            done_y[s][:, pl.ds(TILE, columns - 2 * TILE)] = solved_y[s]
    row = lax.broadcasted_iota(jnp.int32, (8, 1), 0)
    low_first = low_goes_first()
    for lines in tiles_of(rows):
        first, second = from_y_first[:, lines], from_y_second[:, lines]
        from_low, from_high = jnp.where(low_first, first, second), jnp.where(low_first, second, first)
        terms = low_terms(from_low, near_low[:, lines]), high_terms(from_high, near_high[:, lines])
        stacked = jnp.zeros((8, lines.size), F32)
        for side in range(2):
            for s in range(2):
                for which in range(2):
                    stacked = jnp.where(row == 4 * side + 2 * s + which, terms[side][s][which], stacked)
        upper, lower = halves(stacked)
        factors = jnp.concatenate([upper, lower, upper, jnp.zeros_like(upper)], axis=0).astype(BF16)
        added = lax.dot_general(factors, table_y[...], (((0,), (0,)), ((), ())), preferred_element_type=F32)
        for s in range(2):
            for side in range(2):
                block = 2 * s + side
                done_y[s][lines, lanes_of[side]] = strips_y[s, side, lines] + added[:, block * TILE : (block + 1) * TILE]


def finish_kernel(from_low_x, from_high_x, u_near, table_x, strips_x, done_y, done_yy, *refs):
    dx, dxx, dy, dyy, done_x, sems = refs[2:]
    rows, columns = dx.shape
    started = []

    def send(source, target):
        copy = pltpu.make_async_copy(source, target, sems.at[len(started)])
        copy.start()
        started.append(copy)

    send(done_y, dy)
    send(done_yy, dyy)
    for lanes in tiles_of(columns):
        add_side_x(low_terms(from_low_x[:, lanes], u_near[pl.ds(0, 8), lanes]), 0, lanes, table_x, strips_x, done_x.at[0])
        add_side_x(high_terms(from_high_x[:, lanes], u_near[pl.ds(rows - 8, 8), lanes]), 1, lanes, table_x, strips_x, done_x.at[1])
    for s, out in enumerate((dx, dxx)):
        for side in range(2):
            send(done_x.at[side, s], out.at[pl.ds(side * (rows - EDGE), EDGE)])
    for copy in started:
        copy.wait()


def on_chip(*shape):
    return pltpu.VMEM(shape, F32)


def near(array):
    return pltpu.with_memory_space_constraint(array, pltpu.VMEM)


def pack(u):
    rows, columns = u.shape
    wide = max(rows, columns)
    return pl.pallas_call(
        pack_kernel,
        name="pack",
        out_shape=(
            on_chip(MESSAGE, columns),
            on_chip(MESSAGE, columns),
            on_chip(MESSAGE, wide),
            on_chip(MESSAGE, wide),
            on_chip(rows, columns),
            on_chip(8, rows),
            on_chip(8, rows),
            pltpu.VMEM((4, WINDOW, WINDOW), BF16),
            on_chip(2, 2, EDGE, TILE),
            pltpu.VMEM((32, 4 * TILE), BF16),
        ),
        in_specs=[ANY],
        out_specs=[VMEM] * 10,
        scratch_shapes=[pltpu.SemaphoreType.DMA((5,))],
        compiler_params=LIMIT,
    )(pltpu.with_memory_space_constraint(u, pltpu.HBM))


def shapes_x(rows, columns):
    return on_chip(2, 2, EDGE, columns), on_chip(2, rows, columns)


def lead(kernel, name, outs, scratch, u_near, inverses, *messages):
    return pl.pallas_call(
        kernel,
        name=name,
        out_shape=tuple(on_chip(*a.shape) for a in messages[:2]) + outs,
        in_specs=[VMEM] * 2 + [ANY] * len(messages),
        out_specs=[ANY] * 2 + [ANY] * (len(outs) - 2) + [VMEM] * 2,
        input_output_aliases={2: 0, 3: 1},
        scratch_shapes=scratch,
        compiler_params=LIMIT,
    )(*(near(a) for a in (u_near, inverses, *messages)))


def interior(u_near, inverses, dx, *early):
    rows, columns = u_near.shape
    strips_x, solved_x = shapes_x(rows, columns)
    return pl.pallas_call(
        interior_kernel,
        name="interior",
        out_shape=(strips_x,)
        + (pltpu.HBM(u_near.shape, F32),) * 2
        + (on_chip(2, 2, rows, TILE), on_chip(2, rows, max(columns - 2 * TILE, TILE))),
        in_specs=[VMEM] * 2 + [ANY] + [VMEM] * 4,
        out_specs=[VMEM] + [ANY] * 2 + [VMEM] * 2,
        input_output_aliases={2: 1},
        scratch_shapes=[solved_x, pltpu.SemaphoreType.DMA((2,))],
        compiler_params=LIMIT,
        cost_estimate=pl.CostEstimate(flops=2 * 2**28, bytes_accessed=5 * 2**19, transcendentals=0),
    )(near(u_near), near(inverses), dx, *(near(a) for a in early))


def sides(size, *arrays):
    return pl.pallas_call(
        sides_kernel,
        name="sides",
        out_shape=(on_chip(*size),) * 2,
        in_specs=[VMEM] * 7,
        out_specs=[VMEM] * 2,
        compiler_params=LIMIT,
    )(*(near(a) for a in arrays))


def finish(arrays, parts):
    columns = parts[0].shape[1]
    return pl.pallas_call(
        finish_kernel,
        name="finish",
        out_shape=(pltpu.HBM(parts[0].shape, F32),) * 4,
        in_specs=[VMEM] * 7 + [ANY] * 2,
        out_specs=[ANY] * 4,
        input_output_aliases={7: 0, 8: 1},
        scratch_shapes=[on_chip(2, 2, EDGE, columns), pltpu.SemaphoreType.DMA((6,))],
        compiler_params=LIMIT,
    )(*(near(a) for a in arrays), *parts)


def local(velocity):
    to_high_x, to_low_x, to_y_first, to_y_second, u_near, near_low, near_high, inverses, *tables = pack(velocity[0])
    size = u_near.shape
    outs = shapes_x(*size)
    to_high_x, to_y_first, dx, *early = lead(
        first_kernel,
        "solve_first",
        (pltpu.HBM(size, F32),) + outs,
        [pltpu.SemaphoreType.DMA((1,))],
        u_near,
        inverses,
        to_high_x,
        to_y_first,
    )
    to_low_x, to_y_second, *between = lead(between_kernel, "solve_between", outs, [], u_near, inverses, to_low_x, to_y_second, early[0])
    gx = lax.axis_size("gx")
    first, second = trades_along_y()
    from_low_x = lax.ppermute(to_high_x, "gx", [(i, (i + 1) % gx) for i in range(gx)])
    from_y_first = lax.ppermute(to_y_first, ("gx", "gy"), first)
    from_high_x = lax.ppermute(to_low_x, "gx", [(i, (i - 1) % gx) for i in range(gx)])
    from_y_second = lax.ppermute(to_y_second, ("gx", "gy"), second)
    strips_x, dx, dxx, strips_y, solved_y = interior(u_near, inverses, dx, *early, *between)
    table_x, table_y = tables
    done = sides(size, from_y_first, from_y_second, near_low, near_high, table_y, strips_y, solved_y)
    dx, dxx, dy, dyy = finish((from_low_x, from_high_x, u_near, table_x, strips_x, *done), (dx, dxx))
    return tuple(o[None] for o in (dx, dy, dxx, dyy))


def solution(mesh):
    placed = P(None, "gx", "gy")
    return jax.shard_map(local, mesh=mesh, in_specs=(placed,), out_specs=(placed,) * 4, check_vma=False)
```
